32 devices in a mesh: pipe: 2 (over core), dp: 16 (over z, y, x).
Axes of the slice: x: 2, y: 2, z: 4, core: 2. Of those that a mesh axis runs over, the one named last changes fastest.
Arguments:
- board_input: bfloat16 [1536, 8, 8, 256], P('dp'), may hold values from -105 to 105
- conv_weight: bfloat16 [2, 4608, 256], P('pipe', 'dp'), may hold values from -0.125 to 0.125
- norm_gains: bfloat16 [2, 512], P('pipe', 'dp'), may hold values from 0.5 to 1.5
- norm_shifts: bfloat16 [2, 512], P('pipe', 'dp'), may hold values from -3 to 3
- head_params: float32 [35840], P(('pipe', 'dp')), may hold values from -0.6 to 0.6
- policy_target: int32 [1536], P('dp'), may hold values from 0 to 4671
- legal_mask: int32 [1536, 4672], P('dp'), may hold values 0 or 1
- value_target: float32 [1536], P('dp'), may hold values from -0.9 to 0.9
Outputs:
- conv_grad: float32 [2, 4608, 256], P('pipe', 'dp')
- gain_grad: float32 [2, 512], P('pipe', 'dp')
- shift_grad: float32 [2, 512], P('pipe', 'dp')
- head_grad: float32 [35840], P(('pipe', 'dp'))
- input_grad: float32 [1536, 8, 8, 256], P('dp', None, None, 'pipe')
The draws below stay inside these ranges and needn't reach their ends.
All inputs are finite; a program needn't handle non-finite values. No bound on the sum of `legal_mask` on one device may be relied on, other than what follows from the above.
Results may differ from the reference program's by a relative error of at most 0.0074.
Values may be sent and summed in bfloat16 or wider, within the bound.
A program may use at most 192 MiB of HBM per device.

```python
import jax
import jax.numpy as jnp
from jax import lax

FILTERS = 256
PLANES = 73
VHIDDEN = 256
POS_MB = 24
MICRO = 4
MOVES = 4672
POSITIONS = 1536
HEAD_PARAMS = 35840
N_DP = 16


def draw_board_input(key, part):
    key = jax.random.fold_in(key, 11)
    base_key, row_key, col_key = jax.random.split(key, 3)
    shape = (POSITIONS, 8, 8, FILTERS)
    rank = jnp.arange(POSITIONS, dtype=jnp.float32) / POSITIONS
    row_scale = jnp.power(3.0, rank - 0.5) * jnp.exp(jax.random.uniform(row_key, (POSITIONS,), jnp.float32, -1.15, 1.15))
    col_scale = jnp.exp(jax.random.uniform(col_key, (FILTERS,), jnp.float32, -1.15, 1.15))
    base = jax.random.truncated_normal(base_key, -6.0, 6.0, shape, jnp.float32)
    values = base * row_scale[:, None, None, None] * col_scale
    return values.astype(jnp.bfloat16)


def touch_ends(values, key, least, high):
    spot = [jax.random.randint(jax.random.fold_in(key, axis), (), 0, length) for axis, length in enumerate(values.shape)]
    main_axis = values.shape.index(max(values.shape))
    next_to = spot[:main_axis] + [(spot[main_axis] + 1) % values.shape[main_axis]] + spot[main_axis + 1:]
    return values.at[tuple(spot)].set(least).at[tuple(next_to)].set(high)


def steps_of(key, shape, pieces, smallest, top_value):
    factor_of, own = 1.0, jax.random.fold_in(key, 6)
    for axis_at, parts in pieces:
        steps = jnp.exp(jax.random.uniform(jax.random.fold_in(own, axis_at), (parts,), jnp.float32, smallest / len(pieces), top_value / len(pieces)))
        factor_of = factor_of * jnp.repeat(steps, shape[axis_at] // parts).reshape([-1 if axis == axis_at else 1 for axis in range(len(shape))])
    return factor_of


def centred(own_key, dims, deviation, bound, cuts=(), kind=jnp.bfloat16):
    values = deviation * jax.random.normal(own_key, dims, jnp.float32)
    if cuts:
        values = values * steps_of(own_key, dims, cuts, -0.22, 0.18)
    return jnp.clip(values, -bound, bound).astype(kind)


def setup_inputs(seed: int = 0) -> dict:
    key_of = jax.random.split(jax.random.key(seed), 9)
    board_input = draw_board_input(jax.random.fold_in(key_of[8], 71), 0)
    conv_weight = centred(key_of[1], (2, 18 * FILTERS, FILTERS), (9 * FILTERS) ** -0.5, 0.125, ((0, 2), (1, 16)))
    norm_gains = jnp.clip(1.0 + 0.1 * jax.random.normal(key_of[2], (2, 2 * FILTERS), jnp.float32), 0.5, 1.5).astype(jnp.bfloat16)
    norm_shifts = centred(key_of[3], (2, 2 * FILTERS), 0.5, 3.0, ((0, 2), (1, 16)))
    head_params = centred(key_of[4], (HEAD_PARAMS,), 0.1, 0.6, ((0, 32),), jnp.float32)
    policy_target = touch_ends(jax.random.randint(key_of[5], (POSITIONS,), 0, MOVES), jax.random.fold_in(key_of[5], 1), 0, MOVES - 1).astype(jnp.int32)
    legal_mask = touch_ends((jax.random.randint(key_of[6], (POSITIONS, MOVES), 0, 64) < 1).astype(jnp.int32), jax.random.fold_in(key_of[6], 1), 0, 1)
    value_target = jnp.clip(jax.random.uniform(key_of[7], (POSITIONS,), jnp.float32, -0.9, 0.9) * steps_of(key_of[7], (POSITIONS,), ((0, 16),), -0.4, 0.0), -0.9, 0.9)
    return {"board_input": board_input, "conv_weight": conv_weight, "norm_gains": norm_gains, "norm_shifts": norm_shifts, "head_params": head_params, "policy_target": policy_target, "legal_mask": legal_mask, "value_target": value_target}


@jax.custom_vjp
def low(v):
    return lax.optimization_barrier(v.astype(jnp.bfloat16)).astype(jnp.float32)

@jax.custom_vjp
def low_back(v):
    return v

def low_keep(v):
    return (low(v), None)

def low_pass(kept, grad):
    return (grad,)

def back_keep(v):
    return (v, None)

def back_low(kept, grad):
    return (low(grad),)
low.defvjp(low_keep, low_pass)
low_back.defvjp(back_keep, back_low)
EPSILON = 1e-05
PRECISE = lax.Precision.HIGHEST

def offset_board(board_map, delta_row, delta_col):
    padded = jnp.pad(board_map, ((0, 0), (1, 1), (1, 1), (0, 0)))
    return padded[:, 1 + delta_row:9 + delta_row, 1 + delta_col:9 + delta_col, :]

def convolve(board_map, tap_weights):
    running = jnp.zeros(board_map.shape[:3] + (tap_weights.shape[-1],), jnp.float32)
    for offset in range(9):
        moved = offset_board(board_map, offset // 3 - 1, offset % 3 - 1)
        running = running + jnp.einsum('bijc,cd->bijd', moved, tap_weights[offset], precision=PRECISE)
    return running

def normalize(field_map, gain_vec, shift_vec):
    average = lax.optimization_barrier(jnp.mean(field_map, axis=(0, 1, 2)))
    spread = lax.optimization_barrier(jnp.mean(jnp.square(field_map - average), axis=(0, 1, 2)))
    return (field_map - average) * lax.rsqrt(spread + EPSILON) * gain_vec + shift_vec

def residual_block(block_in, tap_weights, gain_rows, shift_rows):
    first_conv = low_back(convolve(block_in, tap_weights[0]))
    inner_act = low(jax.nn.silu(normalize(first_conv, gain_rows[0], shift_rows[0])))
    second = low_back(convolve(inner_act, tap_weights[1]))
    return jax.nn.silu(block_in + normalize(second, gain_rows[1], shift_rows[1]))

def head_loss(board_map, head_all, policy_target, legal_mask, value_target):
    per_batch = board_map.shape[0]
    channels = board_map.shape[-1]
    conv_end = (PLANES + 1) * channels
    head_conv = head_all[:conv_end].reshape(channels, PLANES + 1)
    hidden_weight = head_all[conv_end:conv_end + 64 * VHIDDEN].reshape(64, VHIDDEN)
    hidden_bias = head_all[conv_end + 64 * VHIDDEN:conv_end + 65 * VHIDDEN]
    output_weight = head_all[conv_end + 65 * VHIDDEN:]
    planes = jnp.dot(board_map.reshape(per_batch * 64, channels), head_conv, precision=PRECISE)
    logits = planes[:, :PLANES].reshape(per_batch, MOVES)
    target_hit = jnp.arange(MOVES, dtype=jnp.int32)[None, :] == policy_target[:, None]
    is_legal = jnp.logical_or(legal_mask > 0, target_hit)
    masked = jnp.where(is_legal, logits, -1e+30)
    highest = lax.optimization_barrier(jnp.max(masked, axis=1, keepdims=True))
    log_total = highest[:, 0] + jnp.log(lax.optimization_barrier(jnp.sum(jnp.exp(masked - highest), axis=1)))
    chosen = lax.optimization_barrier(jnp.sum(jnp.where(target_hit, logits, 0.0), axis=1))
    squares = jax.nn.silu(planes[:, PLANES].reshape(per_batch, 64))
    hidden = jax.nn.silu(jnp.dot(squares, hidden_weight, precision=PRECISE) + hidden_bias)
    value_out = jnp.tanh(jnp.dot(hidden, output_weight, precision=PRECISE))
    return jnp.sum(log_total - chosen + jnp.square(value_out - value_target))

def reference(board_input, conv_weight, norm_gains, norm_shifts, head_params, policy_target, legal_mask, value_target):
    channels = board_input.shape[-1]
    targets = policy_target.reshape(N_DP, MICRO, POS_MB)
    masks = legal_mask.reshape(N_DP, MICRO, POS_MB, MOVES)
    values = value_target.reshape(N_DP, MICRO, POS_MB)
    block_step = jax.checkpoint(residual_block)
    head_step = jax.checkpoint(head_loss)

    def forward(board_all, conv_all, gain_all, shift_all, head_all):
        grouped = board_all.reshape(N_DP, MICRO, POS_MB, 8, 8, channels)
        tap_sets = conv_all.reshape(2, 2, 9, channels, channels)
        gain_sets = gain_all.reshape(2, 2, channels)
        shift_sets = shift_all.reshape(2, 2, channels)
        loss_sum = jnp.zeros((), jnp.float32)
        for batch_index in range(MICRO):
            block_in = grouped[:, batch_index].reshape(N_DP * POS_MB, 8, 8, channels)
            first_out = block_step(block_in, tap_sets[0], gain_sets[0], shift_sets[0])
            passed = low_back(low(first_out))
            final = block_step(passed, tap_sets[1], gain_sets[1], shift_sets[1])
            loss_sum = loss_sum + head_step(final, head_all, targets[:, batch_index].reshape(-1), masks[:, batch_index].reshape(-1, MOVES), values[:, batch_index].reshape(-1))
        return loss_sum / (MICRO * POS_MB)
    primals = (board_input.astype(jnp.float32), conv_weight.astype(jnp.float32), norm_gains.astype(jnp.float32), norm_shifts.astype(jnp.float32), head_params)
    loss_value, pull_back = jax.vjp(forward, *primals)
    gradients = pull_back(jnp.ones_like(loss_value))
    return (gradients[1], gradients[2], gradients[3], gradients[4], gradients[0])
```

```python
import functools

import jax
import jax.numpy as jnp
from jax import lax
from jax.experimental import pallas as pl
from jax.experimental.pallas import tpu as pltpu
from jax.sharding import PartitionSpec as P

PLANES = 73
VHIDDEN = 256
MICRO = 4
EPSILON = 1e-05
F32, BF16 = jnp.float32, jnp.bfloat16
PRECISE = lax.Precision.HIGHEST
MESH = pl.DeviceIdType.MESH
LANES = 128
ILLEGAL = -1e30

FOLD, WIDE, PITCH = 4, 8, 10


def sigmoid(v):
    return 0.5 * jnp.tanh(0.5 * v) + 0.5


def silu_slope(v):
    s = sigmoid(v)
    return s * (1.0 + v * (1.0 - s))


def fold8(v):
    return jnp.sum(v.reshape(v.shape[0] // 8, 8, v.shape[1]), axis=0)


def total(v):
    return jnp.sum(v, axis=0, keepdims=True)


def kernel(
    n_dp, per, groups, moves, scale,
    policy, value_goal, board, weights, gains, head_conv, hidden_w, head_vec, legal,
    tap_grad, norm_grad, hc_grad, hw_grad, hv_grad, entry_grad,
    W, X, I, Z, C, B, raw, mask_raw, code, planes, turn, goal, vgoal, stage, stat, slots, back, mine, theirs,
    load_sem, send_sem, recv_sem, out_sem, swap_sem,
):
    core, me = lax.axis_index("pipe"), lax.axis_index("dp")
    block = 2 * per
    span = WIDE * block
    rows = FOLD * span
    channels = X.shape[-1]
    taps = 9 * channels
    all_rows = n_dp * rows

    barrier = pltpu.get_barrier_semaphore()

    def greet(j, carry):
        pl.semaphore_signal(barrier, inc=1, device_id=(core, lax.rem(me + j, n_dp)), device_id_type=MESH)
        return carry

    lax.fori_loop(1, n_dp, greet, 0)
    pl.semaphore_signal(barrier, inc=1, device_id=(1 - core, me), device_id_type=MESH)

    first = pl.multiple_of(core * groups * per, 8)
    loads = [
        pltpu.make_async_copy(board.at[pl.ds(first, groups * per)], raw, load_sem.at[0]),
        pltpu.make_async_copy(legal.at[pl.ds(first, groups * per)], mask_raw, load_sem.at[1]),
        pltpu.make_async_copy(weights, W, load_sem.at[2]),
    ]
    for load in loads:
        load.start()

    edge = jnp.zeros((block, channels), BF16)

    def clear(i, carry):
        for f in range(FOLD + 2):
            for column in (0, WIDE + 1):
                at = pl.ds((f * PITCH + column) * block, block)
                for g in range(groups):
                    X[i, g, at, :] = edge
                    I[i, g, at, :] = edge
                    Z[g, at, :] = edge
        return carry

    lax.fori_loop(0, 2, clear, 0)

    def put(ref, at, f, q, y):
        ref[*at, pl.ds(pl.multiple_of(((f + 1) * PITCH + 1 + q) * block, 16), block), :] = y.astype(BF16)
        none = jnp.zeros((per, channels), F32)
        if f == FOLD - 1:
            halo = jnp.concatenate([none, y[:per]], axis=0)
            ref[*at, pl.ds(pl.multiple_of((1 + q) * block, 16), block), :] = halo.astype(BF16)
        if f == 0:
            halo = jnp.concatenate([y[per:], none], axis=0)
            ref[*at, pl.ds(pl.multiple_of(((FOLD + 1) * PITCH + 1 + q) * block, 16), block), :] = halo.astype(BF16)

    def inside(f, q):
        return pl.ds(pl.multiple_of(((f + 1) * PITCH + 1 + q) * block, 16), block)

    def plain(f, q):
        return pl.ds(pl.multiple_of((f * WIDE + q) * block, 16), block)

    def each(body, carry=0):
        def column(q, carry):
            for f in range(FOLD):
                carry = body(f, q, carry)
            return carry

        return lax.fori_loop(0, WIDE, column, carry)

    loads[0].wait()
    for g in range(groups):

        def widen(b, carry, g=g):
            rows_of = raw[g * per + b].astype(F32).reshape(64, channels)
            for i in range(channels // LANES):
                turn[i, pl.ds(pl.multiple_of(b * 64, 64), 64), :] = rows_of[:, i * LANES : (i + 1) * LANES]
            return carry

        lax.fori_loop(0, per, widen, 0)

        def reorder(f, q, carry, g=g):
            parts = [
                jnp.concatenate(
                    [turn[i, pl.ds((f + FOLD * half) * 8 + q, per, stride=64), :] for half in range(2)], axis=0
                )
                for i in range(channels // LANES)
            ]
            put(X, (0, g), f, q, jnp.concatenate(parts, axis=1))
            return carry

        each(reorder)

    both = groups * per
    row_of = lax.broadcasted_iota(jnp.int32, (both, LANES), 0)
    lane_of = lax.broadcasted_iota(jnp.int32, (both, LANES), 1)

    def column_of(ref, zero):
        def pick(b, acc):
            return jnp.where(row_of == b, ref[first + b], acc)

        return lax.fori_loop(0, both, pick, zero)

    goal[...] = column_of(policy, jnp.zeros((both, LANES), jnp.int32))
    vgoal[...] = column_of(value_goal, jnp.zeros((both, LANES), F32))
    loads[1].wait()
    for square in range(64):
        base = square * PLANES // LANES * LANES
        shift = square * PLANES - base
        width = min(2 * LANES, moves - base)
        window = mask_raw[:, base : base + width]
        if width < 2 * LANES:
            window = jnp.concatenate([window, jnp.zeros((both, 2 * LANES - width), jnp.int32)], axis=1)
        if shift:
            window = pltpu.roll(window, 2 * LANES - shift, axis=1)
        window = window[:, :LANES]
        hit = goal[...] == lane_of + square * PLANES
        kind = jnp.where(hit, 2.0, jnp.where(window > 0, 1.0, 0.0))
        kind = jnp.where(lane_of < PLANES, kind, 0.0)
        f, q, half = square // 8 % FOLD, square % 8, square // 8 // FOLD
        at = ((f * WIDE + q) * 2 + half) * per
        for g in range(groups):
            code[g, pl.ds(at, per), :] = kind[g * per : (g + 1) * per]

    hc_grad[...] = jnp.zeros_like(hc_grad)
    hw_grad[...] = jnp.zeros_like(hw_grad)
    hv_grad[...] = jnp.zeros_like(hv_grad)
    norm_grad[...] = jnp.zeros_like(norm_grad)

    pl.semaphore_wait(barrier, n_dp)
    loads[2].wait()

    def push(k, g, top, bottom):
        slots[k, g, me, pl.ds(0, 1), :] = top
        slots[k, g, me, pl.ds(1, 1), :] = bottom

        def send(j, carry):
            pltpu.make_async_remote_copy(
                src_ref=slots.at[k, g, me],
                dst_ref=slots.at[k, g, me],
                send_sem=send_sem.at[k, g],
                recv_sem=recv_sem.at[k, g],
                device_id=(core, lax.rem(me + j, n_dp)),
                device_id_type=MESH,
            ).start()
            return carry

        lax.fori_loop(1, n_dp, send, 0)

    def arrived(k, g):
        others = slots.at[k, g, pl.ds(0, n_dp - 1)]
        copy = pltpu.make_async_remote_copy(
            src_ref=others, dst_ref=others, send_sem=send_sem.at[k, g], recv_sem=recv_sem.at[k, g],
            device_id=(core, lax.rem(me + 1, n_dp)), device_id_type=MESH,
        )
        copy.wait_send()
        copy.wait_recv()
        return slots[k, g]

    def merge_moments(k, g):
        parts = arrived(k, g)
        both_sums = jnp.sum(parts, axis=0)
        mean = both_sums[0:1] / n_dp
        apart = parts - mean
        between = jnp.sum(apart * apart, axis=0)[0:1]
        spread = (both_sums[1:2] + between * rows) / all_rows
        stat[k, g, pl.ds(0, 1), :] = mean
        stat[k, g, pl.ds(1, 1), :] = lax.rsqrt(spread + EPSILON)

    def norm_of(section, c, g):
        k = 2 * section + c
        gain = gains[section, pl.ds(c, 1), :]
        shift = gains[section, pl.ds(2 + c, 1), :]
        return stat[k, g, pl.ds(0, 1), :], stat[k, g, pl.ds(1, 1), :], gain, shift

    def convolve(field, section, c, g):
        k = 2 * section + c
        sums, parts = [], []
        for f in range(FOLD):
            slabs = [
                field[section, g, pl.ds(((f + t // 3) * PITCH + t % 3) * block, span), :] for t in range(9)
            ]
            out = jnp.dot(
                jnp.concatenate(slabs, axis=1), W[section, pl.ds(c * taps, taps), :],
                preferred_element_type=F32,
            )
            C[section, c, g, pl.ds(f * span, span), :] = out
            part = total(fold8(out))
            apart = out - part / span
            sums.append(part)
            parts.append(total(fold8(apart * apart)))
        mean = sum(sums) / rows
        spread = sum(parts)
        for part in sums:
            spread = spread + span * jnp.square(part / span - mean)
        push(k, g, mean, spread)

    def inner(section, g):
        mean, inv, gain, shift = norm_of(section, 0, g)
        factor = inv * gain

        def body(f, q, carry):
            v = (C[section, 0, g, plain(f, q), :] - mean) * factor + shift
            put(I, (section, g), f, q, v * sigmoid(v))
            return carry

        each(body)

    def outer_pre(section, g, f, q, norm):
        mean, inv, gain, shift = norm
        z = (C[section, 1, g, plain(f, q), :] - mean) * inv
        return X[section, g, inside(f, q), :].astype(F32) + z * gain + shift, z

    for g in range(groups):
        convolve(X, 0, 0, g)
    for section in range(2):
        for g in range(groups):
            merge_moments(2 * section, g)
            inner(section, g)
            convolve(I, section, 1, g)
        if section == 0:
            for g in range(groups):
                merge_moments(1, g)
                norm = norm_of(0, 1, g)

                def hand_on(f, q, carry, g=g, norm=norm):
                    v, _ = outer_pre(0, g, f, q, norm)
                    put(X, (1, g), f, q, v * sigmoid(v))
                    return carry

                each(hand_on)
                convolve(X, 1, 0, g)

    lane = lax.broadcasted_iota(jnp.int32, (per, LANES), 1)

    def heads(g):
        norm = norm_of(1, 1, g)

        def last(f, q, carry):
            v, _ = outer_pre(1, g, f, q, norm)
            B[g, plain(f, q), :] = v * sigmoid(v)
            return carry

        each(last)
        for f in range(FOLD):
            at = pl.ds(f * span, span)
            planes[at, :] = jnp.dot(B[g, at, :], head_conv[...], precision=PRECISE, preferred_element_type=F32)

        def look(f, q, carry):
            top, squares = carry
            a = planes[plain(f, q), :]
            a_legal = jnp.where(code[g, plain(f, q), :] > 0, a, ILLEGAL)
            top = jnp.maximum(top, jnp.maximum(a_legal[:per], a_legal[per:]))
            column = a[:, PLANES : PLANES + 1]
            for half in range(2):
                here = lane == (f + FOLD * half) * 8 + q
                squares = jnp.where(here, column[half * per : (half + 1) * per], squares)
            return top, squares

        top, pre = each(look, (jnp.full((per, LANES), ILLEGAL, F32), jnp.zeros((per, LANES), F32)))
        top = jnp.max(top, axis=1, keepdims=True)
        top = jnp.concatenate([top, top], axis=0)

        def weigh(f, q, acc):
            a = planes[plain(f, q), :]
            e = jnp.where(code[g, plain(f, q), :] > 0, jnp.exp(a - top), 0.0)
            planes[plain(f, q), :] = e
            return acc + e[:per] + e[per:]

        norm_sum = jnp.sum(each(weigh, jnp.zeros((per, LANES), F32)), axis=1, keepdims=True)
        portion = scale / norm_sum
        portion = jnp.concatenate([portion, portion], axis=0)

        squares = pre * sigmoid(pre)
        bias, out_w = head_vec[pl.ds(0, 1), :], head_vec[pl.ds(1, 1), :]
        hidden_pre = jnp.dot(squares, hidden_w[...], precision=PRECISE, preferred_element_type=F32) + bias
        hidden = hidden_pre * sigmoid(hidden_pre)
        value = jnp.tanh(jnp.sum(hidden * out_w, axis=1, keepdims=True))
        wanted = vgoal[pl.ds(g * per, per), 0:1]
        slope = 2.0 * scale * (value - wanted) * (1.0 - value * value)
        hidden_grad = slope * out_w * silu_slope(hidden_pre)
        hw_grad[...] += lax.dot_general(
            squares, hidden_grad, (((0,), (0,)), ((), ())), precision=PRECISE, preferred_element_type=F32
        )
        hv_grad[pl.ds(0, 1), :] += total(hidden_grad)
        hv_grad[pl.ds(1, 1), :] += total(hidden * slope)
        squares_grad = lax.dot_general(
            hidden_grad, hidden_w[...], (((1,), (1,)), ((), ())), precision=PRECISE, preferred_element_type=F32
        )
        pre_grad = squares_grad * silu_slope(pre)

        def slopes(f, q, carry):
            e = planes[plain(f, q), :] * portion
            e = e - jnp.where(code[g, plain(f, q), :] > 1.5, scale, 0.0)
            columns = [
                jnp.sum(jnp.where(lane == (f + FOLD * half) * 8 + q, pre_grad, 0.0), axis=1, keepdims=True)
                for half in range(2)
            ]
            column = jnp.concatenate(columns, axis=0)
            wide = lax.broadcasted_iota(jnp.int32, (block, LANES), 1)
            planes[plain(f, q), :] = jnp.where(wide == PLANES, column, e)
            return carry

        each(slopes)
        hc_grad[...] += lax.dot_general(
            B[g], planes[...], (((0,), (0,)), ((), ())), precision=PRECISE, preferred_element_type=F32
        )
        for f in range(FOLD):
            at = pl.ds(f * span, span)
            B[g, at, :] = lax.dot_general(
                planes[at, :], head_conv[...], (((1,), (1,)), ((), ())), precision=PRECISE,
                preferred_element_type=F32,
            )

    def outer_grad(section, g):
        norm = norm_of(section, 1, g)

        def body(f, q, carry):
            shift_sum, gain_sum = carry
            v, z = outer_pre(section, g, f, q, norm)
            grad = B[g, plain(f, q), :]
            if section == 0:
                grad = grad.astype(BF16).astype(F32)
            grad = grad * silu_slope(v)
            B[g, plain(f, q), :] = grad
            return shift_sum + fold8(grad), gain_sum + fold8(grad * z)

        zero = jnp.zeros((8, channels), F32)
        shift_sum, gain_sum = each(body, (zero, zero))
        push(4 + 2 * section + 1, g, total(shift_sum), total(gain_sum))

    def norm_back(section, c, g):
        sums = jnp.sum(arrived(4 + 2 * section + c, g), axis=0)
        norm_grad[pl.ds(4 * section + c, 1), :] += sums[1:2]
        norm_grad[pl.ds(4 * section + 2 + c, 1), :] += sums[0:1]
        mean, inv, gain, _ = norm_of(section, c, g)
        p_mean, pz_mean = sums[0:1] / all_rows, sums[1:2] / all_rows
        factor = inv * gain

        def body(f, q, carry):
            z = (C[section, c, g, plain(f, q), :] - mean) * inv
            p = B[g, plain(f, q), :] if c else C[section, 1, g, plain(f, q), :]
            put(Z, (g,), f, q, factor * (p - p_mean - z * pz_mean))
            return carry

        each(body)

    def back_field(section, c, g, f):
        acc = None
        for t in range(9):
            part = lax.dot_general(
                Z[g, pl.ds(((f + 2 - t // 3) * PITCH + 2 - t % 3) * block, span), :],
                W[section, pl.ds(c * taps + t * channels, channels), :],
                (((1,), (1,)), ((), ())), preferred_element_type=F32,
            )
            acc = part if acc is None else acc + part
        return acc

    def inner_grad(section, g):
        for f in range(FOLD):
            C[section, 1, g, pl.ds(f * span, span), :] = back_field(section, 1, g, f)
        mean, inv, gain, shift = norm_of(section, 0, g)

        def body(f, q, carry):
            shift_sum, gain_sum = carry
            z = (C[section, 0, g, plain(f, q), :] - mean) * inv
            grad = C[section, 1, g, plain(f, q), :] * silu_slope(z * gain + shift)
            C[section, 1, g, plain(f, q), :] = grad
            return shift_sum + fold8(grad), gain_sum + fold8(grad * z)

        zero = jnp.zeros((8, channels), F32)
        shift_sum, gain_sum = each(body, (zero, zero))
        push(4 + 2 * section, g, total(shift_sum), total(gain_sum))

    def entry(section, g):
        for f in range(FOLD):
            at = pl.ds(f * span, span)
            B[g, at, :] = B[g, at, :] + back_field(section, 0, g, f)

    def tap_gradient(section, c):
        field = I if c else X
        dz = jnp.concatenate(
            [Z[g, pl.ds(((f + 1) * PITCH + 1) * block, span), :] for g in range(groups) for f in range(FOLD)], axis=0
        )
        for t in range(9):
            moved = jnp.concatenate(
                [
                    field[section, g, pl.ds(((f + t // 3) * PITCH + t % 3) * block, span), :]
                    for g in range(groups)
                    for f in range(FOLD)
                ],
                axis=0,
            )
            grad = lax.dot_general(moved, dz, (((0,), (0,)), ((), ())), preferred_element_type=F32)
            stage[section, pl.ds(c * taps + t * channels, channels), :] = grad.astype(BF16)
        at = pl.ds(c * taps, taps)
        pltpu.make_async_copy(stage.at[section, at], tap_grad.at[section, at], out_sem.at[section, c]).start()

    for g in range(groups):
        merge_moments(3, g)
        heads(g)
        outer_grad(1, g)
    for section in (1, 0):
        for g in range(groups):
            norm_back(section, 1, g)
            inner_grad(section, g)
        tap_gradient(section, 1)
        for g in range(groups):
            norm_back(section, 0, g)
            if section == 1:
                entry(section, g)
                outer_grad(0, g)
        tap_gradient(section, 0)
    for g in range(groups):
        entry(0, g)

        def restore(f, q, carry, g=g):
            v = B[g, plain(f, q), :]
            for half in range(2):
                for i in range(channels // LANES):
                    part = v[half * per : (half + 1) * per, i * LANES : (i + 1) * LANES]
                    turn[i, pl.ds((f + FOLD * half) * 8 + q, per, stride=64), :] = part
            return carry

        each(restore)
        for f in range(FOLD):
            at = pl.ds(f * span, span)
            to = pl.ds(g * rows + f * span, span)
            mine[to, :] = turn[core, at, :].astype(BF16)
            theirs[to, :] = turn[1 - core, at, :].astype(BF16)
    own = pl.ds(pl.multiple_of(core * groups * rows, 16), groups * rows)
    swap = pltpu.make_async_remote_copy(
        src_ref=theirs, dst_ref=entry_grad.at[own], send_sem=swap_sem.at[0], recv_sem=swap_sem.at[1],
        device_id=(1 - core, me), device_id_type=MESH,
    )
    swap.start()
    keep = pltpu.make_async_copy(mine, entry_grad.at[own], swap_sem.at[2])
    keep.start()
    keep.wait()
    swap.wait()
    for section in range(2):
        for c in range(2):
            at = pl.ds(c * taps, taps)
            pltpu.make_async_copy(stage.at[section, at], tap_grad.at[section, at], out_sem.at[section, c]).wait()


def local(
    board_input, conv_weight, norm_gains, norm_shifts, head_params, policy_target, legal_mask, value_target
):
    n_dp, n_pipe = lax.axis_size("dp"), lax.axis_size("pipe")
    positions, channels = board_input.shape[0], board_input.shape[-1]
    per = positions // MICRO
    groups = MICRO // n_pipe
    moves = legal_mask.shape[1]
    rows = per * 64
    padded = (FOLD + 2) * PITCH * 2 * per
    taps = 9 * channels

    weights = lax.all_gather(lax.all_gather(conv_weight, "dp", axis=1, tiled=True), "pipe", axis=0, tiled=True)
    norms = jnp.stack([norm_gains, norm_shifts], axis=1)
    norms = lax.all_gather(lax.all_gather(norms, "dp", axis=2, tiled=True), "pipe", axis=0, tiled=True)
    norms = norms.astype(F32).reshape(2, 4, channels)
    norms = jnp.concatenate([norms, jnp.zeros_like(norms)], axis=1)
    head_all = lax.all_gather(head_params, ("pipe", "dp"), axis=0, tiled=True)
    conv_end = (PLANES + 1) * channels
    head_conv = jnp.pad(head_all[:conv_end].reshape(channels, PLANES + 1), ((0, 0), (0, LANES - PLANES - 1)))
    hidden_end = conv_end + 64 * VHIDDEN
    hidden_w = jnp.pad(head_all[conv_end:hidden_end].reshape(64, VHIDDEN), ((0, LANES - 64), (0, 0)))
    head_vec = jnp.pad(head_all[hidden_end:].reshape(2, VHIDDEN), ((0, 6), (0, 0)))

    vmem = pl.BlockSpec(memory_space=pltpu.VMEM)
    smem = pl.BlockSpec(memory_space=pltpu.SMEM)
    anywhere = pl.BlockSpec(memory_space=pl.ANY)
    dma, regular = pltpu.SemaphoreType.DMA, pltpu.VMEM
    tap_grad, norm_grad, hc_grad, hw_grad, hv_grad, entry_grad = pl.pallas_call(
        functools.partial(kernel, n_dp, per, groups, moves, 1.0 / positions),
        out_shape=(
            jax.ShapeDtypeStruct((2, 2 * taps, channels), BF16),
            jax.ShapeDtypeStruct((8, channels), F32),
            jax.ShapeDtypeStruct((channels, LANES), F32),
            jax.ShapeDtypeStruct((LANES, VHIDDEN), F32),
            jax.ShapeDtypeStruct((8, VHIDDEN), F32),
            jax.ShapeDtypeStruct((positions * 64, LANES), BF16),
        ),
        in_specs=[smem, smem, anywhere, anywhere, vmem, vmem, vmem, vmem, anywhere],
        out_specs=(anywhere, vmem, vmem, vmem, vmem, anywhere),
        scratch_shapes=[
            regular((2, 2 * taps, channels), BF16),
            regular((2, groups, padded, channels), BF16),
            regular((2, groups, padded, channels), BF16),
            regular((groups, padded, channels), BF16),
            regular((2, 2, groups, rows, channels), F32),
            regular((groups, rows, channels), F32),
            regular((groups * per, 8, 8, channels), BF16),
            regular((groups * per, moves), jnp.int32),
            regular((groups, rows, LANES), F32),
            regular((rows, LANES), F32),
            regular((channels // LANES, rows, LANES), F32),
            regular((groups * per, LANES), jnp.int32),
            regular((groups * per, LANES), F32),
            regular((2, 2 * taps, channels), BF16),
            regular((4, groups, 8, channels), F32),
            regular((8, groups, n_dp, 2, channels), F32),
            regular((8, LANES), F32),
            regular((groups * rows, LANES), BF16),
            regular((groups * rows, LANES), BF16),
            dma((3,)),
            dma((8, groups)),
            dma((8, groups)),
            dma((2, 2)),
            dma((3,)),
        ],
        compiler_params=pltpu.CompilerParams(
            collective_id=0, has_side_effects=True, vmem_limit_bytes=62 * 2**20
        ),
    )(policy_target, value_target, board_input, weights, norms, head_conv, hidden_w, head_vec, legal_mask)

    conv_grad = lax.psum_scatter(
        tap_grad.astype(F32).reshape(4 * taps, channels), ("pipe", "dp"), scatter_dimension=0, tiled=True
    )
    head_grad = jnp.concatenate(
        [hc_grad[:, : PLANES + 1].reshape(-1), hw_grad[:64].reshape(-1), hv_grad[:2].reshape(-1)]
    )
    head_grad = lax.psum_scatter(head_grad, ("pipe", "dp"), scatter_dimension=0, tiled=True)
    norm_grad = lax.psum(norm_grad, "pipe").reshape(2, 2, 2 * channels)[lax.axis_index("pipe")]
    width = norm_gains.shape[1]
    norm_grad = lax.dynamic_slice_in_dim(norm_grad, lax.axis_index("dp") * width, width, axis=1)
    entry_grad = entry_grad.astype(F32).reshape(positions, 8, 8, LANES)
    return conv_grad[None], norm_grad[:1], norm_grad[1:], head_grad, entry_grad


def solution(mesh):
    placed = (
        P("dp", None, None, None),
        P("pipe", "dp", None),
        P("pipe", "dp"),
        P("pipe", "dp"),
        P(("pipe", "dp")),
        P("dp"),
        P("dp", None),
        P("dp"),
    )
    return jax.shard_map(
        local,
        mesh=mesh,
        in_specs=placed,
        out_specs=(
            P("pipe", "dp", None),
            P("pipe", "dp"),
            P("pipe", "dp"),
            P(("pipe", "dp")),
            P("dp", None, None, "pipe"),
        ),
        check_vma=False,
    )
```

```python
import functools

import jax
import jax.numpy as jnp
from jax import lax
from jax.experimental import pallas as pl
from jax.experimental.pallas import tpu as pltpu
from jax.sharding import PartitionSpec as P

PLANES = 73
VHIDDEN = 256
MICRO = 4
EPSILON = 1e-05
F32, BF16 = jnp.float32, jnp.bfloat16
PRECISE = lax.Precision.HIGHEST
MESH = pl.DeviceIdType.MESH
LANES = 128
ILLEGAL = -1e30
HC_ROWS, HW_ROWS = 24, 16
LAYER = 4

FOLD, WIDE, PITCH = 4, 8, 10


def sigmoid(v):
    return 0.5 * jnp.tanh(0.5 * v) + 0.5


def silu_slope(v):
    s = sigmoid(v)
    return s * (1.0 + v * (1.0 - s))


def fold8(v):
    return jnp.sum(v.reshape(v.shape[0] // 8, 8, v.shape[1]), axis=0)


def total(v):
    return jnp.sum(v, axis=0, keepdims=True)


def kernel(
    sizes, policy, value_goal, board, shard, small, legal,
    tap_out, small_out, entry_grad,
    W, X, I, Z, C, B, raw, mask_raw, code, planes, turn, goal, vgoal, stage, stat, slots, mine, theirs,
    packs, gains, head_conv, hidden_w, norm_grad, hc_grad, hw_grad, norm_in, hc_in, hw_in, hc_slots, hw_slots,
    siblings, layers, columns, arrivals,
    load_sem, send_sem, recv_sem, swap_sem, pack_sem, head_sem, fetch_sem, reduce_sem,
):
    n_dp, per, groups, moves, scale, shard_rows, own_taps, flat = sizes
    core, me = lax.axis_index("pipe"), lax.axis_index("dp")
    block = 2 * per
    span = WIDE * block
    rows = FOLD * span
    channels = X.shape[-1]
    taps = 9 * channels
    all_rows = n_dp * rows
    spot, level = lax.rem(me, LAYER), me // LAYER
    levels = n_dp // LAYER

    def remote(src, dst, send, recv, pipe, dp):
        return pltpu.make_async_remote_copy(
            src_ref=src, dst_ref=dst, send_sem=send, recv_sem=recv, device_id=(pipe, dp), device_id_type=MESH
        )

    def sent(ref, sem):
        remote(ref, ref, sem, sem, 1 - core, me).wait_send()

    def came(ref, sem):
        remote(ref, ref, sem, sem, 1 - core, me).wait_recv()

    barrier = pltpu.get_barrier_semaphore()

    def greet(j, carry):
        pl.semaphore_signal(barrier, inc=1, device_id=(core, lax.rem(me + j, n_dp)), device_id_type=MESH)
        return carry

    def greet_column(j, carry):
        other = lax.rem(me + j * LAYER, n_dp)
        pl.semaphore_signal(barrier, inc=1, device_id=(1 - core, other), device_id_type=MESH)
        return carry

    lax.fori_loop(1, n_dp, greet, 0)
    lax.fori_loop(0, levels, greet_column, 0)

    first = pl.multiple_of(core * groups * per, 8)
    loads = [
        pltpu.make_async_copy(board.at[pl.ds(first, groups * per)], raw, load_sem.at[0]),
        pltpu.make_async_copy(legal.at[pl.ds(first, groups * per)], mask_raw, load_sem.at[1]),
    ]
    if not own_taps:
        loads.append(pltpu.make_async_copy(shard, W, load_sem.at[2]))
    for load in loads:
        load.start()
    pl.semaphore_wait(barrier, n_dp - 1 + levels)

    def shard_at(section, c, half, place):
        start = c * taps + (half * LAYER + place) * shard_rows
        return W.at[section, pl.ds(pl.multiple_of(start, 16), shard_rows)]

    def half_at(ref, section, c, half):
        start = c * taps + half * LAYER * shard_rows
        return ref.at[section, pl.ds(pl.multiple_of(start, 16), LAYER * shard_rows)]

    def fetch_column(section, c):
        if not own_taps:
            return

        @pl.when((core == section) & (level // 2 == c))
        def _():
            half = lax.rem(level, 2)
            at = shard_at(section, c, half, spot)
            src, send, recv = shard.at[0], fetch_sem.at[0, section, c], fetch_sem.at[1, section, c]
            for j in range(1, levels):
                remote(src, at, send, recv, half, lax.rem(me + j * LAYER, n_dp)).start()

            @pl.when(half == core)
            def _():
                pltpu.make_async_copy(src, at, recv).start()

            @pl.when(half != core)
            def _():
                remote(src, at, send, recv, half, me).start()

    def fetch_level(section, c):
        if not own_taps:
            return
        at = shard_at(section, c, core, spot)
        came(at, fetch_sem.at[1, section, c])
        for j in range(1, LAYER):
            peer = level * LAYER + lax.rem(spot + j, LAYER)
            remote(at, at, fetch_sem.at[2, section, c], fetch_sem.at[3, section, c], core, peer).start()

    def fetch_core(section, c):
        if not own_taps:
            return
        three = W.at[section, pl.ds(c * taps, (LAYER - 1) * shard_rows)]
        came(three, fetch_sem.at[3, section, c])
        at = half_at(W, section, c, core)
        remote(at, at, fetch_sem.at[4, section, c], fetch_sem.at[5, section, c], 1 - core, me).start()

    def fetch_done(section, c):
        if not own_taps:
            return
        came(half_at(W, section, c, 1 - core), fetch_sem.at[5, section, c])

    def send_pack(j, carry):
        remote(
            small, packs.at[core, me], pack_sem.at[0], pack_sem.at[1], core, lax.rem(me + j, n_dp)
        ).start()
        return carry

    fetch_column(0, 0)
    lax.fori_loop(1, n_dp, send_pack, 0)
    packs[core, me] = small[...]
    fetch_column(0, 1)

    edge = jnp.zeros((block, channels), BF16)

    def clear(i, carry):
        for f in range(FOLD + 2):
            for column in (0, WIDE + 1):
                at = pl.ds((f * PITCH + column) * block, block)
                for g in range(groups):
                    X[i, g, at, :] = edge
                    I[i, g, at, :] = edge
                    Z[g, at, :] = edge
        return carry

    lax.fori_loop(0, 2, clear, 0)

    def put(ref, at, f, q, y):
        ref[*at, pl.ds(pl.multiple_of(((f + 1) * PITCH + 1 + q) * block, 16), block), :] = y.astype(BF16)
        none = jnp.zeros((per, channels), F32)
        if f == FOLD - 1:
            halo = jnp.concatenate([none, y[:per]], axis=0)
            ref[*at, pl.ds(pl.multiple_of((1 + q) * block, 16), block), :] = halo.astype(BF16)
        if f == 0:
            halo = jnp.concatenate([y[per:], none], axis=0)
            ref[*at, pl.ds(pl.multiple_of(((FOLD + 1) * PITCH + 1 + q) * block, 16), block), :] = halo.astype(BF16)

    def inside(f, q):
        return pl.ds(pl.multiple_of(((f + 1) * PITCH + 1 + q) * block, 16), block)

    def plain(f, q):
        return pl.ds(pl.multiple_of((f * WIDE + q) * block, 16), block)

    def each(body, carry=0):
        def column(q, carry):
            for f in range(FOLD):
                carry = body(f, q, carry)
            return carry

        return lax.fori_loop(0, WIDE, column, carry)

    loads[0].wait()
    for g in range(groups):

        def widen(b, carry, g=g):
            rows_of = raw[g * per + b].astype(F32).reshape(64, channels)
            for i in range(channels // LANES):
                turn[i, pl.ds(pl.multiple_of(b * 64, 64), 64), :] = rows_of[:, i * LANES : (i + 1) * LANES]
            return carry

        lax.fori_loop(0, per, widen, 0)

        def reorder(f, q, carry, g=g):
            parts = [
                jnp.concatenate(
                    [turn[i, pl.ds((f + FOLD * half) * 8 + q, per, stride=64), :] for half in range(2)], axis=0
                )
                for i in range(channels // LANES)
            ]
            put(X, (0, g), f, q, jnp.concatenate(parts, axis=1))
            return carry

        each(reorder)

    fetch_level(0, 0)
    some = packs.at[core, pl.ds(0, n_dp - 1)]
    came(some, pack_sem.at[1])
    remote(packs.at[core], packs.at[core], pack_sem.at[2], pack_sem.at[3], 1 - core, me).start()

    both = groups * per
    row_of = lax.broadcasted_iota(jnp.int32, (both, LANES), 0)
    lane_of = lax.broadcasted_iota(jnp.int32, (both, LANES), 1)

    def column_of(ref, zero):
        def pick(b, acc):
            return jnp.where(row_of == b, ref[first + b], acc)

        return lax.fori_loop(0, both, pick, zero)

    goal[...] = column_of(policy, jnp.zeros((both, LANES), jnp.int32))
    vgoal[...] = column_of(value_goal, jnp.zeros((both, LANES), F32))
    loads[1].wait()
    for square in range(64):
        base = square * PLANES // LANES * LANES
        shift = square * PLANES - base
        width = min(2 * LANES, moves - base)
        window = mask_raw[:, base : base + width]
        if width < 2 * LANES:
            window = jnp.concatenate([window, jnp.zeros((both, 2 * LANES - width), jnp.int32)], axis=1)
        if shift:
            window = pltpu.roll(window, 2 * LANES - shift, axis=1)
        window = window[:, :LANES]
        hit = goal[...] == lane_of + square * PLANES
        kind = jnp.where(hit, 2.0, jnp.where(window > 0, 1.0, 0.0))
        kind = jnp.where(lane_of < PLANES, kind, 0.0)
        f, q, half = square // 8 % FOLD, square % 8, square // 8 // FOLD
        at = ((f * WIDE + q) * 2 + half) * per
        for g in range(groups):
            code[g, pl.ds(at, per), :] = kind[g * per : (g + 1) * per]

    hc_grad[...] = jnp.zeros_like(hc_grad)
    hw_grad[...] = jnp.zeros_like(hw_grad)
    norm_grad[...] = jnp.zeros_like(norm_grad)
    fetch_level(0, 1)
    fetch_core(0, 0)

    came(packs.at[1 - core], pack_sem.at[3])
    share = 2 * channels // n_dp
    tile_share = LANES // share
    for section in range(2):
        for tile in range(2 * channels // LANES):
            acc = jnp.zeros((2, LANES), F32)
            for u in range(tile_share):
                part = packs[section, tile * tile_share + u, pl.ds(0, 2), :]
                acc = acc + (pltpu.roll(part, u * share, axis=1) if u else part)
            c, at = tile * LANES // channels, tile * LANES % channels
            gains[section, pl.ds(c, 1), pl.ds(at, LANES)] = acc[0:1]
            gains[section, pl.ds(2 + c, 1), pl.ds(at, LANES)] = acc[1:2]

    pack_rows = small.shape[0]
    one_lane = lax.broadcasted_iota(jnp.int32, (1, LANES), 1)

    def flat_row(start):
        owner = start // flat
        off = start - owner * flat
        line, lane_at = off // LANES, lax.rem(off, LANES)

        def line_of(owner, line):
            return packs[owner // n_dp, lax.rem(owner, n_dp), pl.ds(line + 2, 1), :]

        near = line_of(owner, line)
        far = line_of(owner, jnp.minimum(line + 1, pack_rows - 3))
        beyond = line_of(jnp.minimum(owner + 1, 2 * n_dp - 1), 0)
        turned = lax.rem(LANES - lane_at, LANES)
        left = flat - off
        row = jnp.where(
            one_lane < LANES - lane_at, pltpu.roll(near, turned, axis=1), pltpu.roll(far, turned, axis=1)
        )
        return jnp.where(one_lane < left, row, pltpu.roll(beyond, lax.rem(left, LANES), axis=1))

    conv_end = (PLANES + 1) * channels

    def head_row(i, carry):
        row = flat_row(i * (PLANES + 1))
        head_conv[pl.ds(i, 1), :] = jnp.where(one_lane <= PLANES, row, 0.0)
        return carry

    lax.fori_loop(0, channels, head_row, 0, unroll=4)
    hidden_w[...] = jnp.zeros_like(hidden_w)

    def hidden_row(i, carry):
        line = i // 2
        line = jnp.where(line < 64, line, line + 64)
        hidden_w[lax.rem(i, 2), pl.ds(line, 1), :] = flat_row(conv_end + i * LANES)
        return carry

    lax.fori_loop(0, 2 * 66, hidden_row, 0, unroll=4)
    fetch_done(0, 0)
    if not own_taps:
        loads[2].wait()

    def push(k, g, top, bottom):
        slots[k, g, me, pl.ds(0, 1), :] = top
        slots[k, g, me, pl.ds(1, 1), :] = bottom

        def send(j, carry):
            pltpu.make_async_remote_copy(
                src_ref=slots.at[k, g, me],
                dst_ref=slots.at[k, g, me],
                send_sem=send_sem.at[k, g],
                recv_sem=recv_sem.at[k, g],
                device_id=(core, lax.rem(me + j, n_dp)),
                device_id_type=MESH,
            ).start()
            return carry

        lax.fori_loop(1, n_dp, send, 0)

    def arrived(k, g):
        others = slots.at[k, g, pl.ds(0, n_dp - 1)]
        copy = pltpu.make_async_remote_copy(
            src_ref=others, dst_ref=others, send_sem=send_sem.at[k, g], recv_sem=recv_sem.at[k, g],
            device_id=(core, lax.rem(me + 1, n_dp)), device_id_type=MESH,
        )
        copy.wait_send()
        copy.wait_recv()
        return slots[k, g]

    def merge_moments(k, g):
        parts = arrived(k, g)
        both_sums = jnp.sum(parts, axis=0)
        mean = both_sums[0:1] / n_dp
        apart = parts - mean
        between = jnp.sum(apart * apart, axis=0)[0:1]
        spread = (both_sums[1:2] + between * rows) / all_rows
        stat[k, g, pl.ds(0, 1), :] = mean
        stat[k, g, pl.ds(1, 1), :] = lax.rsqrt(spread + EPSILON)

    def norm_of(section, c, g):
        k = 2 * section + c
        gain = gains[section, pl.ds(c, 1), :]
        shift = gains[section, pl.ds(2 + c, 1), :]
        return stat[k, g, pl.ds(0, 1), :], stat[k, g, pl.ds(1, 1), :], gain, shift

    def convolve(field, section, c, g):
        k = 2 * section + c
        sums, parts = [], []
        for f in range(FOLD):
            slabs = [
                field[section, g, pl.ds(((f + t // 3) * PITCH + t % 3) * block, span), :] for t in range(9)
            ]
            out = jnp.dot(
                jnp.concatenate(slabs, axis=1), W[section, pl.ds(c * taps, taps), :],
                preferred_element_type=F32,
            )
            C[section, c, g, pl.ds(f * span, span), :] = out
            part = total(fold8(out))
            apart = out - part / span
            sums.append(part)
            parts.append(total(fold8(apart * apart)))
        mean = sum(sums) / rows
        spread = sum(parts)
        for part in sums:
            spread = spread + span * jnp.square(part / span - mean)
        push(k, g, mean, spread)

    def inner(section, g):
        mean, inv, gain, shift = norm_of(section, 0, g)
        factor = inv * gain

        def body(f, q, carry):
            v = (C[section, 0, g, plain(f, q), :] - mean) * factor + shift
            put(I, (section, g), f, q, v * sigmoid(v))
            return carry

        each(body)

    def outer_pre(section, g, f, q, norm):
        mean, inv, gain, shift = norm
        z = (C[section, 1, g, plain(f, q), :] - mean) * inv
        return X[section, g, inside(f, q), :].astype(F32) + z * gain + shift, z

    def for_groups(body):
        def step(g, carry):
            body(g)
            return carry

        lax.fori_loop(0, groups, step, 0)

    def entry_step(g):
        convolve(X, 0, 0, g)

        @pl.when(g == 0)
        def _():
            fetch_core(0, 1)
            fetch_column(1, 0)

    for_groups(entry_step)
    fetch_done(0, 1)
    for section in range(2):

        def inner_step(g, section=section):
            merge_moments(2 * section, g)
            inner(section, g)
            convolve(I, section, 1, g)
            if section == 0:

                @pl.when(g == 0)
                def _():
                    fetch_level(1, 0)
                    fetch_column(1, 1)

        for_groups(inner_step)
        if section == 0:
            fetch_core(1, 0)

            def hand_step(g):
                merge_moments(1, g)
                norm = norm_of(0, 1, g)

                def hand_on(f, q, carry):
                    v, _ = outer_pre(0, g, f, q, norm)
                    put(X, (1, g), f, q, v * sigmoid(v))
                    return carry

                each(hand_on)

                @pl.when(g == 0)
                def _():
                    fetch_done(1, 0)

                convolve(X, 1, 0, g)

                @pl.when(g == 0)
                def _():
                    fetch_level(1, 1)

            for_groups(hand_step)
            fetch_core(1, 1)
            fetch_done(1, 1)

    lane = lax.broadcasted_iota(jnp.int32, (per, LANES), 1)

    def heads(g):
        norm = norm_of(1, 1, g)

        def last(f, q, carry):
            v, _ = outer_pre(1, g, f, q, norm)
            B[g, plain(f, q), :] = v * sigmoid(v)
            return carry

        each(last)
        for f in range(FOLD):
            at = pl.ds(f * span, span)
            planes[at, :] = jnp.dot(B[g, at, :], head_conv[...], precision=PRECISE, preferred_element_type=F32)

        def look(f, q, carry):
            top, squares = carry
            a = planes[plain(f, q), :]
            a_legal = jnp.where(code[g, plain(f, q), :] > 0, a, ILLEGAL)
            top = jnp.maximum(top, jnp.maximum(a_legal[:per], a_legal[per:]))
            column = a[:, PLANES : PLANES + 1]
            for half in range(2):
                here = lane == (f + FOLD * half) * 8 + q
                squares = jnp.where(here, column[half * per : (half + 1) * per], squares)
            return top, squares

        top, pre = each(look, (jnp.full((per, LANES), ILLEGAL, F32), jnp.zeros((per, LANES), F32)))
        top = jnp.max(top, axis=1, keepdims=True)
        top = jnp.concatenate([top, top], axis=0)

        def weigh(f, q, acc):
            a = planes[plain(f, q), :]
            e = jnp.where(code[g, plain(f, q), :] > 0, jnp.exp(a - top), 0.0)
            planes[plain(f, q), :] = e
            return acc + e[:per] + e[per:]

        norm_sum = jnp.sum(each(weigh, jnp.zeros((per, LANES), F32)), axis=1, keepdims=True)
        portion = scale / norm_sum
        portion = jnp.concatenate([portion, portion], axis=0)

        squares = pre * sigmoid(pre)
        hidden_all = jnp.concatenate([hidden_w[0], hidden_w[1]], axis=1)
        hidden_in, bias, out_w = hidden_all[:LANES], hidden_all[LANES : LANES + 1], hidden_all[LANES + 1 : LANES + 2]
        hidden_pre = jnp.dot(squares, hidden_in, precision=PRECISE, preferred_element_type=F32) + bias
        hidden = hidden_pre * sigmoid(hidden_pre)
        value = jnp.tanh(jnp.sum(hidden * out_w, axis=1, keepdims=True))
        wanted = vgoal[pl.ds(g * per, per), 0:1]
        slope = 2.0 * scale * (value - wanted) * (1.0 - value * value)
        hidden_grad = slope * out_w * silu_slope(hidden_pre)
        hw_grad[pl.ds(0, 64), :] += lax.dot_general(
            squares, hidden_grad, (((0,), (0,)), ((), ())), precision=PRECISE, preferred_element_type=F32
        )[:64]
        hw_grad[pl.ds(64, 1), :] += total(hidden_grad)
        hw_grad[pl.ds(65, 1), :] += total(hidden * slope)
        squares_grad = lax.dot_general(
            hidden_grad, hidden_in, (((1,), (1,)), ((), ())), precision=PRECISE,
            preferred_element_type=F32,
        )
        pre_grad = squares_grad * silu_slope(pre)

        def slopes(f, q, carry):
            e = planes[plain(f, q), :] * portion
            e = e - jnp.where(code[g, plain(f, q), :] > 1.5, scale, 0.0)
            columns = [
                jnp.sum(jnp.where(lane == (f + FOLD * half) * 8 + q, pre_grad, 0.0), axis=1, keepdims=True)
                for half in range(2)
            ]
            column = jnp.concatenate(columns, axis=0)
            wide = lax.broadcasted_iota(jnp.int32, (block, LANES), 1)
            planes[plain(f, q), :] = jnp.where(wide == PLANES, column, e)
            return carry

        each(slopes)
        hc_grad[...] += lax.dot_general(
            B[g], planes[...], (((0,), (0,)), ((), ())), precision=PRECISE, preferred_element_type=F32
        )
        for f in range(FOLD):
            at = pl.ds(f * span, span)
            B[g, at, :] = lax.dot_general(
                planes[at, :], head_conv[...], (((1,), (1,)), ((), ())), precision=PRECISE,
                preferred_element_type=F32,
            )

    def outer_grad(section, g):
        norm = norm_of(section, 1, g)

        def body(f, q, carry):
            shift_sum, gain_sum = carry
            v, z = outer_pre(section, g, f, q, norm)
            grad = B[g, plain(f, q), :]
            if section == 0:
                grad = grad.astype(BF16).astype(F32)
            grad = grad * silu_slope(v)
            B[g, plain(f, q), :] = grad
            return shift_sum + fold8(grad), gain_sum + fold8(grad * z)

        zero = jnp.zeros((8, channels), F32)
        shift_sum, gain_sum = each(body, (zero, zero))
        push(4 + 2 * section + 1, g, total(shift_sum), total(gain_sum))

    def norm_back(section, c, g):
        sums = jnp.sum(arrived(4 + 2 * section + c, g), axis=0)
        norm_grad[pl.ds(4 * section + c, 1), :] += sums[1:2]
        norm_grad[pl.ds(4 * section + 2 + c, 1), :] += sums[0:1]
        mean, inv, gain, _ = norm_of(section, c, g)
        p_mean, pz_mean = sums[0:1] / all_rows, sums[1:2] / all_rows
        factor = inv * gain

        def body(f, q, carry):
            z = (C[section, c, g, plain(f, q), :] - mean) * inv
            p = B[g, plain(f, q), :] if c else C[section, 1, g, plain(f, q), :]
            put(Z, (g,), f, q, factor * (p - p_mean - z * pz_mean))
            return carry

        each(body)

    def back_field(section, c, g, f):
        acc = None
        for t in range(9):
            part = lax.dot_general(
                Z[g, pl.ds(((f + 2 - t // 3) * PITCH + 2 - t % 3) * block, span), :],
                W[section, pl.ds(c * taps + t * channels, channels), :],
                (((1,), (1,)), ((), ())), preferred_element_type=F32,
            )
            acc = part if acc is None else acc + part
        return acc

    def inner_grad(section, g):
        for f in range(FOLD):
            C[section, 1, g, pl.ds(f * span, span), :] = back_field(section, 1, g, f)
        mean, inv, gain, shift = norm_of(section, 0, g)

        def body(f, q, carry):
            shift_sum, gain_sum = carry
            z = (C[section, 0, g, plain(f, q), :] - mean) * inv
            grad = C[section, 1, g, plain(f, q), :] * silu_slope(z * gain + shift)
            C[section, 1, g, plain(f, q), :] = grad
            return shift_sum + fold8(grad), gain_sum + fold8(grad * z)

        zero = jnp.zeros((8, channels), F32)
        shift_sum, gain_sum = each(body, (zero, zero))
        push(4 + 2 * section, g, total(shift_sum), total(gain_sum))

    def entry(section, g):
        for f in range(FOLD):
            at = pl.ds(f * span, span)
            B[g, at, :] = B[g, at, :] + back_field(section, 0, g, f)

    def tap_gradient(section, c):
        field = I if c else X
        dz = jnp.concatenate(
            [Z[g, pl.ds(((f + 1) * PITCH + 1) * block, span), :] for g in range(groups) for f in range(FOLD)], axis=0
        )
        for t in range(9):
            moved = jnp.concatenate(
                [
                    field[section, g, pl.ds(((f + t // 3) * PITCH + t % 3) * block, span), :]
                    for g in range(groups)
                    for f in range(FOLD)
                ],
                axis=0,
            )
            grad = lax.dot_general(moved, dz, (((0,), (0,)), ((), ())), preferred_element_type=F32)
            stage[section, pl.ds(c * taps + t * channels, channels), :] = grad.astype(BF16)
        if not own_taps:
            at = pl.ds(c * taps, taps)
            pltpu.make_async_copy(stage.at[section, at], tap_out.at[section, at], reduce_sem.at[0, section, c]).start()
            return
        at = half_at(stage, section, c, 1 - core)
        k = 2 * section + c
        remote(
            at, siblings.at[k], reduce_sem.at[0, section, c], reduce_sem.at[1, section, c], 1 - core, me
        ).start()

    def reduce_level(section, c):
        if not own_taps:
            return
        k = 2 * section + c
        came(siblings.at[k], reduce_sem.at[1, section, c])
        own = half_at(stage, section, c, core)
        own[...] = (own[...].astype(F32) + siblings[k].astype(F32)).astype(BF16)
        for j in range(1, LAYER):
            place = lax.rem(spot + j, LAYER)
            part = own.at[pl.ds(pl.multiple_of(place * shard_rows, 16), shard_rows)]
            remote(
                part, layers.at[k, spot], reduce_sem.at[2, section, c], reduce_sem.at[3, section, c],
                core, level * LAYER + place,
            ).start()
        layers[k, spot] = own[pl.ds(pl.multiple_of(spot * shard_rows, 16), shard_rows), :]

    def reduce_column(section, c):
        if not own_taps:
            return
        k = 2 * section + c
        came(layers.at[k, pl.ds(0, LAYER - 1)], reduce_sem.at[3, section, c])
        columns[k] = sum(layers[k, j].astype(F32) for j in range(LAYER)).astype(BF16)
        to = arrivals.at[level]
        owner = 2 * c + core
        here = (core == section) & (owner == level)

        @pl.when(here)
        def _():
            pltpu.make_async_copy(columns.at[k], to, reduce_sem.at[5, 0, 0]).start()

        @pl.when(jnp.logical_not(here))
        def _():
            remote(
                columns.at[k], to, reduce_sem.at[4, section, c], reduce_sem.at[5, 0, 0],
                section, owner * LAYER + spot,
            ).start()

    def reduce_done():
        if not own_taps:
            return
        came(arrivals, reduce_sem.at[5, 0, 0])
        tap_out[...] = sum(arrivals[j].astype(F32) for j in range(levels))

    def conv_window(owner):
        start = jnp.minimum(owner * flat // (PLANES + 1), channels - HC_ROWS)
        return pl.multiple_of(start // 8 * 8, 8)

    def hidden_window(owner):
        start = jnp.maximum(owner * flat - conv_end, 0) // VHIDDEN
        return pl.multiple_of(jnp.minimum(start // 8 * 8, hw_grad.shape[0] - HW_ROWS), 8)

    def head_exchange():
        remote(hc_grad, hc_in, head_sem.at[0], head_sem.at[1], 1 - core, me).start()
        remote(hw_grad, hw_in, head_sem.at[2], head_sem.at[3], 1 - core, me).start()

    def head_spread():
        sent(hc_grad, head_sem.at[0])
        sent(hw_grad, head_sem.at[2])
        came(hc_in, head_sem.at[1])
        came(hw_in, head_sem.at[3])
        hc_grad[...] += hc_in[...]
        hw_grad[...] += hw_in[...]

        def spread(j, carry):
            peer = lax.rem(me + j, n_dp)
            owner = core * n_dp + peer

            @pl.when(owner * flat < conv_end)
            def _():
                window = hc_grad.at[pl.ds(conv_window(owner), HC_ROWS)]
                remote(window, hc_slots.at[me], head_sem.at[4], head_sem.at[5], core, peer).start()

            @pl.when((owner + 1) * flat > conv_end)
            def _():
                window = hw_grad.at[pl.ds(hidden_window(owner), HW_ROWS)]
                remote(window, hw_slots.at[me], head_sem.at[6], head_sem.at[7], core, peer).start()

            return carry

        lax.fori_loop(1, n_dp, spread, 0)
        owner = core * n_dp + me
        hc_slots[me] = hc_grad[pl.ds(conv_window(owner), HC_ROWS), :]
        hw_slots[me] = hw_grad[pl.ds(hidden_window(owner), HW_ROWS), :]

    def head_done():
        owner = core * n_dp + me
        lines = small_out.shape[0] - 2

        def unsent(j, carry):
            peer = core * n_dp + lax.rem(me + j, n_dp)

            @pl.when(peer * flat < conv_end)
            def _():
                sent(hc_slots.at[0], head_sem.at[4])

            @pl.when((peer + 1) * flat > conv_end)
            def _():
                sent(hw_slots.at[0], head_sem.at[6])

            return carry

        lax.fori_loop(1, n_dp, unsent, 0)

        @pl.when(owner * flat < conv_end)
        def _():
            came(hc_slots.at[pl.ds(0, n_dp - 1)], head_sem.at[5])
            hc_in[pl.ds(0, HC_ROWS), :] = jnp.sum(hc_slots[...], axis=0)
            for line in range(lines):
                start = owner * flat + line * LANES
                row = start // (PLANES + 1)
                off = start - row * (PLANES + 1)
                out = jnp.zeros((1, LANES), F32)
                for m in range(3):
                    at = jnp.clip(row + m - conv_window(owner), 0, HC_ROWS - 1)
                    begin = (PLANES + 1) * m - off
                    part = pltpu.roll(hc_in[pl.ds(at, 1), :], lax.rem(begin + LANES, LANES), axis=1)
                    fits = (one_lane >= begin) & (one_lane < begin + PLANES + 1) & (start + one_lane < conv_end)
                    out = jnp.where(fits, part, out)
                small_out[pl.ds(2 + line, 1), :] = out

        @pl.when((owner + 1) * flat > conv_end)
        def _():
            came(hw_slots.at[pl.ds(0, n_dp - 1)], head_sem.at[7])
            window = jnp.sum(hw_slots[...], axis=0)
            for i in range(2):
                hidden_w[i, pl.ds(0, HW_ROWS), :] = window[:, i * LANES : (i + 1) * LANES]
            for line in range(lines):
                start = owner * flat + line * LANES
                from_end = start - conv_end + 64 * LANES
                row = from_end // LANES
                off = from_end - row * LANES
                out = small_out[pl.ds(2 + line, 1), :]
                for m in range(2):
                    at = jnp.clip(row + m - 64 - 2 * hidden_window(owner), 0, 2 * HW_ROWS - 1)
                    begin = LANES * m - off
                    part = hidden_w[lax.rem(at, 2), pl.ds(at // 2, 1), :]
                    part = pltpu.roll(part, lax.rem(begin + LANES, LANES), axis=1)
                    fits = (one_lane >= begin) & (one_lane < begin + LANES) & (start + one_lane >= conv_end)
                    out = jnp.where(fits, part, out)
                small_out[pl.ds(2 + line, 1), :] = out

    def norm_exchange():
        remote(norm_grad, norm_in, head_sem.at[8], head_sem.at[9], 1 - core, me).start()

    def norm_done():
        came(norm_in, head_sem.at[9])
        sent(norm_grad, head_sem.at[8])
        at = me * share
        tile, off = at // LANES, lax.rem(at, LANES)
        sums = norm_grad[...] + norm_in[...]
        for i in range(2):
            hidden_w[i, pl.ds(0, 8), :] = sums[:, i * LANES : (i + 1) * LANES]
        for i in range(2):
            part = hidden_w[lax.rem(tile, 2), pl.ds(4 * core + 2 * i + tile // 2, 1), :]
            small_out[pl.ds(i, 1), :] = pltpu.roll(part, lax.rem(LANES - off, LANES), axis=1)

    small_out[...] = jnp.zeros_like(small_out)

    def head_step(g):
        merge_moments(3, g)
        heads(g)
        outer_grad(1, g)

    for_groups(head_step)
    head_exchange()
    for section in (1, 0):

        def second_step(g, section=section):
            norm_back(section, 1, g)
            inner_grad(section, g)

        for_groups(second_step)
        if section == 1:
            head_spread()
        else:
            reduce_column(1, 1)
            reduce_level(1, 0)
        tap_gradient(section, 1)

        def first_step(g, section=section):
            norm_back(section, 0, g)
            if section == 1:
                entry(section, g)
                outer_grad(0, g)

        for_groups(first_step)
        if section == 1:
            reduce_level(1, 1)
        else:
            reduce_column(1, 0)
            reduce_level(0, 1)
            norm_exchange()
        tap_gradient(section, 0)

    def last_step(g):
        entry(0, g)

        def restore(f, q, carry):
            v = B[g, plain(f, q), :]
            for half in range(2):
                for i in range(channels // LANES):
                    part = v[half * per : (half + 1) * per, i * LANES : (i + 1) * LANES]
                    turn[i, pl.ds((f + FOLD * half) * 8 + q, per, stride=64), :] = part
            return carry

        each(restore)
        for f in range(FOLD):
            at = pl.ds(f * span, span)
            to = pl.ds(pl.multiple_of(g * rows + f * span, 16), span)
            mine[to, :] = turn[core, at, :].astype(BF16)
            theirs[to, :] = turn[1 - core, at, :].astype(BF16)

        @pl.when(g == 0)
        def _():
            reduce_level(0, 0)
            reduce_column(0, 1)

    for_groups(last_step)
    own = pl.ds(pl.multiple_of(core * groups * rows, 16), groups * rows)
    swap = remote(theirs, entry_grad.at[own], swap_sem.at[0], swap_sem.at[1], 1 - core, me)
    swap.start()
    keep = pltpu.make_async_copy(mine, entry_grad.at[own], swap_sem.at[2])
    keep.start()
    reduce_column(0, 0)
    head_done()
    norm_done()

    sent(packs.at[core, pl.ds(0, n_dp - 1)], pack_sem.at[0])
    sent(packs.at[core], pack_sem.at[2])
    for section in range(2):
        for c in range(2):
            k = 2 * section + c
            if not own_taps:
                at = pl.ds(c * taps, taps)
                pltpu.make_async_copy(
                    stage.at[section, at], tap_out.at[section, at], reduce_sem.at[0, section, c]
                ).wait()
                continue
            three = stage.at[section, pl.ds(0, (LAYER - 1) * shard_rows)]

            @pl.when((core == section) & (level // 2 == c))
            def _(section=section, c=c):
                sent(stage.at[section, pl.ds(0, (levels - 1) * shard_rows)], fetch_sem.at[0, section, c])

                @pl.when(lax.rem(level, 2) != core)
                def _():
                    sent(stage.at[section, pl.ds(0, shard_rows)], fetch_sem.at[0, section, c])

            sent(three, fetch_sem.at[2, section, c])
            sent(half_at(stage, section, c, core), fetch_sem.at[4, section, c])
            sent(siblings.at[k], reduce_sem.at[0, section, c])
            sent(three, reduce_sem.at[2, section, c])

            @pl.when(jnp.logical_not((core == section) & (2 * c + core == level)))
            def _(section=section, c=c, k=k):
                sent(columns.at[k], reduce_sem.at[4, section, c])

    reduce_done()
    keep.wait()
    swap.wait()


def local(
    board_input, conv_weight, norm_gains, norm_shifts, head_params, policy_target, legal_mask, value_target
):
    n_dp, n_pipe = lax.axis_size("dp"), lax.axis_size("pipe")
    positions, channels = board_input.shape[0], board_input.shape[-1]
    per = positions // MICRO
    groups = MICRO // n_pipe
    moves = legal_mask.shape[1]
    rows = per * 64
    padded = (FOLD + 2) * PITCH * 2 * per
    taps = 9 * channels

    shard_rows = conv_weight.shape[1]
    own_taps = shard_rows % 16 == 0 and n_dp == 4 * LAYER
    share, flat = norm_gains.shape[1], head_params.shape[0]
    lines = -(-flat // LANES)
    pack_rows = -(-(2 + lines) // 8) * 8
    head_rows = jnp.pad(head_params, (0, (pack_rows - 2) * LANES - flat)).reshape(pack_rows - 2, LANES)
    norms = jnp.pad(jnp.concatenate([norm_gains, norm_shifts]).astype(F32), ((0, 0), (0, LANES - share)))
    small = jnp.concatenate([norms, head_rows])
    taps_in = conv_weight
    if not own_taps:
        taps_in = lax.all_gather(lax.all_gather(conv_weight, "dp", axis=1, tiled=True), "pipe", axis=0, tiled=True)

    vmem = pl.BlockSpec(memory_space=pltpu.VMEM)
    smem = pl.BlockSpec(memory_space=pltpu.SMEM)
    anywhere = pl.BlockSpec(memory_space=pl.ANY)
    dma, regular = pltpu.SemaphoreType.DMA, pltpu.VMEM
    tap_shape = (shard_rows, channels) if own_taps else (2, 2 * taps, channels)
    lane_rows = shard_rows if own_taps else 16
    tap_grad, small_grad, entry_grad = pl.pallas_call(
        functools.partial(
            kernel, (n_dp, per, groups, moves, 1.0 / positions, shard_rows, own_taps, flat)
        ),
        out_shape=(
            jax.ShapeDtypeStruct(tap_shape, F32 if own_taps else BF16),
            jax.ShapeDtypeStruct((pack_rows, LANES), F32),
            jax.ShapeDtypeStruct((positions * 64, LANES), BF16),
        ),
        in_specs=[smem, smem, anywhere, anywhere, vmem, anywhere],
        out_specs=(vmem if own_taps else anywhere, vmem, anywhere),
        scratch_shapes=[
            regular((2, 2 * taps, channels), BF16),
            regular((2, groups, padded, channels), BF16),
            regular((2, groups, padded, channels), BF16),
            regular((groups, padded, channels), BF16),
            regular((2, 2, groups, rows, channels), F32),
            regular((groups, rows, channels), F32),
            regular((groups * per, 8, 8, channels), BF16),
            regular((groups * per, moves), jnp.int32),
            regular((groups, rows, LANES), F32),
            regular((rows, LANES), F32),
            regular((channels // LANES, rows, LANES), F32),
            regular((groups * per, LANES), jnp.int32),
            regular((groups * per, LANES), F32),
            regular((2, 2 * taps, channels), BF16),
            regular((4, groups, 8, channels), F32),
            regular((8, groups, n_dp, 2, channels), F32),
            regular((groups * rows, LANES), BF16),
            regular((groups * rows, LANES), BF16),
            regular((2, n_dp, pack_rows, LANES), F32),
            regular((2, 8, channels), F32),
            regular((channels, LANES), F32),
            regular((2, LANES + 8, LANES), F32),
            regular((8, channels), F32),
            regular((channels, LANES), F32),
            regular((72, VHIDDEN), F32),
            regular((8, channels), F32),
            regular((channels, LANES), F32),
            regular((72, VHIDDEN), F32),
            regular((n_dp, HC_ROWS, LANES), F32),
            regular((n_dp, HW_ROWS, VHIDDEN), F32),
            regular((4, LAYER * lane_rows, channels), BF16),
            regular((4, LAYER, lane_rows, channels), BF16),
            regular((4, lane_rows, channels), BF16),
            regular((4, lane_rows, channels), BF16),
            dma((3,)),
            dma((8, groups)),
            dma((8, groups)),
            dma((3,)),
            dma((4,)),
            dma((10,)),
            dma((6, 2, 2)),
            dma((6, 2, 2)),
        ],
        compiler_params=pltpu.CompilerParams(
            collective_id=0, has_side_effects=True, vmem_limit_bytes=63 * 2**20
        ),
    )(policy_target, value_target, board_input, taps_in, small, legal_mask)

    conv_grad = tap_grad
    if not own_taps:
        conv_grad = lax.psum_scatter(
            tap_grad.astype(F32).reshape(4 * taps, channels), ("pipe", "dp"), scatter_dimension=0, tiled=True
        )
    head_grad = small_grad[2:].reshape(-1)[:flat]
    entry_grad = entry_grad.astype(F32).reshape(positions, 8, 8, LANES)
    return conv_grad[None], small_grad[0:1, :share], small_grad[1:2, :share], head_grad, entry_grad


def solution(mesh):
    placed = (
        P("dp", None, None, None),
        P("pipe", "dp", None),
        P("pipe", "dp"),
        P("pipe", "dp"),
        P(("pipe", "dp")),
        P("dp"),
        P("dp", None),
        P("dp"),
    )
    return jax.shard_map(
        local,
        mesh=mesh,
        in_specs=placed,
        out_specs=(
            P("pipe", "dp", None),
            P("pipe", "dp"),
            P("pipe", "dp"),
            P(("pipe", "dp")),
            P("dp", None, None, "pipe"),
        ),
        check_vma=False,
    )
```

```python
import functools

import jax
import jax.numpy as jnp
from jax import lax
from jax.experimental import pallas as pl
from jax.experimental.pallas import tpu as pltpu
from jax.sharding import PartitionSpec as P

PLANES = 73
VHIDDEN = 256
MICRO = 4
EPSILON = 1e-05
F32, BF16 = jnp.float32, jnp.bfloat16
PRECISE = lax.Precision.HIGHEST
MESH = pl.DeviceIdType.MESH
LANES = 128
ILLEGAL = -1e30
HC_ROWS, HW_ROWS = 24, 16
LAYER = 4
CUTS = 3
COLS = 8

FOLD, WIDE, PITCH = 4, 8, 10


def sigmoid(v):
    return 0.5 * jnp.tanh(0.5 * v) + 0.5


def silu_slope(v):
    s = sigmoid(v)
    return s * (1.0 + v * (1.0 - s))


def fold8(v):
    return jnp.sum(v.reshape(v.shape[0] // 8, 8, v.shape[1]), axis=0)


def total(v):
    return jnp.sum(v, axis=0, keepdims=True)


def kernel(
    sizes, policy, value_goal, board, shard, small, legal,
    tap_out, small_out, entry_grad,
    W, X, I, Z, C, B, raw, mask_raw, code, planes, turn, goal, vgoal, stage, stat, slots, mine, theirs,
    packs, gains, head_conv, head_pair, hidden_w, norm_grad, hc_grad, hw_grad, norm_in, hc_in, hw_in, hc_slots, hw_slots,
    siblings, layers, columns, arrivals,
    load_sem, send_sem, recv_sem, swap_sem, pack_sem, head_sem, fetch_sem, reduce_sem,
):
    n_dp, per, groups, moves, scale, shard_rows, own_taps, flat = sizes
    core, me = lax.axis_index("pipe"), lax.axis_index("dp")
    block = 2 * per
    span = WIDE * block
    rows = FOLD * span
    channels = X.shape[-1]
    taps = 9 * channels
    all_rows = n_dp * rows
    spot, level = lax.rem(me, LAYER), me // LAYER
    levels = n_dp // LAYER

    def remote(src, dst, send, recv, pipe, dp):
        return pltpu.make_async_remote_copy(
            src_ref=src, dst_ref=dst, send_sem=send, recv_sem=recv, device_id=(pipe, dp), device_id_type=MESH
        )

    def sent(ref, sem):
        remote(ref, ref, sem, sem, 1 - core, me).wait_send()

    def came(ref, sem):
        remote(ref, ref, sem, sem, 1 - core, me).wait_recv()

    barrier = pltpu.get_barrier_semaphore()

    def greet(j, carry):
        pl.semaphore_signal(barrier, inc=1, device_id=(core, lax.rem(me + j, n_dp)), device_id_type=MESH)
        return carry

    def greet_column(j, carry):
        other = lax.rem(me + j * LAYER, n_dp)
        pl.semaphore_signal(barrier, inc=1, device_id=(1 - core, other), device_id_type=MESH)
        return carry

    lax.fori_loop(1, n_dp, greet, 0)
    lax.fori_loop(0, levels, greet_column, 0)

    first = pl.multiple_of(core * groups * per, 8)
    loads = [
        pltpu.make_async_copy(board.at[pl.ds(first, groups * per)], raw, load_sem.at[0]),
        pltpu.make_async_copy(legal.at[pl.ds(first, groups * per)], mask_raw, load_sem.at[1]),
    ]
    if not own_taps:
        loads.append(pltpu.make_async_copy(shard, W, load_sem.at[2]))
    for load in loads:
        load.start()
    pl.semaphore_wait(barrier, n_dp - 1 + levels)

    def shard_at(section, c, half, place):
        start = c * taps + (half * LAYER + place) * shard_rows
        return W.at[section, pl.ds(pl.multiple_of(start, 16), shard_rows)]

    def half_at(ref, section, c, half):
        start = c * taps + half * LAYER * shard_rows
        return ref.at[section, pl.ds(pl.multiple_of(start, 16), LAYER * shard_rows)]

    def cuts_of(section, c):
        return CUTS if section + c == 0 else 1

    def cut_at(ref, section, c, cut):
        some = shard_rows // cuts_of(section, c)
        return ref.at[pl.ds(cut * some, some)]

    def fetch_column(section, c):
        if not own_taps:
            return

        @pl.when((core == section) & (level // 2 == c))
        def _():
            half = lax.rem(level, 2)
            for cut in range(cuts_of(section, c)):
                at = cut_at(shard_at(section, c, half, spot), section, c, cut)
                src = cut_at(shard.at[0], section, c, cut)
                send, recv = fetch_sem.at[0, section, c, 0], fetch_sem.at[1, section, c, cut]
                for j in range(1, levels):
                    remote(src, at, send, recv, half, lax.rem(me + j * LAYER, n_dp)).start()

                @pl.when(half == core)
                def _(src=src, at=at, recv=recv):
                    pltpu.make_async_copy(src, at, recv).start()

                @pl.when(half != core)
                def _(src=src, at=at, send=send, recv=recv):
                    remote(src, at, send, recv, half, me).start()

    def fetch_level(section, c, cut=0):
        if not own_taps:
            return
        at = cut_at(shard_at(section, c, core, spot), section, c, cut)
        came(at, fetch_sem.at[1, section, c, cut])
        for j in range(1, LAYER):
            peer = level * LAYER + lax.rem(spot + j, LAYER)
            remote(at, at, fetch_sem.at[2, section, c, 0], fetch_sem.at[3, section, c, cut], core, peer).start()

    def fetch_core(section, c):
        if not own_taps:
            return
        for cut in range(cuts_of(section, c)):
            some = W.at[section, pl.ds(c * taps, (LAYER - 1) * shard_rows // cuts_of(section, c))]
            came(some, fetch_sem.at[3, section, c, cut])
        at = half_at(W, section, c, core)
        remote(at, at, fetch_sem.at[4, section, c, 0], fetch_sem.at[5, section, c, 0], 1 - core, me).start()

    def fetch_done(section, c):
        if not own_taps:
            return
        came(half_at(W, section, c, 1 - core), fetch_sem.at[5, section, c, 0])

    def send_pack(j, carry):
        remote(
            small, packs.at[core, me], pack_sem.at[0], pack_sem.at[1], core, lax.rem(me + j, n_dp)
        ).start()
        return carry

    fetch_column(0, 0)
    fetch_column(0, 1)

    wide = COLS * block

    def padded(f, q):
        return pl.ds(((f + 1) * PITCH + 1 + q) * block, wide)

    def put(ref, at, f, q, y):
        ref[*at, padded(f, q), :] = y.astype(BF16)
        none = jnp.zeros((COLS, per, channels), F32)
        parts = y.reshape(COLS, block, channels)
        if f == FOLD - 1:
            halo = jnp.concatenate([none, parts[:, :per]], axis=1).reshape(wide, channels)
            ref[*at, padded(-1, q), :] = halo.astype(BF16)
        if f == 0:
            halo = jnp.concatenate([parts[:, per:], none], axis=1).reshape(wide, channels)
            ref[*at, padded(FOLD, q), :] = halo.astype(BF16)

    def plain(f, q):
        return pl.ds((f * WIDE + q) * block, wide)

    def each(body, carry=0):
        for q in range(0, WIDE, COLS):
            for f in range(FOLD):
                carry = body(f, q, carry)
        return carry

    def halves(f, q):
        for i in range(COLS):
            for half in range(2):
                yield pl.ds((2 * i + half) * per, per), (f + FOLD * half) * 8 + q + i

    def part_of(v, at):
        return v[at.start : at.start + per]

    loads[0].wait()
    for g in range(groups):

        def widen(b, carry, g=g):
            rows_of = raw[g * per + b].astype(F32).reshape(64, channels)
            for i in range(channels // LANES):
                turn[i, pl.ds(pl.multiple_of(b * 64, 64), 64), :] = rows_of[:, i * LANES : (i + 1) * LANES]
            return carry

        lax.fori_loop(0, per, widen, 0)

        def reorder(f, q, carry, g=g):
            parts = [
                jnp.concatenate([turn[i, pl.ds(square, per, stride=64), :] for _, square in halves(f, q)], axis=0)
                for i in range(channels // LANES)
            ]
            put(X, (0, g), f, q, jnp.concatenate(parts, axis=1))
            return carry

        each(reorder)
        if g < CUTS - 1:
            fetch_level(0, 0, g)

    for cut in range(min(groups, CUTS - 1), CUTS):
        fetch_level(0, 0, cut)
    packs[core, me] = small[...]
    lax.fori_loop(1, n_dp, send_pack, 0)
    fetch_level(0, 1)
    fetch_column(1, 0)

    both = groups * per
    row_of = lax.broadcasted_iota(jnp.int32, (both, LANES), 0)
    lane_of = lax.broadcasted_iota(jnp.int32, (both, LANES), 1)

    def column_of(ref, zero):
        def pick(b, acc):
            return jnp.where(row_of == b, ref[first + b], acc)

        return lax.fori_loop(0, both, pick, zero)

    goal[...] = column_of(policy, jnp.zeros((both, LANES), jnp.int32))
    vgoal[...] = column_of(value_goal, jnp.zeros((both, LANES), F32))
    loads[1].wait()
    for square in range(64):
        base = square * PLANES // LANES * LANES
        shift = square * PLANES - base
        width = min(2 * LANES, moves - base)
        window = mask_raw[:, base : base + width]
        if width < 2 * LANES:
            window = jnp.concatenate([window, jnp.zeros((both, 2 * LANES - width), jnp.int32)], axis=1)
        if shift:
            window = pltpu.roll(window, 2 * LANES - shift, axis=1)
        window = window[:, :LANES]
        hit = goal[...] == lane_of + square * PLANES
        kind = jnp.where(hit, 2.0, jnp.where(window > 0, 1.0, 0.0))
        kind = jnp.where(lane_of < PLANES, kind, 0.0)
        f, q, half = square // 8 % FOLD, square % 8, square // 8 // FOLD
        at = ((f * WIDE + q) * 2 + half) * per
        for g in range(groups):
            code[g, pl.ds(at, per), :] = kind[g * per : (g + 1) * per]

    hc_grad[...] = jnp.zeros_like(hc_grad)
    hw_grad[...] = jnp.zeros_like(hw_grad)
    norm_grad[...] = jnp.zeros_like(norm_grad)
    fetch_core(0, 0)
    came(packs.at[core, pl.ds(0, n_dp - 1)], pack_sem.at[1])
    remote(packs.at[core], packs.at[core], pack_sem.at[2], pack_sem.at[3], 1 - core, me).start()

    share = 2 * channels // n_dp

    def unpack_gains():
        tile_share = LANES // share
        for section in range(2):
            for tile in range(2 * channels // LANES):
                acc = jnp.zeros((2, LANES), F32)
                for u in range(tile_share):
                    part = packs[section, tile * tile_share + u, pl.ds(0, 2), :]
                    acc = acc + (pltpu.roll(part, u * share, axis=1) if u else part)
                c, at = tile * LANES // channels, tile * LANES % channels
                gains[section, pl.ds(c, 1), pl.ds(at, LANES)] = acc[0:1]
                gains[section, pl.ds(2 + c, 1), pl.ds(at, LANES)] = acc[1:2]

    one_lane = lax.broadcasted_iota(jnp.int32, (1, LANES), 1)
    conv_end = (PLANES + 1) * channels

    def flat_row(start, count):
        owner, off = divmod(start, flat)
        line, lane_at = divmod(off, LANES)

        def line_of(owner, line, back):
            row = packs[owner // n_dp, owner % n_dp, pl.ds(line + 2, 1), :]
            return pltpu.roll(row, back % LANES, axis=1) if back % LANES else row

        row = line_of(owner, line, -lane_at)
        if lane_at + count > LANES and off + LANES - lane_at < flat:
            row = jnp.where(one_lane < LANES - lane_at, row, line_of(owner, line + 1, -lane_at))
        if off + count > flat:
            row = jnp.where(one_lane < flat - off, row, line_of(owner + 1, 0, flat - off))
        return jnp.where(one_lane < count, row, 0.0) if count < LANES else row

    def unpack_heads():
        for i in range(channels):
            head_conv[pl.ds(i, 1), :] = flat_row(i * (PLANES + 1), PLANES + 1)
        near = head_conv[...].astype(BF16)
        rest = (head_conv[...] - near.astype(F32)).astype(BF16)
        head_pair[0] = jnp.concatenate([near, rest], axis=1)
        head_pair[1] = jnp.concatenate([near, near], axis=1)
        hidden_w[...] = jnp.zeros_like(hidden_w)
        for i in range(2 * 66):
            line = i // 2 if i < 128 else i // 2 + 64
            hidden_w[i % 2, pl.ds(line, 1), :] = flat_row(conv_end + i * LANES, LANES)

    fetch_done(0, 0)
    if not own_taps:
        loads[2].wait()

    def push(k, g, top, bottom):
        slots[k, g, me, pl.ds(0, 1), :] = top
        slots[k, g, me, pl.ds(1, 1), :] = bottom

        def send(j, carry):
            pltpu.make_async_remote_copy(
                src_ref=slots.at[k, g, me],
                dst_ref=slots.at[k, g, me],
                send_sem=send_sem.at[k, g],
                recv_sem=recv_sem.at[k, g],
                device_id=(core, lax.rem(me + j, n_dp)),
                device_id_type=MESH,
            ).start()
            return carry

        lax.fori_loop(1, n_dp, send, 0)

    def arrived(k, g):
        others = slots.at[k, g, pl.ds(0, n_dp - 1)]
        copy = pltpu.make_async_remote_copy(
            src_ref=others, dst_ref=others, send_sem=send_sem.at[k, g], recv_sem=recv_sem.at[k, g],
            device_id=(core, lax.rem(me + 1, n_dp)), device_id_type=MESH,
        )
        copy.wait_send()
        copy.wait_recv()
        return slots[k, g]

    def merge_moments(k, g):
        parts = arrived(k, g)
        both_sums = jnp.sum(parts, axis=0)
        mean = both_sums[0:1] / n_dp
        apart = parts - mean
        between = jnp.sum(apart * apart, axis=0)[0:1]
        spread = (both_sums[1:2] + between * rows) / all_rows
        stat[k, g, pl.ds(0, 1), :] = mean
        stat[k, g, pl.ds(1, 1), :] = lax.rsqrt(spread + EPSILON)

    def norm_of(section, c, g):
        k = 2 * section + c
        gain = gains[section, pl.ds(c, 1), :]
        shift = gains[section, pl.ds(2 + c, 1), :]
        return stat[k, g, pl.ds(0, 1), :], stat[k, g, pl.ds(1, 1), :], gain, shift

    def slab(field, at, f, q, width, t):
        start = ((f + t // 3) * PITCH + q + t % 3) * block
        return field[*at, pl.ds(start, width * block), :]

    def taps_of(section, c, some):
        return [W[section, pl.ds(c * taps + t * channels, channels), :] for t in some]

    def convolve(field, section, c, g):
        k = 2 * section + c
        counted = []

        def note(out, count):
            part = total(fold8(out))
            apart = out - part / count
            counted.append((part, total(fold8(apart * apart)), count))

        middle = W[section, pl.ds(c * taps, taps), :]
        for f in range(FOLD):
            slabs = [slab(field, (section, g), f, 1, WIDE - 2, t) for t in range(9)]
            out = jnp.dot(jnp.concatenate(slabs, axis=1), middle, preferred_element_type=F32)
            C[section, c, g, pl.ds(f * span + block, span - 2 * block), :] = out
            note(out, span - 2 * block)
        for q, skip in ((0, 0), (WIDE - 1, 2)):
            some = [t for t in range(9) if t % 3 != skip]
            slabs = [
                jnp.concatenate([slab(field, (section, g), f, q, 1, t) for t in some], axis=1) for f in range(FOLD)
            ]
            out = jnp.dot(
                jnp.concatenate(slabs, axis=0), jnp.concatenate(taps_of(section, c, some), axis=0),
                preferred_element_type=F32,
            )
            for f in range(FOLD):
                C[section, c, g, pl.ds(f * span + q * block, block), :] = out[f * block : (f + 1) * block]
            note(out, FOLD * block)
        mean = sum(part for part, _, _ in counted) / rows
        spread = sum(apart for _, apart, _ in counted)
        for part, _, count in counted:
            spread = spread + count * jnp.square(part / count - mean)
        push(k, g, mean, spread)

    def inner(section, g):
        mean, inv, gain, shift = norm_of(section, 0, g)
        factor = inv * gain

        def body(f, q, carry):
            v = (C[section, 0, g, plain(f, q), :] - mean) * factor + shift
            put(I, (section, g), f, q, v * sigmoid(v))
            return carry

        each(body)

    def outer_pre(section, g, f, q, norm):
        mean, inv, gain, shift = norm
        z = (C[section, 1, g, plain(f, q), :] - mean) * inv
        return X[section, g, padded(f, q), :].astype(F32) + z * gain + shift, z

    def for_groups(body):
        def step(g, carry):
            body(g)
            return carry

        lax.fori_loop(0, groups, step, 0)

    def entry_step(g):
        convolve(X, 0, 0, g)

        @pl.when(g == 0)
        def _():
            fetch_level(1, 0)
            fetch_column(1, 1)

    for_groups(entry_step)
    came(packs.at[1 - core], pack_sem.at[3])
    unpack_gains()
    unpack_heads()
    fetch_core(0, 1)
    for section in range(2):

        def inner_step(g, section=section):
            merge_moments(2 * section, g)
            inner(section, g)
            if section == 0:

                @pl.when(g == 0)
                def _():
                    fetch_done(0, 1)

            if section == 1:

                @pl.when(g == 0)
                def _():
                    fetch_done(1, 1)

            convolve(I, section, 1, g)
            if section == 0:

                @pl.when(g == 0)
                def _():
                    fetch_level(1, 1)

        for_groups(inner_step)
        if section == 0:
            fetch_core(1, 0)

            def hand_step(g):
                merge_moments(1, g)
                norm = norm_of(0, 1, g)

                def hand_on(f, q, carry):
                    v, _ = outer_pre(0, g, f, q, norm)
                    put(X, (1, g), f, q, v * sigmoid(v))
                    return carry

                each(hand_on)

                @pl.when(g == 0)
                def _():
                    fetch_done(1, 0)

                convolve(X, 1, 0, g)

            for_groups(hand_step)
            fetch_core(1, 1)

    lane = lax.broadcasted_iota(jnp.int32, (per, LANES), 1)

    def heads(g):
        norm = norm_of(1, 1, g)

        near, rest, slope_parts = stage.at[0, pl.ds(0, rows)], stage.at[0, pl.ds(rows, rows)], stage.at[1, pl.ds(0, rows)]

        def last(f, q, carry):
            v, _ = outer_pre(1, g, f, q, norm)
            final = v * sigmoid(v)
            head = final.astype(BF16)
            near[plain(f, q), :] = head
            rest[plain(f, q), :] = (final - head.astype(F32)).astype(BF16)
            return carry

        each(last)
        for f in range(FOLD):
            at = pl.ds(f * span, span)
            large = jnp.dot(near[at, :], head_pair[0], preferred_element_type=F32)
            small_part = jnp.dot(rest[at, :], head_pair[0, :, :LANES], preferred_element_type=F32)
            planes[at, :] = large[:, :LANES] + (large[:, LANES:] + small_part)

        def look(f, q, carry):
            top, squares = carry
            a = planes[plain(f, q), :]
            a_legal = jnp.where(code[g, plain(f, q), :] > 0, a, ILLEGAL)
            column = a[:, PLANES : PLANES + 1]
            for at, square in halves(f, q):
                top = jnp.maximum(top, part_of(a_legal, at))
                squares = jnp.where(lane == square, part_of(column, at), squares)
            return top, squares

        top, pre = each(look, (jnp.full((per, LANES), ILLEGAL, F32), jnp.zeros((per, LANES), F32)))
        top = jnp.max(top, axis=1, keepdims=True)
        top = jnp.concatenate([top] * (2 * COLS), axis=0)

        def weigh(f, q, acc):
            a = planes[plain(f, q), :]
            e = jnp.where(code[g, plain(f, q), :] > 0, jnp.exp(a - top), 0.0)
            planes[plain(f, q), :] = e
            return acc + jnp.sum(e.reshape(2 * COLS, per, LANES), axis=0)

        norm_sum = jnp.sum(each(weigh, jnp.zeros((per, LANES), F32)), axis=1, keepdims=True)
        portion = scale / norm_sum
        portion = jnp.concatenate([portion] * (2 * COLS), axis=0)

        squares = pre * sigmoid(pre)
        hidden_all = jnp.concatenate([hidden_w[0], hidden_w[1]], axis=1)
        hidden_in, bias, out_w = hidden_all[:LANES], hidden_all[LANES : LANES + 1], hidden_all[LANES + 1 : LANES + 2]
        hidden_pre = jnp.dot(squares, hidden_in, precision=PRECISE, preferred_element_type=F32) + bias
        hidden = hidden_pre * sigmoid(hidden_pre)
        value = jnp.tanh(jnp.sum(hidden * out_w, axis=1, keepdims=True))
        wanted = vgoal[pl.ds(g * per, per), 0:1]
        slope = 2.0 * scale * (value - wanted) * (1.0 - value * value)
        hidden_grad = slope * out_w * silu_slope(hidden_pre)
        hw_grad[pl.ds(0, 64), :] += lax.dot_general(
            squares, hidden_grad, (((0,), (0,)), ((), ())), precision=PRECISE, preferred_element_type=F32
        )[:64]
        hw_grad[pl.ds(64, 1), :] += total(hidden_grad)
        hw_grad[pl.ds(65, 1), :] += total(hidden * slope)
        squares_grad = lax.dot_general(
            hidden_grad, hidden_in, (((1,), (1,)), ((), ())), precision=PRECISE,
            preferred_element_type=F32,
        )
        pre_grad = squares_grad * silu_slope(pre)

        def slopes(f, q, carry):
            e = planes[plain(f, q), :] * portion
            e = e - jnp.where(code[g, plain(f, q), :] > 1.5, scale, 0.0)
            column = jnp.concatenate([pre_grad[:, square : square + 1] for _, square in halves(f, q)], axis=0)
            lane_wide = lax.broadcasted_iota(jnp.int32, (wide, LANES), 1)
            e = jnp.where(lane_wide == PLANES, column, e)
            head = e.astype(BF16)
            slope_parts[plain(f, q), :] = jnp.concatenate([head, (e - head.astype(F32)).astype(BF16)], axis=1)
            return carry

        each(slopes)
        turned, across = (((0,), (0,)), ((), ())), (((1,), (1,)), ((), ()))
        large = lax.dot_general(near[...], slope_parts[...], turned, preferred_element_type=F32)
        small_part = lax.dot_general(rest[...], slope_parts[:, :LANES], turned, preferred_element_type=F32)
        hc_grad[...] += large[:, :LANES] + (large[:, LANES:] + small_part)
        for f in range(FOLD):
            at = pl.ds(f * span, span)
            large = lax.dot_general(slope_parts[at, :], head_pair[1], across, preferred_element_type=F32)
            small_part = lax.dot_general(
                slope_parts[at, :LANES], head_pair[0, :, LANES:], across, preferred_element_type=F32
            )
            B[g, at, :] = large + small_part

    def outer_grad(section, g):
        norm = norm_of(section, 1, g)

        def body(f, q, carry):
            shift_sum, gain_sum = carry
            v, z = outer_pre(section, g, f, q, norm)
            grad = B[g, plain(f, q), :]
            if section == 0:
                grad = grad.astype(BF16).astype(F32)
            grad = grad * silu_slope(v)
            B[g, plain(f, q), :] = grad
            return shift_sum + fold8(grad), gain_sum + fold8(grad * z)

        zero = jnp.zeros((8, channels), F32)
        shift_sum, gain_sum = each(body, (zero, zero))
        push(4 + 2 * section + 1, g, total(shift_sum), total(gain_sum))

    def norm_back(section, c, g):
        sums = jnp.sum(arrived(4 + 2 * section + c, g), axis=0)
        norm_grad[pl.ds(4 * section + c, 1), :] += sums[1:2]
        norm_grad[pl.ds(4 * section + 2 + c, 1), :] += sums[0:1]
        mean, inv, gain, _ = norm_of(section, c, g)
        p_mean, pz_mean = sums[0:1] / all_rows, sums[1:2] / all_rows
        factor = inv * gain

        def body(f, q, carry):
            z = (C[section, c, g, plain(f, q), :] - mean) * inv
            p = B[g, plain(f, q), :] if c else C[section, 1, g, plain(f, q), :]
            put(Z, (g,), f, q, factor * (p - p_mean - z * pz_mean))
            return carry

        each(body)

    def back_slab(g, f, q, width, t):
        return Z[g, pl.ds(((f + 2 - t // 3) * PITCH + q + 2 - t % 3) * block, width * block), :]

    def back_dot(slabs, section, c, some):
        acc = None
        for part, t in zip(slabs, some):
            part = lax.dot_general(
                part, W[section, pl.ds(c * taps + t * channels, channels), :], (((1,), (1,)), ((), ())),
                preferred_element_type=F32,
            )
            acc = part if acc is None else acc + part
        return acc

    def back_middle(section, c, g, f):
        return back_dot([back_slab(g, f, 1, WIDE - 2, t) for t in range(9)], section, c, range(9))

    def back_outer(section, c, g, q):
        some = [t for t in range(9) if t % 3 != (2 if q == 0 else 0)]
        slabs = [jnp.concatenate([back_slab(g, f, q, 1, t) for f in range(FOLD)], axis=0) for t in some]
        return back_dot(slabs, section, c, some)

    def back_field(section, c, g, add):
        for f in range(FOLD):
            add(pl.ds(f * span + block, span - 2 * block), back_middle(section, c, g, f))
        for q in (0, WIDE - 1):
            out = back_outer(section, c, g, q)
            for f in range(FOLD):
                add(pl.ds(f * span + q * block, block), out[f * block : (f + 1) * block])

    def inner_grad(section, g):
        def keep_field(at, part):
            C[section, 1, g, at, :] = part

        back_field(section, 1, g, keep_field)
        mean, inv, gain, shift = norm_of(section, 0, g)

        def body(f, q, carry):
            shift_sum, gain_sum = carry
            z = (C[section, 0, g, plain(f, q), :] - mean) * inv
            grad = C[section, 1, g, plain(f, q), :] * silu_slope(z * gain + shift)
            C[section, 1, g, plain(f, q), :] = grad
            return shift_sum + fold8(grad), gain_sum + fold8(grad * z)

        zero = jnp.zeros((8, channels), F32)
        shift_sum, gain_sum = each(body, (zero, zero))
        push(4 + 2 * section, g, total(shift_sum), total(gain_sum))

    def entry(section, g):
        def add_field(at, part):
            B[g, at, :] += part

        back_field(section, 0, g, add_field)

    def tap_gradient(section, c):
        field = I if c else X
        for t in range(9):
            left, right = (1, 0) if t % 3 == 0 else (0, 1) if t % 3 == 2 else (0, 0)
            width = WIDE - left - right
            dz = [
                Z[g, pl.ds(((f + 1) * PITCH + 1 + left) * block, width * block), :]
                for g in range(groups)
                for f in range(FOLD)
            ]
            dz = jnp.concatenate(dz, axis=0)
            moved = [slab(field, (section, g), f, left, width, t) for g in range(groups) for f in range(FOLD)]
            moved = jnp.concatenate(moved, axis=0)
            grad = lax.dot_general(moved, dz, (((0,), (0,)), ((), ())), preferred_element_type=F32)
            stage[section, pl.ds(c * taps + t * channels, channels), :] = grad.astype(BF16)
        if not own_taps:
            at = pl.ds(c * taps, taps)
            pltpu.make_async_copy(stage.at[section, at], tap_out.at[section, at], reduce_sem.at[0, section, c, 0]).start()
            return
        k = 2 * section + c
        for cut in range(cuts_of(section, c)):
            for place in range(LAYER) if cuts_of(section, c) > 1 else ():
                at = cut_at(half_at(stage, section, c, 1 - core).at[pl.ds(place * shard_rows, shard_rows)], section, c, cut)
                to = cut_at(siblings.at[k, pl.ds(place * shard_rows, shard_rows)], section, c, cut)
                remote(
                    at, to, reduce_sem.at[0, section, c, 0], reduce_sem.at[1, section, c, cut], 1 - core, me
                ).start()
            if cuts_of(section, c) == 1:
                at = half_at(stage, section, c, 1 - core)
                remote(
                    at, siblings.at[k], reduce_sem.at[0, section, c, 0], reduce_sem.at[1, section, c, 0], 1 - core, me
                ).start()

    def reduce_level(section, c, cut=0):
        if not own_taps:
            return
        k = 2 * section + c
        some = shard_rows // cuts_of(section, c)
        came(siblings.at[k, pl.ds(0, LAYER * some)], reduce_sem.at[1, section, c, cut])
        own = half_at(stage, section, c, core)
        for place in range(LAYER):
            at = pl.ds(place * shard_rows + cut * some, some)
            own[at, :] = (own[at, :].astype(F32) + siblings[k, at, :].astype(F32)).astype(BF16)
        for j in range(1, LAYER):
            place = lax.rem(spot + j, LAYER)
            part = own.at[pl.ds(pl.multiple_of(place * shard_rows + cut * some, 16), some)]
            remote(
                part, layers.at[k, spot, pl.ds(cut * some, some)], reduce_sem.at[2, section, c, 0],
                reduce_sem.at[3, section, c, cut], core, level * LAYER + place,
            ).start()
        mine_at = pl.ds(pl.multiple_of(spot * shard_rows + cut * some, 16), some)
        layers[k, spot, pl.ds(cut * some, some), :] = own[mine_at, :]

    def reduce_column(section, c, cut=0):
        if not own_taps:
            return
        k = 2 * section + c
        some = shard_rows // cuts_of(section, c)
        at = pl.ds(cut * some, some)
        came(siblings.at[k, pl.ds(0, (LAYER - 1) * some)], reduce_sem.at[3, section, c, cut])
        columns[k, at, :] = sum(layers[k, j, at, :].astype(F32) for j in range(LAYER)).astype(BF16)
        part, to = columns.at[k, at], arrivals.at[level, at]
        owner = 2 * c + core
        here = (core == section) & (owner == level)

        @pl.when(here)
        def _():
            pltpu.make_async_copy(part, to, reduce_sem.at[5, 0, 0, 0]).start()

        @pl.when(jnp.logical_not(here))
        def _():
            remote(
                part, to, reduce_sem.at[4, section, c, 0], reduce_sem.at[5, 0, 0, 0], section, owner * LAYER + spot
            ).start()

    def reduce_done():
        if not own_taps:
            return
        came(arrivals, reduce_sem.at[5, 0, 0, 0])
        tap_out[...] = sum(arrivals[j].astype(F32) for j in range(levels))

    def conv_window(owner):
        start = jnp.minimum(owner * flat // (PLANES + 1), channels - HC_ROWS)
        return pl.multiple_of(start // 8 * 8, 8)

    def hidden_window(owner):
        start = jnp.maximum(owner * flat - conv_end, 0) // VHIDDEN
        return pl.multiple_of(jnp.minimum(start // 8 * 8, hw_grad.shape[0] - HW_ROWS), 8)

    def head_exchange():
        remote(hc_grad, hc_in, head_sem.at[0], head_sem.at[1], 1 - core, me).start()
        remote(hw_grad, hw_in, head_sem.at[2], head_sem.at[3], 1 - core, me).start()

    def head_spread():
        sent(hc_grad, head_sem.at[0])
        sent(hw_grad, head_sem.at[2])
        came(hc_in, head_sem.at[1])
        came(hw_in, head_sem.at[3])
        hc_grad[...] += hc_in[...]
        hw_grad[...] += hw_in[...]

        def spread(j, carry):
            peer = lax.rem(me + j, n_dp)
            owner = core * n_dp + peer

            @pl.when(owner * flat < conv_end)
            def _():
                window = hc_grad.at[pl.ds(conv_window(owner), HC_ROWS)]
                remote(window, hc_slots.at[me], head_sem.at[4], head_sem.at[5], core, peer).start()

            @pl.when((owner + 1) * flat > conv_end)
            def _():
                window = hw_grad.at[pl.ds(hidden_window(owner), HW_ROWS)]
                remote(window, hw_slots.at[me], head_sem.at[6], head_sem.at[7], core, peer).start()

            return carry

        lax.fori_loop(1, n_dp, spread, 0)
        owner = core * n_dp + me
        hc_slots[me] = hc_grad[pl.ds(conv_window(owner), HC_ROWS), :]
        hw_slots[me] = hw_grad[pl.ds(hidden_window(owner), HW_ROWS), :]

    def head_done():
        owner = core * n_dp + me
        lines = small_out.shape[0] - 2

        def unsent(j, carry):
            peer = core * n_dp + lax.rem(me + j, n_dp)

            @pl.when(peer * flat < conv_end)
            def _():
                sent(hc_slots.at[0], head_sem.at[4])

            @pl.when((peer + 1) * flat > conv_end)
            def _():
                sent(hw_slots.at[0], head_sem.at[6])

            return carry

        lax.fori_loop(1, n_dp, unsent, 0)

        @pl.when(owner * flat < conv_end)
        def _():
            came(hc_slots.at[pl.ds(0, n_dp - 1)], head_sem.at[5])
            hc_in[pl.ds(0, HC_ROWS), :] = jnp.sum(hc_slots[...], axis=0)
            for line in range(lines):
                start = owner * flat + line * LANES
                row = start // (PLANES + 1)
                off = start - row * (PLANES + 1)
                out = jnp.zeros((1, LANES), F32)
                for m in range(3):
                    at = jnp.clip(row + m - conv_window(owner), 0, HC_ROWS - 1)
                    begin = (PLANES + 1) * m - off
                    part = pltpu.roll(hc_in[pl.ds(at, 1), :], lax.rem(begin + LANES, LANES), axis=1)
                    fits = (one_lane >= begin) & (one_lane < begin + PLANES + 1) & (start + one_lane < conv_end)
                    out = jnp.where(fits, part, out)
                small_out[pl.ds(2 + line, 1), :] = out

        @pl.when((owner + 1) * flat > conv_end)
        def _():
            came(hw_slots.at[pl.ds(0, n_dp - 1)], head_sem.at[7])
            window = jnp.sum(hw_slots[...], axis=0)
            for i in range(2):
                hidden_w[i, pl.ds(0, HW_ROWS), :] = window[:, i * LANES : (i + 1) * LANES]
            for line in range(lines):
                start = owner * flat + line * LANES
                from_end = start - conv_end + 64 * LANES
                row = from_end // LANES
                off = from_end - row * LANES
                out = small_out[pl.ds(2 + line, 1), :]
                for m in range(2):
                    at = jnp.clip(row + m - 64 - 2 * hidden_window(owner), 0, 2 * HW_ROWS - 1)
                    begin = LANES * m - off
                    part = hidden_w[lax.rem(at, 2), pl.ds(at // 2, 1), :]
                    part = pltpu.roll(part, lax.rem(begin + LANES, LANES), axis=1)
                    fits = (one_lane >= begin) & (one_lane < begin + LANES) & (start + one_lane >= conv_end)
                    out = jnp.where(fits, part, out)
                small_out[pl.ds(2 + line, 1), :] = out

    def norm_exchange():
        remote(norm_grad, norm_in, head_sem.at[8], head_sem.at[9], 1 - core, me).start()

    def norm_done():
        came(norm_in, head_sem.at[9])
        sent(norm_grad, head_sem.at[8])
        at = me * share
        tile, off = at // LANES, lax.rem(at, LANES)
        sums = norm_grad[...] + norm_in[...]
        for i in range(2):
            hidden_w[i, pl.ds(0, 8), :] = sums[:, i * LANES : (i + 1) * LANES]
        for i in range(2):
            part = hidden_w[lax.rem(tile, 2), pl.ds(4 * core + 2 * i + tile // 2, 1), :]
            small_out[pl.ds(i, 1), :] = pltpu.roll(part, lax.rem(LANES - off, LANES), axis=1)

    small_out[...] = jnp.zeros_like(small_out)

    def head_step(g):
        merge_moments(3, g)
        heads(g)
        outer_grad(1, g)

    for_groups(head_step)
    head_exchange()
    for section in (1, 0):

        def second_step(g, section=section):
            norm_back(section, 1, g)
            inner_grad(section, g)

        for_groups(second_step)
        if section == 1:
            head_spread()
        else:
            reduce_column(1, 1)
            reduce_level(1, 0)
        tap_gradient(section, 1)

        def first_step(g, section=section):
            norm_back(section, 0, g)
            if section == 1:
                entry(section, g)
                outer_grad(0, g)

        for_groups(first_step)
        if section == 1:
            reduce_level(1, 1)
        else:
            reduce_column(1, 0)
            reduce_level(0, 1)
            norm_exchange()
        tap_gradient(section, 0)

    swap_at = pl.multiple_of(core * groups * rows, 16)

    def last_step(g, after_half, after_field, after_all):
        def add_field(at, part):
            B[g, at, :] += part

        for f in range(FOLD):
            add_field(pl.ds(f * span + block, span - 2 * block), back_middle(0, 0, g, f))
            if f == 1:
                after_half()
        for q in (0, WIDE - 1):
            out = back_outer(0, 0, g, q)
            for f in range(FOLD):
                add_field(pl.ds(f * span + q * block, block), out[f * block : (f + 1) * block])
        after_field()

        def restore(f, q, carry):
            v = B[g, plain(f, q), :]
            for at, square in halves(f, q):
                for i in range(channels // LANES):
                    turn[i, pl.ds(square, per, stride=64), :] = part_of(v, at)[:, i * LANES : (i + 1) * LANES]
            return carry

        each(restore)
        to = pl.ds(g * rows, rows)
        mine[to, :] = turn[core].astype(BF16)
        theirs[to, :] = turn[1 - core].astype(BF16)
        at = pl.ds(pl.multiple_of(swap_at + g * rows, 16), rows)
        remote(
            theirs.at[to], entry_grad.at[at], swap_sem.at[0, g], swap_sem.at[1, g], 1 - core, me
        ).start()
        pltpu.make_async_copy(mine.at[to], entry_grad.at[at], swap_sem.at[2, g]).start()
        after_all()

    def nothing():
        pass

    steps = [functools.partial(reduce_level, 0, 0, cut) for cut in range(CUTS)]
    steps += [functools.partial(reduce_column, 0, 0, cut) for cut in range(CUTS)]
    reduce_column(0, 1)
    if not own_taps:
        steps = [nothing] * len(steps)
    for g in range(groups):
        last_step(g, *(steps[3 * g : 3 * g + 3] + [nothing] * 3)[:3])
    for step in steps[3 * groups :]:
        step()
    head_done()
    norm_done()

    sent(packs.at[core, pl.ds(0, n_dp - 1)], pack_sem.at[0])
    sent(packs.at[core], pack_sem.at[2])
    for section in range(2):
        for c in range(2):
            k = 2 * section + c
            if not own_taps:
                at = pl.ds(c * taps, taps)
                pltpu.make_async_copy(
                    stage.at[section, at], tap_out.at[section, at], reduce_sem.at[0, section, c, 0]
                ).wait()
                continue
            three = stage.at[section, pl.ds(0, (LAYER - 1) * shard_rows)]

            @pl.when((core == section) & (level // 2 == c))
            def _(section=section, c=c):
                sent(stage.at[section, pl.ds(0, (levels - 1) * shard_rows)], fetch_sem.at[0, section, c, 0])

                @pl.when(lax.rem(level, 2) != core)
                def _():
                    sent(stage.at[section, pl.ds(0, shard_rows)], fetch_sem.at[0, section, c, 0])

            sent(three, fetch_sem.at[2, section, c, 0])
            sent(half_at(stage, section, c, core), fetch_sem.at[4, section, c, 0])
            sent(siblings.at[k], reduce_sem.at[0, section, c, 0])
            sent(three, reduce_sem.at[2, section, c, 0])

            @pl.when(jnp.logical_not((core == section) & (2 * c + core == level)))
            def _(section=section, c=c, k=k):
                sent(columns.at[k], reduce_sem.at[4, section, c, 0])

    reduce_done()
    for g in range(groups):
        to = pl.ds(g * rows, rows)
        at = pl.ds(pl.multiple_of(swap_at + g * rows, 16), rows)
        remote(theirs.at[to], entry_grad.at[at], swap_sem.at[0, g], swap_sem.at[1, g], 1 - core, me).wait()
        pltpu.make_async_copy(mine.at[to], entry_grad.at[at], swap_sem.at[2, g]).wait()


def local(
    board_input, conv_weight, norm_gains, norm_shifts, head_params, policy_target, legal_mask, value_target
):
    n_dp, n_pipe = lax.axis_size("dp"), lax.axis_size("pipe")
    positions, channels = board_input.shape[0], board_input.shape[-1]
    per = positions // MICRO
    groups = MICRO // n_pipe
    moves = legal_mask.shape[1]
    rows = per * 64
    padded = (FOLD + 2) * PITCH * 2 * per
    taps = 9 * channels

    shard_rows = conv_weight.shape[1]
    own_taps = shard_rows % 16 == 0 and n_dp == 4 * LAYER
    share, flat = norm_gains.shape[1], head_params.shape[0]
    lines = -(-flat // LANES)
    pack_rows = -(-(2 + lines) // 8) * 8
    head_rows = jnp.pad(head_params, (0, (pack_rows - 2) * LANES - flat)).reshape(pack_rows - 2, LANES)
    norms = jnp.pad(jnp.concatenate([norm_gains, norm_shifts]).astype(F32), ((0, 0), (0, LANES - share)))
    small = jnp.concatenate([norms, head_rows])
    taps_in = conv_weight
    if not own_taps:
        taps_in = lax.all_gather(lax.all_gather(conv_weight, "dp", axis=1, tiled=True), "pipe", axis=0, tiled=True)

    vmem = pl.BlockSpec(memory_space=pltpu.VMEM)
    smem = pl.BlockSpec(memory_space=pltpu.SMEM)
    anywhere = pl.BlockSpec(memory_space=pl.ANY)
    dma, regular = pltpu.SemaphoreType.DMA, pltpu.VMEM
    tap_shape = (shard_rows, channels) if own_taps else (2, 2 * taps, channels)
    lane_rows = shard_rows if own_taps else 16
    tap_grad, small_grad, entry_grad = pl.pallas_call(
        functools.partial(
            kernel, (n_dp, per, groups, moves, 1.0 / positions, shard_rows, own_taps, flat)
        ),
        out_shape=(
            jax.ShapeDtypeStruct(tap_shape, F32 if own_taps else BF16),
            jax.ShapeDtypeStruct((pack_rows, LANES), F32),
            jax.ShapeDtypeStruct((positions * 64, LANES), BF16),
        ),
        in_specs=[smem, smem, anywhere, anywhere, vmem, anywhere],
        out_specs=(vmem if own_taps else anywhere, vmem, anywhere),
        scratch_shapes=[
            regular((2, 2 * taps, channels), BF16),
            regular((2, groups, padded, channels), BF16),
            regular((2, groups, padded, channels), BF16),
            regular((groups, padded, channels), BF16),
            regular((2, 2, groups, rows, channels), F32),
            regular((groups, rows, channels), F32),
            regular((groups * per, 8, 8, channels), BF16),
            regular((groups * per, moves), jnp.int32),
            regular((groups, rows, LANES), F32),
            regular((rows, LANES), F32),
            regular((channels // LANES, rows, LANES), F32),
            regular((groups * per, LANES), jnp.int32),
            regular((groups * per, LANES), F32),
            regular((2, 2 * taps, channels), BF16),
            regular((4, groups, 8, channels), F32),
            regular((8, groups, n_dp, 2, channels), F32),
            regular((groups * rows, LANES), BF16),
            regular((groups * rows, LANES), BF16),
            regular((2, n_dp, pack_rows, LANES), F32),
            regular((2, 8, channels), F32),
            regular((channels, LANES), F32),
            regular((2, channels, 2 * LANES), BF16),
            regular((2, LANES + 8, LANES), F32),
            regular((8, channels), F32),
            regular((channels, LANES), F32),
            regular((72, VHIDDEN), F32),
            regular((8, channels), F32),
            regular((channels, LANES), F32),
            regular((72, VHIDDEN), F32),
            regular((n_dp, HC_ROWS, LANES), F32),
            regular((n_dp, HW_ROWS, VHIDDEN), F32),
            regular((4, LAYER * lane_rows, channels), BF16),
            regular((4, LAYER, lane_rows, channels), BF16),
            regular((4, lane_rows, channels), BF16),
            regular((4, lane_rows, channels), BF16),
            dma((3,)),
            dma((8, groups)),
            dma((8, groups)),
            dma((3, groups)),
            dma((4,)),
            dma((10,)),
            dma((6, 2, 2, CUTS)),
            dma((6, 2, 2, CUTS)),
        ],
        compiler_params=pltpu.CompilerParams(
            collective_id=0, has_side_effects=True, vmem_limit_bytes=63 * 2**20
        ),
    )(policy_target, value_target, board_input, taps_in, small, legal_mask)

    conv_grad = tap_grad
    if not own_taps:
        conv_grad = lax.psum_scatter(
            tap_grad.astype(F32).reshape(4 * taps, channels), ("pipe", "dp"), scatter_dimension=0, tiled=True
        )
    head_grad = small_grad[2:].reshape(-1)[:flat]
    entry_grad = entry_grad.astype(F32).reshape(positions, 8, 8, LANES)
    return conv_grad[None], small_grad[0:1, :share], small_grad[1:2, :share], head_grad, entry_grad


def solution(mesh):
    placed = (
        P("dp", None, None, None),
        P("pipe", "dp", None),
        P("pipe", "dp"),
        P("pipe", "dp"),
        P(("pipe", "dp")),
        P("dp"),
        P("dp", None),
        P("dp"),
    )
    return jax.shard_map(
        local,
        mesh=mesh,
        in_specs=placed,
        out_specs=(
            P("pipe", "dp", None),
            P("pipe", "dp"),
            P("pipe", "dp"),
            P(("pipe", "dp")),
            P("dp", None, None, "pipe"),
        ),
        check_vma=False,
    )
```

```python
import functools

import jax
import jax.numpy as jnp
from jax import lax
from jax.experimental import pallas as pl
from jax.experimental.pallas import tpu as pltpu
from jax.sharding import PartitionSpec as P

PLANES = 73
VHIDDEN = 256
MICRO = 4
EPSILON = 1e-05
F32, BF16 = jnp.float32, jnp.bfloat16
PRECISE = lax.Precision.HIGHEST
MESH = pl.DeviceIdType.MESH
LANES = 128
ILLEGAL = -1e30
HC_ROWS, HW_ROWS = 24, 16
LAYER = 4
CUTS = 3
FETCH_CUTS = 6
COLS = 8

FOLD, WIDE, PITCH = 4, 8, 10


def sigmoid(v):
    return 0.5 * jnp.tanh(0.5 * v) + 0.5


def silu_slope(v):
    s = sigmoid(v)
    return s * (1.0 + v * (1.0 - s))


def fold8(v):
    return jnp.sum(v.reshape(v.shape[0] // 8, 8, v.shape[1]), axis=0)


def total(v):
    return jnp.sum(v, axis=0, keepdims=True)


def kernel(
    sizes, policy, value_goal, board, shard, gain_part, shift_part, head_part, legal,
    tap_out, small_out, entry_grad,
    W, X, I, Z, C, B, raw, mask_raw, code, planes, turn, goal, vgoal, stage, stat, slots, mine, theirs,
    packs, gains, head_conv, head_pair, hidden_w, norm_grad, hc_grad, hw_grad, norm_in, hc_in, hw_in, hc_slots, hw_slots,
    siblings, layers, columns, arrivals,
    load_sem, send_sem, recv_sem, swap_sem, pack_sem, head_sem, fetch_sem, reduce_sem,
):
    n_dp, per, groups, moves, scale, shard_rows, own_taps, flat = sizes
    core, me = lax.axis_index("pipe"), lax.axis_index("dp")
    block = 2 * per
    span = WIDE * block
    rows = FOLD * span
    channels = X.shape[-1]
    taps = 9 * channels
    all_rows = n_dp * rows
    spot, level = lax.rem(me, LAYER), me // LAYER
    levels = n_dp // LAYER

    def remote(src, dst, send, recv, pipe, dp):
        return pltpu.make_async_remote_copy(
            src_ref=src, dst_ref=dst, send_sem=send, recv_sem=recv, device_id=(pipe, dp), device_id_type=MESH
        )

    def sent(ref, sem):
        remote(ref, ref, sem, sem, 1 - core, me).wait_send()

    def came(ref, sem):
        remote(ref, ref, sem, sem, 1 - core, me).wait_recv()

    barrier = pltpu.get_barrier_semaphore()

    def greet(j, carry):
        pl.semaphore_signal(barrier, inc=1, device_id=(core, lax.rem(me + j, n_dp)), device_id_type=MESH)
        return carry

    def greet_column(j, carry):
        other = lax.rem(me + j * LAYER, n_dp)
        pl.semaphore_signal(barrier, inc=1, device_id=(1 - core, other), device_id_type=MESH)
        return carry

    lax.fori_loop(1, n_dp, greet, 0)
    lax.fori_loop(0, levels, greet_column, 0)

    first = pl.multiple_of(core * groups * per, 8)
    loads = [
        pltpu.make_async_copy(board.at[pl.ds(first, groups * per)], raw, load_sem.at[0]),
        pltpu.make_async_copy(legal.at[pl.ds(first, groups * per)], mask_raw, load_sem.at[1]),
    ]
    if not own_taps:
        loads.append(pltpu.make_async_copy(shard, W, load_sem.at[2]))
    for load in loads:
        load.start()
    pl.semaphore_wait(barrier, n_dp - 1 + levels)

    def shard_at(section, c, half, place):
        start = c * taps + (half * LAYER + place) * shard_rows
        return W.at[section, pl.ds(pl.multiple_of(start, 16), shard_rows)]

    def half_at(ref, section, c, half):
        start = c * taps + half * LAYER * shard_rows
        return ref.at[section, pl.ds(pl.multiple_of(start, 16), LAYER * shard_rows)]

    def cuts_of(section, c):
        return CUTS if section + c == 0 else 1

    def fetch_cuts_of(section, c):
        return FETCH_CUTS if section + c == 0 else 1

    def cut_at(ref, cuts, cut):
        some = shard_rows // cuts
        return ref.at[pl.ds(cut * some, some)]

    def fetch_column(section, c):
        if not own_taps:
            return

        @pl.when((core == section) & (level // 2 == c))
        def _():
            half = lax.rem(level, 2)
            cuts = fetch_cuts_of(section, c)
            for cut in range(cuts):
                at = cut_at(shard_at(section, c, half, spot), cuts, cut)
                src = cut_at(shard.at[0], cuts, cut)
                send, recv = fetch_sem.at[0, section, c, 0], fetch_sem.at[1, section, c, cut]
                for j in range(1, levels):
                    remote(src, at, send, recv, half, lax.rem(me + j * LAYER, n_dp)).start()

                @pl.when(half == core)
                def _(src=src, at=at, recv=recv):
                    pltpu.make_async_copy(src, at, recv).start()

                @pl.when(half != core)
                def _(src=src, at=at, send=send, recv=recv):
                    remote(src, at, send, recv, half, me).start()

    def fetch_level(section, c, cut=0):
        if not own_taps:
            return
        at = cut_at(shard_at(section, c, core, spot), fetch_cuts_of(section, c), cut)
        came(at, fetch_sem.at[1, section, c, cut])
        for j in range(1, LAYER):
            peer = level * LAYER + lax.rem(spot + j, LAYER)
            remote(at, at, fetch_sem.at[2, section, c, 0], fetch_sem.at[3, section, c, cut], core, peer).start()

    def fetch_core(section, c):
        if not own_taps:
            return
        cuts = fetch_cuts_of(section, c)
        send, recv = fetch_sem.at[4, section, c, 0], fetch_sem.at[5, section, c, 0]
        for cut in range(cuts):
            some = W.at[section, pl.ds(c * taps, (LAYER - 1) * shard_rows // cuts)]
            came(some, fetch_sem.at[3, section, c, cut])
            for place in range(LAYER) if cuts > 1 else ():
                at = cut_at(shard_at(section, c, core, place), cuts, cut)
                remote(at, at, send, recv, 1 - core, me).start()
        if cuts == 1:
            at = half_at(W, section, c, core)
            remote(at, at, send, recv, 1 - core, me).start()

    def fetch_done(section, c):
        if not own_taps:
            return
        came(half_at(W, section, c, 1 - core), fetch_sem.at[5, section, c, 0])

    def send_pack(j, carry):
        remote(
            packs.at[core, me], packs.at[core, me], pack_sem.at[0], pack_sem.at[1], core, lax.rem(me + j, n_dp)
        ).start()
        return carry

    fetch_column(0, 0)
    fetch_column(0, 1)

    wide = COLS * block

    def padded(f, q):
        return pl.ds(((f + 1) * PITCH + 1 + q) * block, wide)

    def put(ref, at, f, q, y):
        ref[*at, padded(f, q), :] = y.astype(BF16)
        none = jnp.zeros((COLS, per, channels), F32)
        parts = y.reshape(COLS, block, channels)
        if f == FOLD - 1:
            halo = jnp.concatenate([none, parts[:, :per]], axis=1).reshape(wide, channels)
            ref[*at, padded(-1, q), :] = halo.astype(BF16)
        if f == 0:
            halo = jnp.concatenate([parts[:, per:], none], axis=1).reshape(wide, channels)
            ref[*at, padded(FOLD, q), :] = halo.astype(BF16)

    def plain(f, q):
        return pl.ds((f * WIDE + q) * block, wide)

    def each(body, carry=0):
        for q in range(0, WIDE, COLS):
            for f in range(FOLD):
                carry = body(f, q, carry)
        return carry

    def halves(f, q):
        for i in range(COLS):
            for half in range(2):
                yield pl.ds((2 * i + half) * per, per), (f + FOLD * half) * 8 + q + i

    def part_of(v, at):
        return v[at.start : at.start + per]

    loads[0].wait()
    for g in range(groups):

        def widen(b, carry, g=g):
            rows_of = raw[g * per + b].astype(F32).reshape(64, channels)
            for i in range(channels // LANES):
                turn[i, pl.ds(pl.multiple_of(b * 64, 64), 64), :] = rows_of[:, i * LANES : (i + 1) * LANES]
            return carry

        lax.fori_loop(0, per, widen, 0)

        def reorder(f, q, carry, g=g):
            parts = [
                jnp.concatenate([turn[i, pl.ds(square, per, stride=64), :] for _, square in halves(f, q)], axis=0)
                for i in range(channels // LANES)
            ]
            put(X, (0, g), f, q, jnp.concatenate(parts, axis=1))
            return carry

        each(reorder)
        if g < FETCH_CUTS - 1:
            fetch_level(0, 0, g)

    for cut in range(min(groups, FETCH_CUTS - 1), FETCH_CUTS):
        fetch_level(0, 0, cut)
    packs[core, me] = jnp.zeros(packs.shape[2:], F32)
    for i, part in enumerate((gain_part, shift_part)):
        packs[core, me, pl.ds(i, 1), pl.ds(0, part.shape[1])] = part[...].astype(F32)
    for line in range(0, flat, LANES):
        count = min(LANES, flat - line)
        packs[core, me, pl.ds(2 + line // LANES, 1), pl.ds(0, count)] = head_part[pl.ds(line, count)].reshape(1, count)
    lax.fori_loop(1, n_dp, send_pack, 0)
    fetch_level(0, 1)
    fetch_column(1, 0)

    both = groups * per
    row_of = lax.broadcasted_iota(jnp.int32, (both, LANES), 0)
    lane_of = lax.broadcasted_iota(jnp.int32, (both, LANES), 1)

    def column_of(ref, zero):
        def pick(b, acc):
            return jnp.where(row_of == b, ref[first + b], acc)

        return lax.fori_loop(0, both, pick, zero)

    goal[...] = column_of(policy, jnp.zeros((both, LANES), jnp.int32))
    vgoal[...] = column_of(value_goal, jnp.zeros((both, LANES), F32))
    loads[1].wait()
    for square in range(64):
        base = square * PLANES // LANES * LANES
        shift = square * PLANES - base
        width = min(2 * LANES, moves - base)
        window = mask_raw[:, base : base + width]
        if width < 2 * LANES:
            window = jnp.concatenate([window, jnp.zeros((both, 2 * LANES - width), jnp.int32)], axis=1)
        if shift:
            window = pltpu.roll(window, 2 * LANES - shift, axis=1)
        window = window[:, :LANES]
        hit = goal[...] == lane_of + square * PLANES
        kind = jnp.where(hit, 2.0, jnp.where(window > 0, 1.0, 0.0))
        kind = jnp.where(lane_of < PLANES, kind, 0.0)
        f, q, half = square // 8 % FOLD, square % 8, square // 8 // FOLD
        at = ((f * WIDE + q) * 2 + half) * per
        for g in range(groups):
            code[g, pl.ds(at, per), :] = kind[g * per : (g + 1) * per]

    hc_grad[...] = jnp.zeros_like(hc_grad)
    hw_grad[...] = jnp.zeros_like(hw_grad)
    norm_grad[...] = jnp.zeros_like(norm_grad)
    fetch_core(0, 0)
    came(packs.at[core, pl.ds(0, n_dp - 1)], pack_sem.at[1])
    remote(packs.at[core], packs.at[core], pack_sem.at[2], pack_sem.at[3], 1 - core, me).start()

    share = 2 * channels // n_dp

    def unpack_gains():
        tile_share = LANES // share
        for section in range(2):
            for tile in range(2 * channels // LANES):
                acc = jnp.zeros((2, LANES), F32)
                for u in range(tile_share):
                    part = packs[section, tile * tile_share + u, pl.ds(0, 2), :]
                    acc = acc + (pltpu.roll(part, u * share, axis=1) if u else part)
                c, at = tile * LANES // channels, tile * LANES % channels
                gains[section, pl.ds(c, 1), pl.ds(at, LANES)] = acc[0:1]
                gains[section, pl.ds(2 + c, 1), pl.ds(at, LANES)] = acc[1:2]

    one_lane = lax.broadcasted_iota(jnp.int32, (1, LANES), 1)
    conv_end = (PLANES + 1) * channels

    def flat_row(start, count):
        owner, off = divmod(start, flat)
        line, lane_at = divmod(off, LANES)

        def line_of(owner, line, back):
            row = packs[owner // n_dp, owner % n_dp, pl.ds(line + 2, 1), :]
            return pltpu.roll(row, back % LANES, axis=1) if back % LANES else row

        row = line_of(owner, line, -lane_at)
        if lane_at + count > LANES and off + LANES - lane_at < flat:
            row = jnp.where(one_lane < LANES - lane_at, row, line_of(owner, line + 1, -lane_at))
        if off + count > flat:
            row = jnp.where(one_lane < flat - off, row, line_of(owner + 1, 0, flat - off))
        return jnp.where(one_lane < count, row, 0.0) if count < LANES else row

    def unpack_heads():
        for i in range(channels):
            head_conv[pl.ds(i, 1), :] = flat_row(i * (PLANES + 1), PLANES + 1)
        near = head_conv[...].astype(BF16)
        rest = (head_conv[...] - near.astype(F32)).astype(BF16)
        head_pair[0] = jnp.concatenate([near, rest], axis=1)
        head_pair[1] = jnp.concatenate([near, near], axis=1)
        hidden_w[...] = jnp.zeros_like(hidden_w)
        for i in range(2 * 66):
            line = i // 2 if i < 128 else i // 2 + 64
            hidden_w[i % 2, pl.ds(line, 1), :] = flat_row(conv_end + i * LANES, LANES)

    fetch_done(0, 0)
    if not own_taps:
        loads[2].wait()

    def push(k, g, top, bottom):
        slots[k, g, me, pl.ds(0, 1), :] = top
        slots[k, g, me, pl.ds(1, 1), :] = bottom

        def send(j, carry):
            pltpu.make_async_remote_copy(
                src_ref=slots.at[k, g, me],
                dst_ref=slots.at[k, g, me],
                send_sem=send_sem.at[k, g],
                recv_sem=recv_sem.at[k, g],
                device_id=(core, lax.rem(me + j, n_dp)),
                device_id_type=MESH,
            ).start()
            return carry

        lax.fori_loop(1, n_dp, send, 0)

    def arrived(k, g):
        others = slots.at[k, g, pl.ds(0, n_dp - 1)]
        copy = pltpu.make_async_remote_copy(
            src_ref=others, dst_ref=others, send_sem=send_sem.at[k, g], recv_sem=recv_sem.at[k, g],
            device_id=(core, lax.rem(me + 1, n_dp)), device_id_type=MESH,
        )
        copy.wait_send()
        copy.wait_recv()
        return slots[k, g]

    def merge_moments(k, g):
        parts = arrived(k, g)
        both_sums = jnp.sum(parts, axis=0)
        mean = both_sums[0:1] / n_dp
        apart = parts - mean
        between = jnp.sum(apart * apart, axis=0)[0:1]
        spread = (both_sums[1:2] + between * rows) / all_rows
        stat[k, g, pl.ds(0, 1), :] = mean
        stat[k, g, pl.ds(1, 1), :] = lax.rsqrt(spread + EPSILON)

    def norm_of(section, c, g):
        k = 2 * section + c
        gain = gains[section, pl.ds(c, 1), :]
        shift = gains[section, pl.ds(2 + c, 1), :]
        return stat[k, g, pl.ds(0, 1), :], stat[k, g, pl.ds(1, 1), :], gain, shift

    def slab(field, at, f, q, width, t):
        start = ((f + t // 3) * PITCH + q + t % 3) * block
        return field[*at, pl.ds(start, width * block), :]

    def taps_of(section, c, some):
        return [W[section, pl.ds(c * taps + t * channels, channels), :] for t in some]

    def convolve(field, section, c, g):
        k = 2 * section + c
        counted = []

        def note(out, count):
            part = total(fold8(out))
            apart = out - part / count
            counted.append((part, total(fold8(apart * apart)), count))

        middle = W[section, pl.ds(c * taps, taps), :]
        for f in range(FOLD):
            slabs = [slab(field, (section, g), f, 1, WIDE - 2, t) for t in range(9)]
            out = jnp.dot(jnp.concatenate(slabs, axis=1), middle, preferred_element_type=F32)
            C[section, c, g, pl.ds(f * span + block, span - 2 * block), :] = out
            note(out, span - 2 * block)
        for q, skip in ((0, 0), (WIDE - 1, 2)):
            some = [t for t in range(9) if t % 3 != skip]
            slabs = [
                jnp.concatenate([slab(field, (section, g), f, q, 1, t) for t in some], axis=1) for f in range(FOLD)
            ]
            out = jnp.dot(
                jnp.concatenate(slabs, axis=0), jnp.concatenate(taps_of(section, c, some), axis=0),
                preferred_element_type=F32,
            )
            for f in range(FOLD):
                C[section, c, g, pl.ds(f * span + q * block, block), :] = out[f * block : (f + 1) * block]
            note(out, FOLD * block)
        mean = sum(part for part, _, _ in counted) / rows
        spread = sum(apart for _, apart, _ in counted)
        for part, _, count in counted:
            spread = spread + count * jnp.square(part / count - mean)
        push(k, g, mean, spread)

    def inner(section, g):
        mean, inv, gain, shift = norm_of(section, 0, g)
        factor = inv * gain

        def body(f, q, carry):
            v = (C[section, 0, g, plain(f, q), :] - mean) * factor + shift
            put(I, (section, g), f, q, v * sigmoid(v))
            return carry

        each(body)

    def outer_pre(section, g, f, q, norm):
        mean, inv, gain, shift = norm
        z = (C[section, 1, g, plain(f, q), :] - mean) * inv
        return X[section, g, padded(f, q), :].astype(F32) + z * gain + shift, z

    def for_groups(body):
        def step(g, carry):
            body(g)
            return carry

        lax.fori_loop(0, groups, step, 0)

    def entry_step(g):
        convolve(X, 0, 0, g)

        @pl.when(g == 0)
        def _():
            fetch_level(1, 0)
            fetch_column(1, 1)

    for_groups(entry_step)
    came(packs.at[1 - core], pack_sem.at[3])
    unpack_gains()
    unpack_heads()
    fetch_core(0, 1)
    for section in range(2):

        def inner_step(g, section=section):
            merge_moments(2 * section, g)
            inner(section, g)
            if section == 0:

                @pl.when(g == 0)
                def _():
                    fetch_done(0, 1)

            if section == 1:

                @pl.when(g == 0)
                def _():
                    fetch_done(1, 1)

            convolve(I, section, 1, g)
            if section == 0:

                @pl.when(g == 0)
                def _():
                    fetch_level(1, 1)

        for_groups(inner_step)
        if section == 0:
            fetch_core(1, 0)

            def hand_step(g):
                merge_moments(1, g)
                norm = norm_of(0, 1, g)

                def hand_on(f, q, carry):
                    v, _ = outer_pre(0, g, f, q, norm)
                    put(X, (1, g), f, q, v * sigmoid(v))
                    return carry

                each(hand_on)

                @pl.when(g == 0)
                def _():
                    fetch_done(1, 0)

                convolve(X, 1, 0, g)

            for_groups(hand_step)
            fetch_core(1, 1)

    lane = lax.broadcasted_iota(jnp.int32, (per, LANES), 1)

    def head_fields(g):
        return [stage.at[g, pl.ds(i * rows, rows)] for i in range(3)]

    def heads(g):
        norm = norm_of(1, 1, g)

        near, rest, slope_parts = head_fields(g)

        def last(f, q, carry):
            v, _ = outer_pre(1, g, f, q, norm)
            final = v * sigmoid(v)
            head = final.astype(BF16)
            near[plain(f, q), :] = head
            rest[plain(f, q), :] = (final - head.astype(F32)).astype(BF16)
            return carry

        each(last)
        for f in range(FOLD):
            at = pl.ds(f * span, span)
            large = jnp.dot(near[at, :], head_pair[0], preferred_element_type=F32)
            small_part = jnp.dot(rest[at, :], head_pair[0, :, :LANES], preferred_element_type=F32)
            planes[at, :] = large[:, :LANES] + (large[:, LANES:] + small_part)

        def look(f, q, carry):
            top, squares = carry
            a = planes[plain(f, q), :]
            a_legal = jnp.where(code[g, plain(f, q), :] > 0, a, ILLEGAL)
            column = a[:, PLANES : PLANES + 1]
            for at, square in halves(f, q):
                top = jnp.maximum(top, part_of(a_legal, at))
                squares = jnp.where(lane == square, part_of(column, at), squares)
            return top, squares

        top, pre = each(look, (jnp.full((per, LANES), ILLEGAL, F32), jnp.zeros((per, LANES), F32)))
        top = jnp.max(top, axis=1, keepdims=True)
        top = jnp.concatenate([top] * (2 * COLS), axis=0)

        def weigh(f, q, acc):
            a = planes[plain(f, q), :]
            e = jnp.where(code[g, plain(f, q), :] > 0, jnp.exp(a - top), 0.0)
            planes[plain(f, q), :] = e
            return acc + jnp.sum(e.reshape(2 * COLS, per, LANES), axis=0)

        norm_sum = jnp.sum(each(weigh, jnp.zeros((per, LANES), F32)), axis=1, keepdims=True)
        portion = scale / norm_sum
        portion = jnp.concatenate([portion] * (2 * COLS), axis=0)

        squares = pre * sigmoid(pre)
        hidden_all = jnp.concatenate([hidden_w[0], hidden_w[1]], axis=1)
        hidden_in, bias, out_w = hidden_all[:LANES], hidden_all[LANES : LANES + 1], hidden_all[LANES + 1 : LANES + 2]
        hidden_pre = jnp.dot(squares, hidden_in, precision=PRECISE, preferred_element_type=F32) + bias
        hidden = hidden_pre * sigmoid(hidden_pre)
        value = jnp.tanh(jnp.sum(hidden * out_w, axis=1, keepdims=True))
        wanted = vgoal[pl.ds(g * per, per), 0:1]
        slope = 2.0 * scale * (value - wanted) * (1.0 - value * value)
        hidden_grad = slope * out_w * silu_slope(hidden_pre)
        hw_grad[pl.ds(0, 64), :] += lax.dot_general(
            squares, hidden_grad, (((0,), (0,)), ((), ())), precision=PRECISE, preferred_element_type=F32
        )[:64]
        hw_grad[pl.ds(64, 1), :] += total(hidden_grad)
        hw_grad[pl.ds(65, 1), :] += total(hidden * slope)
        squares_grad = lax.dot_general(
            hidden_grad, hidden_in, (((1,), (1,)), ((), ())), precision=PRECISE,
            preferred_element_type=F32,
        )
        pre_grad = squares_grad * silu_slope(pre)

        def slopes(f, q, carry):
            e = planes[plain(f, q), :] * portion
            e = e - jnp.where(code[g, plain(f, q), :] > 1.5, scale, 0.0)
            column = jnp.concatenate([pre_grad[:, square : square + 1] for _, square in halves(f, q)], axis=0)
            lane_wide = lax.broadcasted_iota(jnp.int32, (wide, LANES), 1)
            e = jnp.where(lane_wide == PLANES, column, e)
            head = e.astype(BF16)
            slope_parts[plain(f, q), :] = jnp.concatenate([head, (e - head.astype(F32)).astype(BF16)], axis=1)
            return carry

        each(slopes)
        across = (((1,), (1,)), ((), ()))
        for f in range(FOLD):
            at = pl.ds(f * span, span)
            large = lax.dot_general(slope_parts[at, :], head_pair[1], across, preferred_element_type=F32)
            small_part = lax.dot_general(
                slope_parts[at, :LANES], head_pair[0, :, LANES:], across, preferred_element_type=F32
            )
            B[g, at, :] = large + small_part

    def head_taps(g):
        near, rest, slope_parts = head_fields(g)
        turned = (((0,), (0,)), ((), ()))
        large = lax.dot_general(near[...], slope_parts[...], turned, preferred_element_type=F32)
        small_part = lax.dot_general(rest[...], slope_parts[:, :LANES], turned, preferred_element_type=F32)
        hc_grad[...] += large[:, :LANES] + (large[:, LANES:] + small_part)

    def outer_grad(section, g):
        norm = norm_of(section, 1, g)

        def body(f, q, carry):
            shift_sum, gain_sum = carry
            v, z = outer_pre(section, g, f, q, norm)
            grad = B[g, plain(f, q), :]
            if section == 0:
                grad = grad.astype(BF16).astype(F32)
            grad = grad * silu_slope(v)
            B[g, plain(f, q), :] = grad
            return shift_sum + fold8(grad), gain_sum + fold8(grad * z)

        zero = jnp.zeros((8, channels), F32)
        shift_sum, gain_sum = each(body, (zero, zero))
        push(4 + 2 * section + 1, g, total(shift_sum), total(gain_sum))

    def norm_back(section, c, g):
        sums = jnp.sum(arrived(4 + 2 * section + c, g), axis=0)
        norm_grad[pl.ds(4 * section + c, 1), :] += sums[1:2]
        norm_grad[pl.ds(4 * section + 2 + c, 1), :] += sums[0:1]
        mean, inv, gain, _ = norm_of(section, c, g)
        p_mean, pz_mean = sums[0:1] / all_rows, sums[1:2] / all_rows
        factor = inv * gain

        def body(f, q, carry):
            z = (C[section, c, g, plain(f, q), :] - mean) * inv
            p = B[g, plain(f, q), :] if c else C[section, 1, g, plain(f, q), :]
            put(Z, (g,), f, q, factor * (p - p_mean - z * pz_mean))
            return carry

        each(body)

    def back_slab(g, f, q, width, t):
        return Z[g, pl.ds(((f + 2 - t // 3) * PITCH + q + 2 - t % 3) * block, width * block), :]

    def back_dot(slabs, section, c, some):
        acc = None
        for part, t in zip(slabs, some):
            part = lax.dot_general(
                part, W[section, pl.ds(c * taps + t * channels, channels), :], (((1,), (1,)), ((), ())),
                preferred_element_type=F32,
            )
            acc = part if acc is None else acc + part
        return acc

    def back_middle(section, c, g, f):
        return back_dot([back_slab(g, f, 1, WIDE - 2, t) for t in range(9)], section, c, range(9))

    def back_outer(section, c, g, q):
        some = [t for t in range(9) if t % 3 != (2 if q == 0 else 0)]
        slabs = [jnp.concatenate([back_slab(g, f, q, 1, t) for f in range(FOLD)], axis=0) for t in some]
        return back_dot(slabs, section, c, some)

    def back_field(section, c, g, add):
        for f in range(FOLD):
            add(pl.ds(f * span + block, span - 2 * block), back_middle(section, c, g, f))
        for q in (0, WIDE - 1):
            out = back_outer(section, c, g, q)
            for f in range(FOLD):
                add(pl.ds(f * span + q * block, block), out[f * block : (f + 1) * block])

    def inner_grad(section, g):
        def keep_field(at, part):
            C[section, 1, g, at, :] = part

        back_field(section, 1, g, keep_field)
        mean, inv, gain, shift = norm_of(section, 0, g)

        def body(f, q, carry):
            shift_sum, gain_sum = carry
            z = (C[section, 0, g, plain(f, q), :] - mean) * inv
            grad = C[section, 1, g, plain(f, q), :] * silu_slope(z * gain + shift)
            C[section, 1, g, plain(f, q), :] = grad
            return shift_sum + fold8(grad), gain_sum + fold8(grad * z)

        zero = jnp.zeros((8, channels), F32)
        shift_sum, gain_sum = each(body, (zero, zero))
        push(4 + 2 * section, g, total(shift_sum), total(gain_sum))

    def entry(section, g):
        def add_field(at, part):
            B[g, at, :] += part

        back_field(section, 0, g, add_field)

    def reduce_core(section, c):
        k = 2 * section + c
        for cut in range(cuts_of(section, c)):
            for place in range(LAYER) if cuts_of(section, c) > 1 else ():
                at = half_at(stage, section, c, 1 - core).at[pl.ds(place * shard_rows, shard_rows)]
                at = cut_at(at, cuts_of(section, c), cut)
                to = siblings.at[k, pl.ds(place * shard_rows, shard_rows)]
                to = cut_at(to, cuts_of(section, c), cut)
                remote(
                    at, to, reduce_sem.at[0, section, c, 0], reduce_sem.at[1, section, c, cut], 1 - core, me
                ).start()
            if cuts_of(section, c) == 1:
                at = half_at(stage, section, c, 1 - core)
                remote(
                    at, siblings.at[k], reduce_sem.at[0, section, c, 0], reduce_sem.at[1, section, c, 0], 1 - core, me
                ).start()

    def tap_gradient(section, c, meanwhile=()):
        field = I if c else X
        for i in range(9):
            t = i + (1 - core) * (8 - 2 * i)
            left = (core, 0, 1 - core)[i % 3]
            width = WIDE if i % 3 == 1 else WIDE - 1

            def start(row, column):
                return pl.multiple_of((row * PITCH + column) * block, 16)

            fields = [(g, f) for g in range(groups) for f in range(FOLD)]
            dz = [Z[g, pl.ds(start(f + 1, left + 1), width * block), :] for g, f in fields]
            dz = jnp.concatenate(dz, axis=0)
            moved = [
                field[section, g, pl.ds(start(f + t // 3, left + lax.rem(t, 3)), width * block), :] for g, f in fields
            ]
            moved = jnp.concatenate(moved, axis=0)
            grad = lax.dot_general(moved, dz, (((0,), (0,)), ((), ())), preferred_element_type=F32)
            at = pl.ds(pl.multiple_of(c * taps + t * channels, channels), channels)
            stage[section, at, :] = grad.astype(BF16)
            if i == 4 and own_taps:
                reduce_core(section, c)
            for after, step in meanwhile:
                if after == i:
                    step()
        if not own_taps:
            at = pl.ds(c * taps, taps)
            pltpu.make_async_copy(stage.at[section, at], tap_out.at[section, at], reduce_sem.at[0, section, c, 0]).start()

    def reduce_level(section, c, cut=0):
        if not own_taps:
            return
        k = 2 * section + c
        some = shard_rows // cuts_of(section, c)
        came(siblings.at[k, pl.ds(0, LAYER * some)], reduce_sem.at[1, section, c, cut])
        own = half_at(stage, section, c, core)
        for place in range(LAYER):
            at = pl.ds(place * shard_rows + cut * some, some)
            own[at, :] = (own[at, :].astype(F32) + siblings[k, at, :].astype(F32)).astype(BF16)
        for j in range(1, LAYER):
            place = lax.rem(spot + j, LAYER)
            part = own.at[pl.ds(pl.multiple_of(place * shard_rows + cut * some, 16), some)]
            remote(
                part, layers.at[k, spot, pl.ds(cut * some, some)], reduce_sem.at[2, section, c, 0],
                reduce_sem.at[3, section, c, cut], core, level * LAYER + place,
            ).start()
        mine_at = pl.ds(pl.multiple_of(spot * shard_rows + cut * some, 16), some)
        layers[k, spot, pl.ds(cut * some, some), :] = own[mine_at, :]

    def reduce_column(section, c, cut=0):
        if not own_taps:
            return
        k = 2 * section + c
        some = shard_rows // cuts_of(section, c)
        at = pl.ds(cut * some, some)
        came(siblings.at[k, pl.ds(0, (LAYER - 1) * some)], reduce_sem.at[3, section, c, cut])
        columns[k, at, :] = sum(layers[k, j, at, :].astype(F32) for j in range(LAYER)).astype(BF16)
        part, to = columns.at[k, at], arrivals.at[level, at]
        owner = 2 * c + core
        here = (core == section) & (owner == level)

        @pl.when(here)
        def _():
            pltpu.make_async_copy(part, to, reduce_sem.at[5, 0, 0, 0]).start()

        @pl.when(jnp.logical_not(here))
        def _():
            remote(
                part, to, reduce_sem.at[4, section, c, 0], reduce_sem.at[5, 0, 0, 0], section, owner * LAYER + spot
            ).start()

    def reduce_done():
        if not own_taps:
            return
        came(arrivals, reduce_sem.at[5, 0, 0, 0])
        tap_out[...] = sum(arrivals[j].astype(F32) for j in range(levels))

    def conv_window(owner):
        start = jnp.minimum(owner * flat // (PLANES + 1), channels - HC_ROWS)
        return pl.multiple_of(start // 8 * 8, 8)

    def hidden_window(owner):
        start = jnp.maximum(owner * flat - conv_end, 0) // VHIDDEN
        return pl.multiple_of(jnp.minimum(start // 8 * 8, hw_grad.shape[0] - HW_ROWS), 8)

    def head_exchange():
        remote(hc_grad, hc_in, head_sem.at[0], head_sem.at[1], 1 - core, me).start()
        remote(hw_grad, hw_in, head_sem.at[2], head_sem.at[3], 1 - core, me).start()

    def head_spread():
        sent(hc_grad, head_sem.at[0])
        sent(hw_grad, head_sem.at[2])
        came(hc_in, head_sem.at[1])
        came(hw_in, head_sem.at[3])
        hc_grad[...] += hc_in[...]
        hw_grad[...] += hw_in[...]

        def spread(j, carry):
            peer = lax.rem(me + j, n_dp)
            owner = core * n_dp + peer

            @pl.when(owner * flat < conv_end)
            def _():
                window = hc_grad.at[pl.ds(conv_window(owner), HC_ROWS)]
                remote(window, hc_slots.at[me], head_sem.at[4], head_sem.at[5], core, peer).start()

            @pl.when((owner + 1) * flat > conv_end)
            def _():
                window = hw_grad.at[pl.ds(hidden_window(owner), HW_ROWS)]
                remote(window, hw_slots.at[me], head_sem.at[6], head_sem.at[7], core, peer).start()

            return carry

        lax.fori_loop(1, n_dp, spread, 0)
        owner = core * n_dp + me
        hc_slots[me] = hc_grad[pl.ds(conv_window(owner), HC_ROWS), :]
        hw_slots[me] = hw_grad[pl.ds(hidden_window(owner), HW_ROWS), :]

    def head_done():
        owner = core * n_dp + me
        lines = small_out.shape[0] - 2

        def unsent(j, carry):
            peer = core * n_dp + lax.rem(me + j, n_dp)

            @pl.when(peer * flat < conv_end)
            def _():
                sent(hc_slots.at[0], head_sem.at[4])

            @pl.when((peer + 1) * flat > conv_end)
            def _():
                sent(hw_slots.at[0], head_sem.at[6])

            return carry

        lax.fori_loop(1, n_dp, unsent, 0)

        @pl.when(owner * flat < conv_end)
        def _():
            came(hc_slots.at[pl.ds(0, n_dp - 1)], head_sem.at[5])
            hc_in[pl.ds(0, HC_ROWS), :] = jnp.sum(hc_slots[...], axis=0)
            for line in range(lines):
                start = owner * flat + line * LANES
                row = start // (PLANES + 1)
                off = start - row * (PLANES + 1)
                out = jnp.zeros((1, LANES), F32)
                for m in range(3):
                    at = jnp.clip(row + m - conv_window(owner), 0, HC_ROWS - 1)
                    begin = (PLANES + 1) * m - off
                    part = pltpu.roll(hc_in[pl.ds(at, 1), :], lax.rem(begin + LANES, LANES), axis=1)
                    fits = (one_lane >= begin) & (one_lane < begin + PLANES + 1) & (start + one_lane < conv_end)
                    out = jnp.where(fits, part, out)
                small_out[pl.ds(2 + line, 1), :] = out

        @pl.when((owner + 1) * flat > conv_end)
        def _():
            came(hw_slots.at[pl.ds(0, n_dp - 1)], head_sem.at[7])
            window = jnp.sum(hw_slots[...], axis=0)
            for i in range(2):
                hidden_w[i, pl.ds(0, HW_ROWS), :] = window[:, i * LANES : (i + 1) * LANES]
            for line in range(lines):
                start = owner * flat + line * LANES
                from_end = start - conv_end + 64 * LANES
                row = from_end // LANES
                off = from_end - row * LANES
                out = small_out[pl.ds(2 + line, 1), :]
                for m in range(2):
                    at = jnp.clip(row + m - 64 - 2 * hidden_window(owner), 0, 2 * HW_ROWS - 1)
                    begin = LANES * m - off
                    part = hidden_w[lax.rem(at, 2), pl.ds(at // 2, 1), :]
                    part = pltpu.roll(part, lax.rem(begin + LANES, LANES), axis=1)
                    fits = (one_lane >= begin) & (one_lane < begin + LANES) & (start + one_lane >= conv_end)
                    out = jnp.where(fits, part, out)
                small_out[pl.ds(2 + line, 1), :] = out

    def norm_exchange():
        remote(norm_grad, norm_in, head_sem.at[8], head_sem.at[9], 1 - core, me).start()

    def norm_done():
        came(norm_in, head_sem.at[9])
        sent(norm_grad, head_sem.at[8])
        at = me * share
        tile, off = at // LANES, lax.rem(at, LANES)
        sums = norm_grad[...] + norm_in[...]
        for i in range(2):
            hidden_w[i, pl.ds(0, 8), :] = sums[:, i * LANES : (i + 1) * LANES]
        for i in range(2):
            part = hidden_w[lax.rem(tile, 2), pl.ds(4 * core + 2 * i + tile // 2, 1), :]
            small_out[pl.ds(i, 1), :] = pltpu.roll(part, lax.rem(LANES - off, LANES), axis=1)

    small_out[...] = jnp.zeros_like(small_out)

    def head_step(g):
        merge_moments(3, g)
        heads(g)
        outer_grad(1, g)

    for_groups(head_step)
    for_groups(head_taps)
    head_exchange()
    for section in (1, 0):

        def second_step(g, section=section):
            norm_back(section, 1, g)
            inner_grad(section, g)
            if section == 0:

                @pl.when(g == 0)
                def _():
                    reduce_level(1, 0)

        for_groups(second_step)
        if section == 1:
            head_spread()
        else:
            reduce_column(1, 1)
        tap_gradient(section, 1)

        def first_step(g, section=section):
            norm_back(section, 0, g)
            if section == 1:
                entry(section, g)
                outer_grad(0, g)

                @pl.when(g == 0)
                def _():
                    reduce_level(1, 1)

        for_groups(first_step)
        if section == 1:
            tap_gradient(1, 0)
        else:
            reduce_level(0, 1)
            norm_exchange()
            tap_gradient(0, 0, ((2, functools.partial(reduce_column, 1, 0)),))

    swap_at = pl.multiple_of(core * groups * rows, 16)

    def last_step(g, after_half, after_field, after_all):
        def add_field(at, part):
            B[g, at, :] += part

        for f in range(FOLD):
            add_field(pl.ds(f * span + block, span - 2 * block), back_middle(0, 0, g, f))
            if f == 1:
                after_half()
        for q in (0, WIDE - 1):
            out = back_outer(0, 0, g, q)
            for f in range(FOLD):
                add_field(pl.ds(f * span + q * block, block), out[f * block : (f + 1) * block])
        after_field()

        def restore(f, q, carry):
            v = B[g, plain(f, q), :]
            for at, square in halves(f, q):
                for i in range(channels // LANES):
                    turn[i, pl.ds(square, per, stride=64), :] = part_of(v, at)[:, i * LANES : (i + 1) * LANES]
            return carry

        each(restore)
        to = pl.ds(g * rows, rows)
        mine[to, :] = turn[core].astype(BF16)
        theirs[to, :] = turn[1 - core].astype(BF16)
        at = pl.ds(pl.multiple_of(swap_at + g * rows, 16), rows)
        remote(
            theirs.at[to], entry_grad.at[at], swap_sem.at[0, g], swap_sem.at[1, g], 1 - core, me
        ).start()
        pltpu.make_async_copy(mine.at[to], entry_grad.at[at], swap_sem.at[2, g]).start()
        after_all()

    def nothing():
        pass

    steps = [functools.partial(reduce_level, 0, 0, cut) for cut in range(CUTS)]
    steps += [functools.partial(reduce_column, 0, 1)]
    steps += [functools.partial(reduce_column, 0, 0, cut) for cut in range(CUTS)]
    if not own_taps:
        steps = [nothing] * len(steps)
    for g in range(groups):
        last_step(g, *(steps[3 * g : 3 * g + 3] + [nothing] * 3)[:3])
    for step in steps[3 * groups :]:
        step()
    head_done()
    norm_done()

    sent(packs.at[core, pl.ds(0, n_dp - 1)], pack_sem.at[0])
    sent(packs.at[core], pack_sem.at[2])
    for section in range(2):
        for c in range(2):
            k = 2 * section + c
            if not own_taps:
                at = pl.ds(c * taps, taps)
                pltpu.make_async_copy(
                    stage.at[section, at], tap_out.at[section, at], reduce_sem.at[0, section, c, 0]
                ).wait()
                continue
            three = stage.at[section, pl.ds(0, (LAYER - 1) * shard_rows)]

            @pl.when((core == section) & (level // 2 == c))
            def _(section=section, c=c):
                sent(stage.at[section, pl.ds(0, (levels - 1) * shard_rows)], fetch_sem.at[0, section, c, 0])

                @pl.when(lax.rem(level, 2) != core)
                def _():
                    sent(stage.at[section, pl.ds(0, shard_rows)], fetch_sem.at[0, section, c, 0])

            sent(three, fetch_sem.at[2, section, c, 0])
            sent(half_at(stage, section, c, core), fetch_sem.at[4, section, c, 0])
            sent(siblings.at[k], reduce_sem.at[0, section, c, 0])
            sent(three, reduce_sem.at[2, section, c, 0])

            @pl.when(jnp.logical_not((core == section) & (2 * c + core == level)))
            def _(section=section, c=c, k=k):
                sent(columns.at[k], reduce_sem.at[4, section, c, 0])

    reduce_done()
    for g in range(groups):
        to = pl.ds(g * rows, rows)
        at = pl.ds(pl.multiple_of(swap_at + g * rows, 16), rows)
        remote(theirs.at[to], entry_grad.at[at], swap_sem.at[0, g], swap_sem.at[1, g], 1 - core, me).wait()
        pltpu.make_async_copy(mine.at[to], entry_grad.at[at], swap_sem.at[2, g]).wait()


def finish(parts, entry_in, tap_in, small_in, entry_out, tap_out, gain_out, shift_out, head_out, narrow, broad, taps, small, sem):
    some = entry_in.shape[0] // parts
    cuts = [pl.ds(i * some, some) for i in range(parts)]
    loads = [pltpu.make_async_copy(entry_in.at[at], narrow.at[at], sem.at[0, i]) for i, at in enumerate(cuts)]
    stores = [pltpu.make_async_copy(broad.at[at], entry_out.at[at], sem.at[1, i]) for i, at in enumerate(cuts)]
    tap_load = pltpu.make_async_copy(tap_in, taps, sem.at[0, parts])
    tap_store = pltpu.make_async_copy(taps, tap_out, sem.at[1, parts])
    for load in loads:
        load.start()
    tap_load.start()
    small_load = pltpu.make_async_copy(small_in, small, sem.at[0, parts + 1])
    small_load.start()
    small_load.wait()
    gain_out[...] = small[pl.ds(0, 1), pl.ds(0, gain_out.shape[1])]
    shift_out[...] = small[pl.ds(1, 1), pl.ds(0, gain_out.shape[1])]
    flat = head_out.shape[0]
    for line in range(0, flat, LANES):
        count = min(LANES, flat - line)
        head_out[pl.ds(line, count)] = small[pl.ds(2 + line // LANES, 1), pl.ds(0, count)].reshape(count)
    for at, load, store in zip(cuts, loads, stores):
        load.wait()
        broad[at, :] = narrow[at, :].astype(F32)
        store.start()
    tap_load.wait()
    tap_store.start()
    for store in stores:
        store.wait()
    tap_store.wait()


def local(
    board_input, conv_weight, norm_gains, norm_shifts, head_params, policy_target, legal_mask, value_target
):
    n_dp, n_pipe = lax.axis_size("dp"), lax.axis_size("pipe")
    positions, channels = board_input.shape[0], board_input.shape[-1]
    per = positions // MICRO
    groups = MICRO // n_pipe
    moves = legal_mask.shape[1]
    rows = per * 64
    padded = (FOLD + 2) * PITCH * 2 * per
    taps = 9 * channels

    shard_rows = conv_weight.shape[1]
    own_taps = shard_rows % 16 == 0 and n_dp == 4 * LAYER
    share, flat = norm_gains.shape[1], head_params.shape[0]
    lines = -(-flat // LANES)
    pack_rows = -(-(2 + lines) // 8) * 8
    taps_in = conv_weight
    if not own_taps:
        taps_in = lax.all_gather(lax.all_gather(conv_weight, "dp", axis=1, tiled=True), "pipe", axis=0, tiled=True)

    vmem = pl.BlockSpec(memory_space=pltpu.VMEM)
    smem = pl.BlockSpec(memory_space=pltpu.SMEM)
    anywhere = pl.BlockSpec(memory_space=pl.ANY)
    dma, regular = pltpu.SemaphoreType.DMA, pltpu.VMEM
    tap_shape = (shard_rows, channels) if own_taps else (2, 2 * taps, channels)
    lane_rows = shard_rows if own_taps else 16
    tap_grad, small_grad, entry_grad = pl.pallas_call(
        functools.partial(
            kernel, (n_dp, per, groups, moves, 1.0 / positions, shard_rows, own_taps, flat)
        ),
        out_shape=(
            jax.ShapeDtypeStruct(tap_shape, F32 if own_taps else BF16),
            jax.ShapeDtypeStruct((pack_rows, LANES), F32),
            jax.ShapeDtypeStruct((positions * 64, LANES), BF16),
        ),
        in_specs=[smem, smem, anywhere, anywhere, vmem, vmem, vmem, anywhere],
        out_specs=(vmem if own_taps else anywhere, vmem, anywhere),
        scratch_shapes=[
            regular((2, 2 * taps, channels), BF16),
            regular((2, groups, padded, channels), BF16),
            regular((2, groups, padded, channels), BF16),
            regular((groups, padded, channels), BF16),
            regular((2, 2, groups, rows, channels), F32),
            regular((groups, rows, channels), F32),
            regular((groups * per, 8, 8, channels), BF16),
            regular((groups * per, moves), jnp.int32),
            regular((groups, rows, LANES), F32),
            regular((rows, LANES), F32),
            regular((channels // LANES, rows, LANES), F32),
            regular((groups * per, LANES), jnp.int32),
            regular((groups * per, LANES), F32),
            regular((2, 2 * taps, channels), BF16),
            regular((4, groups, 8, channels), F32),
            regular((8, groups, n_dp, 2, channels), F32),
            regular((groups * rows, LANES), BF16),
            regular((groups * rows, LANES), BF16),
            regular((2, n_dp, pack_rows, LANES), F32),
            regular((2, 8, channels), F32),
            regular((channels, LANES), F32),
            regular((2, channels, 2 * LANES), BF16),
            regular((2, LANES + 8, LANES), F32),
            regular((8, channels), F32),
            regular((channels, LANES), F32),
            regular((72, VHIDDEN), F32),
            regular((8, channels), F32),
            regular((channels, LANES), F32),
            regular((72, VHIDDEN), F32),
            regular((n_dp, HC_ROWS, LANES), F32),
            regular((n_dp, HW_ROWS, VHIDDEN), F32),
            regular((4, LAYER * lane_rows, channels), BF16),
            regular((4, LAYER, lane_rows, channels), BF16),
            regular((4, lane_rows, channels), BF16),
            regular((4, lane_rows, channels), BF16),
            dma((3,)),
            dma((8, groups)),
            dma((8, groups)),
            dma((3, groups)),
            dma((4,)),
            dma((10,)),
            dma((6, 2, 2, FETCH_CUTS)),
            dma((6, 2, 2, CUTS)),
        ],
        compiler_params=pltpu.CompilerParams(
            collective_id=0, has_side_effects=True, vmem_limit_bytes=63 * 2**20
        ),
    )(
        policy_target, value_target, board_input, taps_in, norm_gains, norm_shifts, head_params,
        legal_mask,
    )

    conv_grad = tap_grad
    if not own_taps:
        conv_grad = lax.psum_scatter(
            tap_grad.astype(F32).reshape(4 * taps, channels), ("pipe", "dp"), scatter_dimension=0, tiled=True
        )
    parts = 6
    entry_grad, conv_grad, gain_grad, shift_grad, head_grad = pl.pallas_call(
        functools.partial(finish, parts),
        out_shape=(
            jax.ShapeDtypeStruct(entry_grad.shape, F32),
            jax.ShapeDtypeStruct(conv_grad.shape, F32),
            jax.ShapeDtypeStruct((1, share), F32),
            jax.ShapeDtypeStruct((1, share), F32),
            jax.ShapeDtypeStruct((flat,), F32),
        ),
        in_specs=[anywhere, anywhere, anywhere],
        out_specs=(anywhere, anywhere, vmem, vmem, vmem),
        scratch_shapes=[
            regular(entry_grad.shape, BF16),
            regular(entry_grad.shape, F32),
            regular(conv_grad.shape, F32),
            regular(small_grad.shape, F32),
            dma((2, parts + 2)),
        ],
        compiler_params=pltpu.CompilerParams(vmem_limit_bytes=60 * 2**20),
    )(entry_grad, conv_grad, small_grad)
    entry_grad = entry_grad.reshape(positions, 8, 8, LANES)
    return conv_grad[None], gain_grad, shift_grad, head_grad, entry_grad


def solution(mesh):
    placed = (
        P("dp", None, None, None),
        P("pipe", "dp", None),
        P("pipe", "dp"),
        P("pipe", "dp"),
        P(("pipe", "dp")),
        P("dp"),
        P("dp", None),
        P("dp"),
    )
    return jax.shard_map(
        local,
        mesh=mesh,
        in_specs=placed,
        out_specs=(
            P("pipe", "dp", None),
            P("pipe", "dp"),
            P("pipe", "dp"),
            P(("pipe", "dp")),
            P("dp", None, None, "pipe"),
        ),
        check_vma=False,
    )
```

```python
import functools

import jax
import jax.numpy as jnp
from jax import lax
from jax.experimental import pallas as pl
from jax.experimental.pallas import tpu as pltpu
from jax.sharding import PartitionSpec as P

PLANES = 73
VHIDDEN = 256
MICRO = 4
EPSILON = 1e-05
F32, BF16 = jnp.float32, jnp.bfloat16
PRECISE = lax.Precision.HIGHEST
MESH = pl.DeviceIdType.MESH
LANES = 128
ILLEGAL = -1e30
HC_ROWS, HW_ROWS = 24, 16
LAYER = 4
CUTS = 3
FETCH_CUTS = 6
COLS = 8

FOLD, WIDE, PITCH = 4, 8, 10


def sigmoid(v):
    return 0.5 * jnp.tanh(0.5 * v) + 0.5


def silu_slope(v):
    s = sigmoid(v)
    return s * (1.0 + v * (1.0 - s))


def fold8(v):
    return jnp.sum(v.reshape(v.shape[0] // 8, 8, v.shape[1]), axis=0)


def total(v):
    return jnp.sum(v, axis=0, keepdims=True)


def kernel(
    sizes, policy, value_goal, board, shard, gain_part, shift_part, head_part, legal,
    tap_out, small_out, entry_grad,
    W, X, I, Z, C, B, raw, mask_raw, code, planes, turn, goal, vgoal, stage, stat, slots, mine, theirs,
    packs, gains, head_conv, head_pair, hidden_w, norm_grad, hc_grad, hw_grad, norm_in, hc_in, hw_in, hc_slots, hw_slots,
    siblings, layers, columns, arrivals,
    load_sem, send_sem, recv_sem, swap_sem, pack_sem, head_sem, fetch_sem, reduce_sem,
):
    n_dp, per, groups, moves, scale, shard_rows, own_taps, flat = sizes
    core, me = lax.axis_index("pipe"), lax.axis_index("dp")
    block = 2 * per
    span = WIDE * block
    rows = FOLD * span
    channels = X.shape[-1]
    taps = 9 * channels
    all_rows = n_dp * rows
    spot, level = lax.rem(me, LAYER), me // LAYER
    levels = n_dp // LAYER

    def remote(src, dst, send, recv, pipe, dp):
        return pltpu.make_async_remote_copy(
            src_ref=src, dst_ref=dst, send_sem=send, recv_sem=recv, device_id=(pipe, dp), device_id_type=MESH
        )

    def sent(ref, sem):
        remote(ref, ref, sem, sem, 1 - core, me).wait_send()

    def came(ref, sem):
        remote(ref, ref, sem, sem, 1 - core, me).wait_recv()

    barrier = pltpu.get_barrier_semaphore()

    def greet(j, carry):
        pl.semaphore_signal(barrier, inc=1, device_id=(core, lax.rem(me + j, n_dp)), device_id_type=MESH)
        return carry

    def greet_column(j, carry):
        other = lax.rem(me + j * LAYER, n_dp)
        pl.semaphore_signal(barrier, inc=1, device_id=(1 - core, other), device_id_type=MESH)
        return carry

    lax.fori_loop(1, n_dp, greet, 0)
    lax.fori_loop(0, levels, greet_column, 0)

    first = pl.multiple_of(core * groups * per, 8)
    loads = [
        pltpu.make_async_copy(board.at[pl.ds(first, groups * per)], raw, load_sem.at[0]),
        pltpu.make_async_copy(legal.at[pl.ds(first, groups * per)], mask_raw, load_sem.at[1]),
    ]
    if not own_taps:
        loads.append(pltpu.make_async_copy(shard, W, load_sem.at[2]))
    for load in loads:
        load.start()
    pl.semaphore_wait(barrier, n_dp - 1 + levels)

    def shard_at(section, c, half, place):
        start = c * taps + (half * LAYER + place) * shard_rows
        return W.at[section, pl.ds(pl.multiple_of(start, 16), shard_rows)]

    def half_at(ref, section, c, half):
        start = c * taps + half * LAYER * shard_rows
        return ref.at[section, pl.ds(pl.multiple_of(start, 16), LAYER * shard_rows)]

    def cuts_of(section, c):
        return CUTS if section + c == 0 else 1

    def fetch_cuts_of(section, c):
        return FETCH_CUTS if section + c == 0 else 1

    def cut_at(ref, cuts, cut):
        some = shard_rows // cuts
        return ref.at[pl.ds(cut * some, some)]

    def fetch_column(section, c):
        if not own_taps:
            return

        @pl.when((core == section) & (level // 2 == c))
        def _():
            half = lax.rem(level, 2)
            cuts = fetch_cuts_of(section, c)
            for cut in range(cuts):
                at = cut_at(shard_at(section, c, half, spot), cuts, cut)
                src = cut_at(shard.at[0], cuts, cut)
                send, recv = fetch_sem.at[0, section, c, 0], fetch_sem.at[1, section, c, cut]
                for j in range(1, levels):
                    remote(src, at, send, recv, half, lax.rem(me + j * LAYER, n_dp)).start()

                @pl.when(half == core)
                def _(src=src, at=at, recv=recv):
                    pltpu.make_async_copy(src, at, recv).start()

                @pl.when(half != core)
                def _(src=src, at=at, send=send, recv=recv):
                    remote(src, at, send, recv, half, me).start()

    def fetch_level(section, c, cut=0):
        if not own_taps:
            return
        at = cut_at(shard_at(section, c, core, spot), fetch_cuts_of(section, c), cut)
        came(at, fetch_sem.at[1, section, c, cut])
        for j in range(1, LAYER):
            peer = level * LAYER + lax.rem(spot + j, LAYER)
            remote(at, at, fetch_sem.at[2, section, c, 0], fetch_sem.at[3, section, c, cut], core, peer).start()

    def fetch_core(section, c):
        if not own_taps:
            return
        cuts = fetch_cuts_of(section, c)
        send, recv = fetch_sem.at[4, section, c, 0], fetch_sem.at[5, section, c, 0]
        for cut in range(cuts):
            some = W.at[section, pl.ds(c * taps, (LAYER - 1) * shard_rows // cuts)]
            came(some, fetch_sem.at[3, section, c, cut])
            for place in range(LAYER) if cuts > 1 else ():
                at = cut_at(shard_at(section, c, core, place), cuts, cut)
                remote(at, at, send, recv, 1 - core, me).start()
        if cuts == 1:
            at = half_at(W, section, c, core)
            remote(at, at, send, recv, 1 - core, me).start()

    def fetch_done(section, c):
        if not own_taps:
            return
        came(half_at(W, section, c, 1 - core), fetch_sem.at[5, section, c, 0])

    def send_pack(j, carry):
        remote(
            packs.at[core, me], packs.at[core, me], pack_sem.at[0], pack_sem.at[1], core, lax.rem(me + j, n_dp)
        ).start()
        return carry

    fetch_column(0, 0)
    fetch_column(0, 1)

    wide = COLS * block

    def padded(f, q):
        return pl.ds(((f + 1) * PITCH + 1 + q) * block, wide)

    def put(ref, at, f, q, y):
        ref[*at, padded(f, q), :] = y.astype(BF16)
        none = jnp.zeros((COLS, per, channels), F32)
        parts = y.reshape(COLS, block, channels)
        if f == FOLD - 1:
            halo = jnp.concatenate([none, parts[:, :per]], axis=1).reshape(wide, channels)
            ref[*at, padded(-1, q), :] = halo.astype(BF16)
        if f == 0:
            halo = jnp.concatenate([parts[:, per:], none], axis=1).reshape(wide, channels)
            ref[*at, padded(FOLD, q), :] = halo.astype(BF16)

    def plain(f, q):
        return pl.ds((f * WIDE + q) * block, wide)

    def each(body, carry=0):
        for q in range(0, WIDE, COLS):
            for f in range(FOLD):
                carry = body(f, q, carry)
        return carry

    def halves(f, q):
        for i in range(COLS):
            for half in range(2):
                yield pl.ds((2 * i + half) * per, per), (f + FOLD * half) * 8 + q + i

    def part_of(v, at):
        return v[at.start : at.start + per]

    loads[0].wait()
    for g in range(groups):

        def widen(b, carry, g=g):
            rows_of = raw[g * per + b].astype(F32).reshape(64, channels)
            for i in range(channels // LANES):
                turn[i, pl.ds(pl.multiple_of(b * 64, 64), 64), :] = rows_of[:, i * LANES : (i + 1) * LANES]
            return carry

        lax.fori_loop(0, per, widen, 0)

        def reorder(f, q, carry, g=g):
            parts = [
                jnp.concatenate([turn[i, pl.ds(square, per, stride=64), :] for _, square in halves(f, q)], axis=0)
                for i in range(channels // LANES)
            ]
            put(X, (0, g), f, q, jnp.concatenate(parts, axis=1))
            return carry

        each(reorder)
        if g < FETCH_CUTS - 1:
            fetch_level(0, 0, g)

    for cut in range(min(groups, FETCH_CUTS - 1), FETCH_CUTS):
        fetch_level(0, 0, cut)
    packs[core, me] = jnp.zeros(packs.shape[2:], F32)
    for i, part in enumerate((gain_part, shift_part)):
        packs[core, me, pl.ds(i, 1), pl.ds(0, part.shape[1])] = part[...].astype(F32)
    for line in range(0, flat, LANES):
        count = min(LANES, flat - line)
        packs[core, me, pl.ds(2 + line // LANES, 1), pl.ds(0, count)] = head_part[pl.ds(line, count)].reshape(1, count)
    lax.fori_loop(1, n_dp, send_pack, 0)
    fetch_level(0, 1)
    fetch_column(1, 0)
    fetch_column(1, 1)

    both = groups * per
    row_of = lax.broadcasted_iota(jnp.int32, (both, LANES), 0)
    lane_of = lax.broadcasted_iota(jnp.int32, (both, LANES), 1)

    def column_of(ref, zero):
        def pick(b, acc):
            return jnp.where(row_of == b, ref[first + b], acc)

        return lax.fori_loop(0, both, pick, zero)

    goal[...] = column_of(policy, jnp.zeros((both, LANES), jnp.int32))
    vgoal[...] = column_of(value_goal, jnp.zeros((both, LANES), F32))
    loads[1].wait()
    def legal_moves():
        for square in range(64):
            base = square * PLANES // LANES * LANES
            shift = square * PLANES - base
            width = min(2 * LANES, moves - base)
            window = mask_raw[:, base : base + width]
            if width < 2 * LANES:
                window = jnp.concatenate([window, jnp.zeros((both, 2 * LANES - width), jnp.int32)], axis=1)
            if shift:
                window = pltpu.roll(window, 2 * LANES - shift, axis=1)
            window = window[:, :LANES]
            hit = goal[...] == lane_of + square * PLANES
            kind = jnp.where(hit, 2.0, jnp.where(window > 0, 1.0, 0.0))
            kind = jnp.where(lane_of < PLANES, kind, 0.0)
            f, q, half = square // 8 % FOLD, square % 8, square // 8 // FOLD
            at = ((f * WIDE + q) * 2 + half) * per
            for g in range(groups):
                code[g, pl.ds(at, per), :] = kind[g * per : (g + 1) * per]

    legal_moves()
    hc_grad[...] = jnp.zeros_like(hc_grad)
    hw_grad[...] = jnp.zeros_like(hw_grad)
    norm_grad[...] = jnp.zeros_like(norm_grad)
    fetch_core(0, 0)
    came(packs.at[core, pl.ds(0, n_dp - 1)], pack_sem.at[1])
    remote(packs.at[core], packs.at[core], pack_sem.at[2], pack_sem.at[3], 1 - core, me).start()

    share = 2 * channels // n_dp

    def unpack_gains():
        tile_share = LANES // share
        for section in range(2):
            for tile in range(2 * channels // LANES):
                acc = jnp.zeros((2, LANES), F32)
                for u in range(tile_share):
                    part = packs[section, tile * tile_share + u, pl.ds(0, 2), :]
                    acc = acc + (pltpu.roll(part, u * share, axis=1) if u else part)
                c, at = tile * LANES // channels, tile * LANES % channels
                gains[section, pl.ds(c, 1), pl.ds(at, LANES)] = acc[0:1]
                gains[section, pl.ds(2 + c, 1), pl.ds(at, LANES)] = acc[1:2]

    one_lane = lax.broadcasted_iota(jnp.int32, (1, LANES), 1)
    conv_end = (PLANES + 1) * channels

    def flat_row(start, count):
        owner, off = divmod(start, flat)
        line, lane_at = divmod(off, LANES)

        def line_of(owner, line, back):
            row = packs[owner // n_dp, owner % n_dp, pl.ds(line + 2, 1), :]
            return pltpu.roll(row, back % LANES, axis=1) if back % LANES else row

        row = line_of(owner, line, -lane_at)
        if lane_at + count > LANES and off + LANES - lane_at < flat:
            row = jnp.where(one_lane < LANES - lane_at, row, line_of(owner, line + 1, -lane_at))
        if off + count > flat:
            row = jnp.where(one_lane < flat - off, row, line_of(owner + 1, 0, flat - off))
        return jnp.where(one_lane < count, row, 0.0) if count < LANES else row

    def unpack_heads():
        for i in range(channels):
            head_conv[pl.ds(i, 1), :] = flat_row(i * (PLANES + 1), PLANES + 1)
        near = head_conv[...].astype(BF16)
        rest = (head_conv[...] - near.astype(F32)).astype(BF16)
        head_pair[0] = jnp.concatenate([near, rest], axis=1)
        head_pair[1] = jnp.concatenate([near, near], axis=1)
        hidden_w[...] = jnp.zeros_like(hidden_w)
        for i in range(2 * 66):
            line = i // 2 if i < 128 else i // 2 + 64
            hidden_w[i % 2, pl.ds(line, 1), :] = flat_row(conv_end + i * LANES, LANES)

    fetch_done(0, 0)
    if not own_taps:
        loads[2].wait()

    def push(k, g, top, bottom):
        slots[k, g, me, pl.ds(0, 1), :] = top
        slots[k, g, me, pl.ds(1, 1), :] = bottom

        def send(j, carry):
            pltpu.make_async_remote_copy(
                src_ref=slots.at[k, g, me],
                dst_ref=slots.at[k, g, me],
                send_sem=send_sem.at[k, g],
                recv_sem=recv_sem.at[k, g],
                device_id=(core, lax.rem(me + j, n_dp)),
                device_id_type=MESH,
            ).start()
            return carry

        lax.fori_loop(1, n_dp, send, 0)

    def arrived(k, g):
        others = slots.at[k, g, pl.ds(0, n_dp - 1)]
        copy = pltpu.make_async_remote_copy(
            src_ref=others, dst_ref=others, send_sem=send_sem.at[k, g], recv_sem=recv_sem.at[k, g],
            device_id=(core, lax.rem(me + 1, n_dp)), device_id_type=MESH,
        )
        copy.wait_send()
        copy.wait_recv()
        return slots[k, g]

    def merge_moments(k, g):
        parts = arrived(k, g)
        both_sums = jnp.sum(parts, axis=0)
        mean = both_sums[0:1] / n_dp
        apart = parts - mean
        between = jnp.sum(apart * apart, axis=0)[0:1]
        spread = (both_sums[1:2] + between * rows) / all_rows
        stat[k, g, pl.ds(0, 1), :] = mean
        stat[k, g, pl.ds(1, 1), :] = lax.rsqrt(spread + EPSILON)

    def norm_of(section, c, g):
        k = 2 * section + c
        gain = gains[section, pl.ds(c, 1), :]
        shift = gains[section, pl.ds(2 + c, 1), :]
        return stat[k, g, pl.ds(0, 1), :], stat[k, g, pl.ds(1, 1), :], gain, shift

    def slab(field, at, f, q, width, t):
        start = ((f + t // 3) * PITCH + q + t % 3) * block
        return field[*at, pl.ds(start, width * block), :]

    def taps_of(section, c, some):
        return [W[section, pl.ds(c * taps + t * channels, channels), :] for t in some]

    def convolve(field, section, c, g):
        k = 2 * section + c
        counted = []

        def note(out, count):
            part = total(fold8(out))
            apart = out - part / count
            counted.append((part, total(fold8(apart * apart)), count))

        middle = W[section, pl.ds(c * taps, taps), :]
        for f in range(FOLD):
            slabs = [slab(field, (section, g), f, 1, WIDE - 2, t) for t in range(9)]
            out = jnp.dot(jnp.concatenate(slabs, axis=1), middle, preferred_element_type=F32)
            C[section, c, g, pl.ds(f * span + block, span - 2 * block), :] = out
            note(out, span - 2 * block)
        for q, skip in ((0, 0), (WIDE - 1, 2)):
            some = [t for t in range(9) if t % 3 != skip]
            slabs = [
                jnp.concatenate([slab(field, (section, g), f, q, 1, t) for t in some], axis=1) for f in range(FOLD)
            ]
            out = jnp.dot(
                jnp.concatenate(slabs, axis=0), jnp.concatenate(taps_of(section, c, some), axis=0),
                preferred_element_type=F32,
            )
            for f in range(FOLD):
                C[section, c, g, pl.ds(f * span + q * block, block), :] = out[f * block : (f + 1) * block]
            note(out, FOLD * block)
        mean = sum(part for part, _, _ in counted) / rows
        spread = sum(apart for _, apart, _ in counted)
        for part, _, count in counted:
            spread = spread + count * jnp.square(part / count - mean)
        push(k, g, mean, spread)

    def inner(section, g):
        mean, inv, gain, shift = norm_of(section, 0, g)
        factor = inv * gain

        def body(f, q, carry):
            v = (C[section, 0, g, plain(f, q), :] - mean) * factor + shift
            put(I, (section, g), f, q, v * sigmoid(v))
            return carry

        each(body)

    def outer_pre(section, g, f, q, norm):
        mean, inv, gain, shift = norm
        z = (C[section, 1, g, plain(f, q), :] - mean) * inv
        return X[section, g, padded(f, q), :].astype(F32) + z * gain + shift, z

    def for_groups(body):
        def step(g, carry):
            body(g)
            return carry

        lax.fori_loop(0, groups, step, 0)

    def entry_step(g):
        convolve(X, 0, 0, g)

    fetch_level(1, 0)
    for_groups(entry_step)
    fetch_level(1, 1)
    came(packs.at[1 - core], pack_sem.at[3])
    unpack_gains()
    unpack_heads()
    fetch_core(0, 1)
    for section in range(2):

        def inner_step(g, section=section):
            merge_moments(2 * section, g)
            inner(section, g)
            if section == 0:

                @pl.when(g == 0)
                def _():
                    fetch_done(0, 1)

            if section == 1:

                @pl.when(g == 0)
                def _():
                    fetch_done(1, 1)

            convolve(I, section, 1, g)

        for_groups(inner_step)
        if section == 0:
            fetch_core(1, 0)

            def hand_step(g):
                merge_moments(1, g)
                norm = norm_of(0, 1, g)

                def hand_on(f, q, carry):
                    v, _ = outer_pre(0, g, f, q, norm)
                    put(X, (1, g), f, q, v * sigmoid(v))
                    return carry

                each(hand_on)

                @pl.when(g == 0)
                def _():
                    fetch_done(1, 0)

                convolve(X, 1, 0, g)

            for_groups(hand_step)
            fetch_core(1, 1)

    lane = lax.broadcasted_iota(jnp.int32, (per, LANES), 1)

    def head_fields(g):
        return [stage.at[g, pl.ds(i * rows, rows)] for i in range(3)]

    def heads(g):
        norm = norm_of(1, 1, g)

        near, rest, slope_parts = head_fields(g)

        def last(f, q, carry):
            v, _ = outer_pre(1, g, f, q, norm)
            final = v * sigmoid(v)
            head = final.astype(BF16)
            near[plain(f, q), :] = head
            rest[plain(f, q), :] = (final - head.astype(F32)).astype(BF16)
            return carry

        each(last)
        for f in range(FOLD):
            at = pl.ds(f * span, span)
            large = jnp.dot(near[at, :], head_pair[0], preferred_element_type=F32)
            small_part = jnp.dot(rest[at, :], head_pair[0, :, :LANES], preferred_element_type=F32)
            planes[at, :] = large[:, :LANES] + (large[:, LANES:] + small_part)

        def look(f, q, carry):
            top, squares = carry
            a = planes[plain(f, q), :]
            a_legal = jnp.where(code[g, plain(f, q), :] > 0, a, ILLEGAL)
            column = a[:, PLANES : PLANES + 1]
            for at, square in halves(f, q):
                top = jnp.maximum(top, part_of(a_legal, at))
                squares = jnp.where(lane == square, part_of(column, at), squares)
            return top, squares

        top, pre = each(look, (jnp.full((per, LANES), ILLEGAL, F32), jnp.zeros((per, LANES), F32)))
        top = jnp.max(top, axis=1, keepdims=True)
        top = jnp.concatenate([top] * (2 * COLS), axis=0)

        def weigh(f, q, acc):
            a = planes[plain(f, q), :]
            e = jnp.where(code[g, plain(f, q), :] > 0, jnp.exp(a - top), 0.0)
            planes[plain(f, q), :] = e
            return acc + jnp.sum(e.reshape(2 * COLS, per, LANES), axis=0)

        norm_sum = jnp.sum(each(weigh, jnp.zeros((per, LANES), F32)), axis=1, keepdims=True)
        portion = scale / norm_sum
        portion = jnp.concatenate([portion] * (2 * COLS), axis=0)

        squares = pre * sigmoid(pre)
        hidden_all = jnp.concatenate([hidden_w[0], hidden_w[1]], axis=1)
        hidden_in, bias, out_w = hidden_all[:LANES], hidden_all[LANES : LANES + 1], hidden_all[LANES + 1 : LANES + 2]
        hidden_pre = jnp.dot(squares, hidden_in, precision=PRECISE, preferred_element_type=F32) + bias
        hidden = hidden_pre * sigmoid(hidden_pre)
        value = jnp.tanh(jnp.sum(hidden * out_w, axis=1, keepdims=True))
        wanted = vgoal[pl.ds(g * per, per), 0:1]
        slope = 2.0 * scale * (value - wanted) * (1.0 - value * value)
        hidden_grad = slope * out_w * silu_slope(hidden_pre)
        hw_grad[pl.ds(0, 64), :] += lax.dot_general(
            squares, hidden_grad, (((0,), (0,)), ((), ())), precision=PRECISE, preferred_element_type=F32
        )[:64]
        hw_grad[pl.ds(64, 1), :] += total(hidden_grad)
        hw_grad[pl.ds(65, 1), :] += total(hidden * slope)
        squares_grad = lax.dot_general(
            hidden_grad, hidden_in, (((1,), (1,)), ((), ())), precision=PRECISE,
            preferred_element_type=F32,
        )
        pre_grad = squares_grad * silu_slope(pre)

        def slopes(f, q, carry):
            e = planes[plain(f, q), :] * portion
            e = e - jnp.where(code[g, plain(f, q), :] > 1.5, scale, 0.0)
            column = jnp.concatenate([pre_grad[:, square : square + 1] for _, square in halves(f, q)], axis=0)
            lane_wide = lax.broadcasted_iota(jnp.int32, (wide, LANES), 1)
            e = jnp.where(lane_wide == PLANES, column, e)
            head = e.astype(BF16)
            slope_parts[plain(f, q), :] = jnp.concatenate([head, (e - head.astype(F32)).astype(BF16)], axis=1)
            return carry

        each(slopes)
        across = (((1,), (1,)), ((), ()))
        for f in range(FOLD):
            at = pl.ds(f * span, span)
            large = lax.dot_general(slope_parts[at, :], head_pair[1], across, preferred_element_type=F32)
            small_part = lax.dot_general(
                slope_parts[at, :LANES], head_pair[0, :, LANES:], across, preferred_element_type=F32
            )
            B[g, at, :] = large + small_part

    def head_taps(g):
        near, rest, slope_parts = head_fields(g)
        turned = (((0,), (0,)), ((), ()))
        large = lax.dot_general(near[...], slope_parts[...], turned, preferred_element_type=F32)
        small_part = lax.dot_general(rest[...], slope_parts[:, :LANES], turned, preferred_element_type=F32)
        hc_grad[...] += large[:, :LANES] + (large[:, LANES:] + small_part)

    def outer_grad(section, g):
        norm = norm_of(section, 1, g)

        def body(f, q, carry):
            shift_sum, gain_sum = carry
            v, z = outer_pre(section, g, f, q, norm)
            grad = B[g, plain(f, q), :]
            if section == 0:
                grad = grad.astype(BF16).astype(F32)
            grad = grad * silu_slope(v)
            B[g, plain(f, q), :] = grad
            return shift_sum + fold8(grad), gain_sum + fold8(grad * z)

        zero = jnp.zeros((8, channels), F32)
        shift_sum, gain_sum = each(body, (zero, zero))
        push(4 + 2 * section + 1, g, total(shift_sum), total(gain_sum))

    def norm_back(section, c, g):
        sums = jnp.sum(arrived(4 + 2 * section + c, g), axis=0)
        norm_grad[pl.ds(4 * section + c, 1), :] += sums[1:2]
        norm_grad[pl.ds(4 * section + 2 + c, 1), :] += sums[0:1]
        mean, inv, gain, _ = norm_of(section, c, g)
        p_mean, pz_mean = sums[0:1] / all_rows, sums[1:2] / all_rows
        factor = inv * gain

        def body(f, q, carry):
            z = (C[section, c, g, plain(f, q), :] - mean) * inv
            p = B[g, plain(f, q), :] if c else C[section, 1, g, plain(f, q), :]
            put(Z, (g,), f, q, factor * (p - p_mean - z * pz_mean))
            return carry

        each(body)

    def back_slab(g, f, q, width, t):
        return Z[g, pl.ds(((f + 2 - t // 3) * PITCH + q + 2 - t % 3) * block, width * block), :]

    def back_dot(slabs, section, c, some):
        acc = None
        for part, t in zip(slabs, some):
            part = lax.dot_general(
                part, W[section, pl.ds(c * taps + t * channels, channels), :], (((1,), (1,)), ((), ())),
                preferred_element_type=F32,
            )
            acc = part if acc is None else acc + part
        return acc

    def back_middle(section, c, g, f):
        return back_dot([back_slab(g, f, 1, WIDE - 2, t) for t in range(9)], section, c, range(9))

    def back_outer(section, c, g, q):
        some = [t for t in range(9) if t % 3 != (2 if q == 0 else 0)]
        slabs = [jnp.concatenate([back_slab(g, f, q, 1, t) for f in range(FOLD)], axis=0) for t in some]
        return back_dot(slabs, section, c, some)

    def back_field(section, c, g, add):
        for f in range(FOLD):
            add(pl.ds(f * span + block, span - 2 * block), back_middle(section, c, g, f))
        for q in (0, WIDE - 1):
            out = back_outer(section, c, g, q)
            for f in range(FOLD):
                add(pl.ds(f * span + q * block, block), out[f * block : (f + 1) * block])

    def inner_grad(section, g):
        def keep_field(at, part):
            C[section, 1, g, at, :] = part

        back_field(section, 1, g, keep_field)
        mean, inv, gain, shift = norm_of(section, 0, g)

        def body(f, q, carry):
            shift_sum, gain_sum = carry
            z = (C[section, 0, g, plain(f, q), :] - mean) * inv
            grad = C[section, 1, g, plain(f, q), :] * silu_slope(z * gain + shift)
            C[section, 1, g, plain(f, q), :] = grad
            return shift_sum + fold8(grad), gain_sum + fold8(grad * z)

        zero = jnp.zeros((8, channels), F32)
        shift_sum, gain_sum = each(body, (zero, zero))
        push(4 + 2 * section, g, total(shift_sum), total(gain_sum))

    def entry(section, g):
        def add_field(at, part):
            B[g, at, :] += part

        back_field(section, 0, g, add_field)

    def reduce_core(section, c):
        k = 2 * section + c
        for cut in range(cuts_of(section, c)):
            for place in range(LAYER) if cuts_of(section, c) > 1 else ():
                at = half_at(stage, section, c, 1 - core).at[pl.ds(place * shard_rows, shard_rows)]
                at = cut_at(at, cuts_of(section, c), cut)
                to = siblings.at[k, pl.ds(place * shard_rows, shard_rows)]
                to = cut_at(to, cuts_of(section, c), cut)
                remote(
                    at, to, reduce_sem.at[0, section, c, 0], reduce_sem.at[1, section, c, cut], 1 - core, me
                ).start()
            if cuts_of(section, c) == 1:
                at = half_at(stage, section, c, 1 - core)
                remote(
                    at, siblings.at[k], reduce_sem.at[0, section, c, 0], reduce_sem.at[1, section, c, 0], 1 - core, me
                ).start()

    def tap_gradient(section, c, meanwhile=()):
        field = I if c else X
        for i in range(9):
            t = i + (1 - core) * (8 - 2 * i)
            left = (core, 0, 1 - core)[i % 3]
            width = WIDE if i % 3 == 1 else WIDE - 1

            def start(row, column):
                return pl.multiple_of((row * PITCH + column) * block, 16)

            fields = [(g, f) for g in range(groups) for f in range(FOLD)]
            dz = [Z[g, pl.ds(start(f + 1, left + 1), width * block), :] for g, f in fields]
            dz = jnp.concatenate(dz, axis=0)
            moved = [
                field[section, g, pl.ds(start(f + t // 3, left + lax.rem(t, 3)), width * block), :] for g, f in fields
            ]
            moved = jnp.concatenate(moved, axis=0)
            grad = lax.dot_general(moved, dz, (((0,), (0,)), ((), ())), preferred_element_type=F32)
            at = pl.ds(pl.multiple_of(c * taps + t * channels, channels), channels)
            stage[section, at, :] = grad.astype(BF16)
            if i == 4 and own_taps:
                reduce_core(section, c)
            for after, step in meanwhile:
                if after == i:
                    step()
        if not own_taps:
            at = pl.ds(c * taps, taps)
            pltpu.make_async_copy(stage.at[section, at], tap_out.at[section, at], reduce_sem.at[0, section, c, 0]).start()

    def reduce_level(section, c, cut=0):
        if not own_taps:
            return
        k = 2 * section + c
        some = shard_rows // cuts_of(section, c)
        came(siblings.at[k, pl.ds(0, LAYER * some)], reduce_sem.at[1, section, c, cut])
        own = half_at(stage, section, c, core)
        for place in range(LAYER):
            at = pl.ds(place * shard_rows + cut * some, some)
            own[at, :] = (own[at, :].astype(F32) + siblings[k, at, :].astype(F32)).astype(BF16)
        for j in range(1, LAYER):
            place = lax.rem(spot + j, LAYER)
            part = own.at[pl.ds(pl.multiple_of(place * shard_rows + cut * some, 16), some)]
            remote(
                part, layers.at[k, spot, pl.ds(cut * some, some)], reduce_sem.at[2, section, c, 0],
                reduce_sem.at[3, section, c, cut], core, level * LAYER + place,
            ).start()
        mine_at = pl.ds(pl.multiple_of(spot * shard_rows + cut * some, 16), some)
        layers[k, spot, pl.ds(cut * some, some), :] = own[mine_at, :]

    def reduce_column(section, c, cut=0):
        if not own_taps:
            return
        k = 2 * section + c
        some = shard_rows // cuts_of(section, c)
        at = pl.ds(cut * some, some)
        came(siblings.at[k, pl.ds(0, (LAYER - 1) * some)], reduce_sem.at[3, section, c, cut])
        columns[k, at, :] = sum(layers[k, j, at, :].astype(F32) for j in range(LAYER)).astype(BF16)
        part, to = columns.at[k, at], arrivals.at[level, at]
        owner = 2 * c + core
        here = (core == section) & (owner == level)

        @pl.when(here)
        def _():
            pltpu.make_async_copy(part, to, reduce_sem.at[5, 0, 0, 0]).start()

        @pl.when(jnp.logical_not(here))
        def _():
            remote(
                part, to, reduce_sem.at[4, section, c, 0], reduce_sem.at[5, 0, 0, 0], section, owner * LAYER + spot
            ).start()

    def reduce_done():
        if not own_taps:
            return
        came(arrivals, reduce_sem.at[5, 0, 0, 0])
        tap_out[...] = sum(arrivals[j].astype(F32) for j in range(levels))

    def conv_window(owner):
        start = jnp.minimum(owner * flat // (PLANES + 1), channels - HC_ROWS)
        return pl.multiple_of(start // 8 * 8, 8)

    def hidden_window(owner):
        start = jnp.maximum(owner * flat - conv_end, 0) // VHIDDEN
        return pl.multiple_of(jnp.minimum(start // 8 * 8, hw_grad.shape[0] - HW_ROWS), 8)

    def head_exchange():
        remote(hc_grad, hc_in, head_sem.at[0], head_sem.at[1], 1 - core, me).start()
        remote(hw_grad, hw_in, head_sem.at[2], head_sem.at[3], 1 - core, me).start()

    def head_spread():
        sent(hc_grad, head_sem.at[0])
        sent(hw_grad, head_sem.at[2])
        came(hc_in, head_sem.at[1])
        came(hw_in, head_sem.at[3])
        hc_grad[...] += hc_in[...]
        hw_grad[...] += hw_in[...]

        def spread(j, carry):
            peer = lax.rem(me + j, n_dp)
            owner = core * n_dp + peer

            @pl.when(owner * flat < conv_end)
            def _():
                window = hc_grad.at[pl.ds(conv_window(owner), HC_ROWS)]
                remote(window, hc_slots.at[me], head_sem.at[4], head_sem.at[5], core, peer).start()

            @pl.when((owner + 1) * flat > conv_end)
            def _():
                window = hw_grad.at[pl.ds(hidden_window(owner), HW_ROWS)]
                remote(window, hw_slots.at[me], head_sem.at[6], head_sem.at[7], core, peer).start()

            return carry

        lax.fori_loop(1, n_dp, spread, 0)
        owner = core * n_dp + me
        hc_slots[me] = hc_grad[pl.ds(conv_window(owner), HC_ROWS), :]
        hw_slots[me] = hw_grad[pl.ds(hidden_window(owner), HW_ROWS), :]

    def head_done():
        owner = core * n_dp + me
        lines = small_out.shape[0] - 2

        def unsent(j, carry):
            peer = core * n_dp + lax.rem(me + j, n_dp)

            @pl.when(peer * flat < conv_end)
            def _():
                sent(hc_slots.at[0], head_sem.at[4])

            @pl.when((peer + 1) * flat > conv_end)
            def _():
                sent(hw_slots.at[0], head_sem.at[6])

            return carry

        lax.fori_loop(1, n_dp, unsent, 0)

        @pl.when(owner * flat < conv_end)
        def _():
            came(hc_slots.at[pl.ds(0, n_dp - 1)], head_sem.at[5])
            hc_in[pl.ds(0, HC_ROWS), :] = jnp.sum(hc_slots[...], axis=0)
            for line in range(lines):
                start = owner * flat + line * LANES
                row = start // (PLANES + 1)
                off = start - row * (PLANES + 1)
                out = jnp.zeros((1, LANES), F32)
                for m in range(3):
                    at = jnp.clip(row + m - conv_window(owner), 0, HC_ROWS - 1)
                    begin = (PLANES + 1) * m - off
                    part = pltpu.roll(hc_in[pl.ds(at, 1), :], lax.rem(begin + LANES, LANES), axis=1)
                    fits = (one_lane >= begin) & (one_lane < begin + PLANES + 1) & (start + one_lane < conv_end)
                    out = jnp.where(fits, part, out)
                small_out[pl.ds(2 + line, 1), :] = out

        @pl.when((owner + 1) * flat > conv_end)
        def _():
            came(hw_slots.at[pl.ds(0, n_dp - 1)], head_sem.at[7])
            window = jnp.sum(hw_slots[...], axis=0)
            for i in range(2):
                hidden_w[i, pl.ds(0, HW_ROWS), :] = window[:, i * LANES : (i + 1) * LANES]
            for line in range(lines):
                start = owner * flat + line * LANES
                from_end = start - conv_end + 64 * LANES
                row = from_end // LANES
                off = from_end - row * LANES
                out = small_out[pl.ds(2 + line, 1), :]
                for m in range(2):
                    at = jnp.clip(row + m - 64 - 2 * hidden_window(owner), 0, 2 * HW_ROWS - 1)
                    begin = LANES * m - off
                    part = hidden_w[lax.rem(at, 2), pl.ds(at // 2, 1), :]
                    part = pltpu.roll(part, lax.rem(begin + LANES, LANES), axis=1)
                    fits = (one_lane >= begin) & (one_lane < begin + LANES) & (start + one_lane >= conv_end)
                    out = jnp.where(fits, part, out)
                small_out[pl.ds(2 + line, 1), :] = out

    def norm_exchange():
        remote(norm_grad, norm_in, head_sem.at[8], head_sem.at[9], 1 - core, me).start()

    def norm_done():
        came(norm_in, head_sem.at[9])
        sent(norm_grad, head_sem.at[8])
        at = me * share
        tile, off = at // LANES, lax.rem(at, LANES)
        sums = norm_grad[...] + norm_in[...]
        for i in range(2):
            hidden_w[i, pl.ds(0, 8), :] = sums[:, i * LANES : (i + 1) * LANES]
        for i in range(2):
            part = hidden_w[lax.rem(tile, 2), pl.ds(4 * core + 2 * i + tile // 2, 1), :]
            small_out[pl.ds(i, 1), :] = pltpu.roll(part, lax.rem(LANES - off, LANES), axis=1)

    small_out[...] = jnp.zeros_like(small_out)

    def head_step(g):
        merge_moments(3, g)
        heads(g)
        outer_grad(1, g)

    for_groups(head_step)
    for_groups(head_taps)
    head_exchange()
    for section in (1, 0):

        def second_step(g, section=section):
            norm_back(section, 1, g)
            inner_grad(section, g)

        for_groups(second_step)
        if section == 1:
            head_spread()
        else:
            reduce_level(1, 0)
            reduce_column(1, 1)
        tap_gradient(section, 1)

        def first_step(g, section=section):
            norm_back(section, 0, g)
            if section == 1:
                entry(section, g)
                outer_grad(0, g)

        for_groups(first_step)
        if section == 1:
            reduce_level(1, 1)
            tap_gradient(1, 0)
        else:
            reduce_level(0, 1)
            norm_exchange()
            tap_gradient(0, 0, ((2, functools.partial(reduce_column, 1, 0)),))

    swap_at = pl.multiple_of(core * groups * rows, 16)

    def last_step(g, after_half, after_field, after_all):
        def add_field(at, part):
            B[g, at, :] += part

        for f in range(FOLD):
            add_field(pl.ds(f * span + block, span - 2 * block), back_middle(0, 0, g, f))
            if f == 1:
                after_half()
        for q in (0, WIDE - 1):
            out = back_outer(0, 0, g, q)
            for f in range(FOLD):
                add_field(pl.ds(f * span + q * block, block), out[f * block : (f + 1) * block])
        after_field()

        def restore(f, q, carry):
            v = B[g, plain(f, q), :]
            for at, square in halves(f, q):
                for i in range(channels // LANES):
                    turn[i, pl.ds(square, per, stride=64), :] = part_of(v, at)[:, i * LANES : (i + 1) * LANES]
            return carry

        each(restore)
        to = pl.ds(g * rows, rows)
        mine[to, :] = turn[core].astype(BF16)
        theirs[to, :] = turn[1 - core].astype(BF16)
        at = pl.ds(pl.multiple_of(swap_at + g * rows, 16), rows)
        remote(
            theirs.at[to], entry_grad.at[at], swap_sem.at[0, g], swap_sem.at[1, g], 1 - core, me
        ).start()
        pltpu.make_async_copy(mine.at[to], entry_grad.at[at], swap_sem.at[2, g]).start()
        after_all()

    def nothing():
        pass

    steps = [functools.partial(reduce_level, 0, 0, cut) for cut in range(CUTS)]
    steps += [functools.partial(reduce_column, 0, 1)]
    steps += [functools.partial(reduce_column, 0, 0, cut) for cut in range(CUTS)]
    if not own_taps:
        steps = [nothing] * len(steps)
    for g in range(groups):
        last_step(g, *(steps[3 * g : 3 * g + 3] + [nothing] * 3)[:3])
    for step in steps[3 * groups :]:
        step()
    head_done()
    norm_done()

    sent(packs.at[core, pl.ds(0, n_dp - 1)], pack_sem.at[0])
    sent(packs.at[core], pack_sem.at[2])
    for section in range(2):
        for c in range(2):
            k = 2 * section + c
            if not own_taps:
                at = pl.ds(c * taps, taps)
                pltpu.make_async_copy(
                    stage.at[section, at], tap_out.at[section, at], reduce_sem.at[0, section, c, 0]
                ).wait()
                continue
            three = stage.at[section, pl.ds(0, (LAYER - 1) * shard_rows)]

            @pl.when((core == section) & (level // 2 == c))
            def _(section=section, c=c):
                sent(stage.at[section, pl.ds(0, (levels - 1) * shard_rows)], fetch_sem.at[0, section, c, 0])

                @pl.when(lax.rem(level, 2) != core)
                def _():
                    sent(stage.at[section, pl.ds(0, shard_rows)], fetch_sem.at[0, section, c, 0])

            sent(three, fetch_sem.at[2, section, c, 0])
            sent(half_at(stage, section, c, core), fetch_sem.at[4, section, c, 0])
            sent(siblings.at[k], reduce_sem.at[0, section, c, 0])
            sent(three, reduce_sem.at[2, section, c, 0])

            @pl.when(jnp.logical_not((core == section) & (2 * c + core == level)))
            def _(section=section, c=c, k=k):
                sent(columns.at[k], reduce_sem.at[4, section, c, 0])

    reduce_done()
    for g in range(groups):
        to = pl.ds(g * rows, rows)
        at = pl.ds(pl.multiple_of(swap_at + g * rows, 16), rows)
        remote(theirs.at[to], entry_grad.at[at], swap_sem.at[0, g], swap_sem.at[1, g], 1 - core, me).wait()
        pltpu.make_async_copy(mine.at[to], entry_grad.at[at], swap_sem.at[2, g]).wait()


def finish(parts, entry_in, tap_in, small_in, entry_out, tap_out, gain_out, shift_out, head_out, narrow, broad, taps, small, sem):
    some = entry_in.shape[0] // parts
    cuts = [pl.ds(i * some, some) for i in range(parts)]
    loads = [pltpu.make_async_copy(entry_in.at[at], narrow.at[at], sem.at[0, i]) for i, at in enumerate(cuts)]
    stores = [pltpu.make_async_copy(broad.at[at], entry_out.at[at], sem.at[1, i]) for i, at in enumerate(cuts)]
    tap_load = pltpu.make_async_copy(tap_in, taps, sem.at[0, parts])
    tap_store = pltpu.make_async_copy(taps, tap_out, sem.at[1, parts])
    for load in loads:
        load.start()
    tap_load.start()
    small_load = pltpu.make_async_copy(small_in, small, sem.at[0, parts + 1])
    small_load.start()
    small_load.wait()
    gain_out[...] = small[pl.ds(0, 1), pl.ds(0, gain_out.shape[1])]
    shift_out[...] = small[pl.ds(1, 1), pl.ds(0, gain_out.shape[1])]
    flat = head_out.shape[0]
    for line in range(0, flat, LANES):
        count = min(LANES, flat - line)
        head_out[pl.ds(line, count)] = small[pl.ds(2 + line // LANES, 1), pl.ds(0, count)].reshape(count)
    for at, load, store in zip(cuts, loads, stores):
        load.wait()
        broad[at, :] = narrow[at, :].astype(F32)
        store.start()
    tap_load.wait()
    tap_store.start()
    for store in stores:
        store.wait()
    tap_store.wait()


def local(
    board_input, conv_weight, norm_gains, norm_shifts, head_params, policy_target, legal_mask, value_target
):
    n_dp, n_pipe = lax.axis_size("dp"), lax.axis_size("pipe")
    positions, channels = board_input.shape[0], board_input.shape[-1]
    per = positions // MICRO
    groups = MICRO // n_pipe
    moves = legal_mask.shape[1]
    rows = per * 64
    padded = (FOLD + 2) * PITCH * 2 * per
    taps = 9 * channels

    shard_rows = conv_weight.shape[1]
    own_taps = shard_rows % 16 == 0 and n_dp == 4 * LAYER
    share, flat = norm_gains.shape[1], head_params.shape[0]
    lines = -(-flat // LANES)
    pack_rows = -(-(2 + lines) // 8) * 8
    taps_in = conv_weight
    if not own_taps:
        taps_in = lax.all_gather(lax.all_gather(conv_weight, "dp", axis=1, tiled=True), "pipe", axis=0, tiled=True)

    vmem = pl.BlockSpec(memory_space=pltpu.VMEM)
    smem = pl.BlockSpec(memory_space=pltpu.SMEM)
    anywhere = pl.BlockSpec(memory_space=pl.ANY)
    dma, regular = pltpu.SemaphoreType.DMA, pltpu.VMEM
    tap_shape = (shard_rows, channels) if own_taps else (2, 2 * taps, channels)
    lane_rows = shard_rows if own_taps else 16
    tap_grad, small_grad, entry_grad = pl.pallas_call(
        functools.partial(
            kernel, (n_dp, per, groups, moves, 1.0 / positions, shard_rows, own_taps, flat)
        ),
        out_shape=(
            jax.ShapeDtypeStruct(tap_shape, F32 if own_taps else BF16),
            jax.ShapeDtypeStruct((pack_rows, LANES), F32),
            jax.ShapeDtypeStruct((positions * 64, LANES), BF16),
        ),
        in_specs=[smem, smem, anywhere, anywhere, vmem, vmem, vmem, anywhere],
        out_specs=(vmem if own_taps else anywhere, vmem, anywhere),
        scratch_shapes=[
            regular((2, 2 * taps, channels), BF16),
            regular((2, groups, padded, channels), BF16),
            regular((2, groups, padded, channels), BF16),
            regular((groups, padded, channels), BF16),
            regular((2, 2, groups, rows, channels), F32),
            regular((groups, rows, channels), F32),
            regular((groups * per, 8, 8, channels), BF16),
            regular((groups * per, moves), jnp.int32),
            regular((groups, rows, LANES), F32),
            regular((rows, LANES), F32),
            regular((channels // LANES, rows, LANES), F32),
            regular((groups * per, LANES), jnp.int32),
            regular((groups * per, LANES), F32),
            regular((2, 2 * taps, channels), BF16),
            regular((4, groups, 8, channels), F32),
            regular((8, groups, n_dp, 2, channels), F32),
            regular((groups * rows, LANES), BF16),
            regular((groups * rows, LANES), BF16),
            regular((2, n_dp, pack_rows, LANES), F32),
            regular((2, 8, channels), F32),
            regular((channels, LANES), F32),
            regular((2, channels, 2 * LANES), BF16),
            regular((2, LANES + 8, LANES), F32),
            regular((8, channels), F32),
            regular((channels, LANES), F32),
            regular((72, VHIDDEN), F32),
            regular((8, channels), F32),
            regular((channels, LANES), F32),
            regular((72, VHIDDEN), F32),
            regular((n_dp, HC_ROWS, LANES), F32),
            regular((n_dp, HW_ROWS, VHIDDEN), F32),
            regular((4, LAYER * lane_rows, channels), BF16),
            regular((4, LAYER, lane_rows, channels), BF16),
            regular((4, lane_rows, channels), BF16),
            regular((4, lane_rows, channels), BF16),
            dma((3,)),
            dma((8, groups)),
            dma((8, groups)),
            dma((3, groups)),
            dma((4,)),
            dma((10,)),
            dma((6, 2, 2, FETCH_CUTS)),
            dma((6, 2, 2, CUTS)),
        ],
        compiler_params=pltpu.CompilerParams(
            collective_id=0, has_side_effects=True, vmem_limit_bytes=63 * 2**20
        ),
    )(
        policy_target, value_target, board_input, taps_in, norm_gains, norm_shifts, head_params,
        legal_mask,
    )

    conv_grad = tap_grad
    if not own_taps:
        conv_grad = lax.psum_scatter(
            tap_grad.astype(F32).reshape(4 * taps, channels), ("pipe", "dp"), scatter_dimension=0, tiled=True
        )
    parts = 6
    entry_grad, conv_grad, gain_grad, shift_grad, head_grad = pl.pallas_call(
        functools.partial(finish, parts),
        out_shape=(
            jax.ShapeDtypeStruct(entry_grad.shape, F32),
            jax.ShapeDtypeStruct(conv_grad.shape, F32),
            jax.ShapeDtypeStruct((1, share), F32),
            jax.ShapeDtypeStruct((1, share), F32),
            jax.ShapeDtypeStruct((flat,), F32),
        ),
        in_specs=[anywhere, anywhere, anywhere],
        out_specs=(anywhere, anywhere, vmem, vmem, vmem),
        scratch_shapes=[
            regular(entry_grad.shape, BF16),
            regular(entry_grad.shape, F32),
            regular(conv_grad.shape, F32),
            regular(small_grad.shape, F32),
            dma((2, parts + 2)),
        ],
        compiler_params=pltpu.CompilerParams(vmem_limit_bytes=60 * 2**20),
    )(entry_grad, conv_grad, small_grad)
    entry_grad = entry_grad.reshape(positions, 8, 8, LANES)
    return conv_grad[None], gain_grad, shift_grad, head_grad, entry_grad


def solution(mesh):
    placed = (
        P("dp", None, None, None),
        P("pipe", "dp", None),
        P("pipe", "dp"),
        P("pipe", "dp"),
        P(("pipe", "dp")),
        P("dp"),
        P("dp", None),
        P("dp"),
    )
    return jax.shard_map(
        local,
        mesh=mesh,
        in_specs=placed,
        out_specs=(
            P("pipe", "dp", None),
            P("pipe", "dp"),
            P("pipe", "dp"),
            P(("pipe", "dp")),
            P("dp", None, None, "pipe"),
        ),
        check_vma=False,
    )
```
